32 devices in a mesh: grp: 2 (over y), fsdp: 16 (over z, x, core).
Axes of the slice: x: 2, y: 2, z: 4, core: 2. Of those that a mesh axis runs over, the one named last changes fastest.
Arguments:
- hidden_in: bfloat16 [65536, 768], P(('grp', 'fsdp')), may hold values from -6 to 6
- out_grad: bfloat16 [65536, 768], P(('grp', 'fsdp')), may hold values from -6 to 6
- pooled_gradient: float32 [128, 2, 768], P(('grp', 'fsdp')), may hold values from -384 to 384
- gain_attn: bfloat16 [768], P('fsdp'), may hold values from 0.5 to 1.5
- w_query: bfloat16 [768, 768], P('fsdp'), may hold values from -0.0546875 to 0.0546875
- w_key: bfloat16 [768, 768], P('fsdp'), may hold values from -0.21875 to 0.21875
- w_value: bfloat16 [768, 768], P('fsdp'), may hold values from -0.21875 to 0.21875
- w_output: bfloat16 [768, 768], P('fsdp'), may hold values from -0.4375 to 0.4375
- rel_table: bfloat16 [384], P('fsdp'), may hold values from -4 to 4
- gain_ffn: bfloat16 [768], P('fsdp'), may hold values from 0.5 to 1.5
- w_in: bfloat16 [768, 3072], P('fsdp'), may hold values from -0.21875 to 0.21875
- w_out: bfloat16 [3072, 768], P('fsdp'), may hold values from -0.109375 to 0.109375
- pair_flags: int32 [65536], P(('grp', 'fsdp')), may hold values from 0 to 1, as said below
- instruction_mask: int32 [65536], P(('grp', 'fsdp')), may hold values from 0 to 1, as said below
Outputs:
- output: bfloat16 [65536, 768], P(('grp', 'fsdp'))
- pooled: float32 [128, 2, 768], P(('grp', 'fsdp'))
- input_grad: bfloat16 [65536, 768], P(('grp', 'fsdp'))
- grad_gain_attn: float32 [768], P('fsdp')
- grad_w_query: float32 [768, 768], P('fsdp')
- grad_w_key: float32 [768, 768], P('fsdp')
- grad_w_value: float32 [768, 768], P('fsdp')
- grad_w_output: float32 [768, 768], P('fsdp')
- grad_rel_table: float32 [384], P('fsdp')
- grad_gain_ffn: float32 [768], P('fsdp')
- grad_w_in: float32 [768, 3072], P('fsdp')
- grad_w_out: float32 [3072, 768], P('fsdp')
The draws below stay inside these ranges and needn't reach their ends.
Inputs may be any that keep to these rules, and one draw needn't show every extreme that they name: `pair_flags`: in each sequence of 512 tokens, 0 on a first run and 1 on the rest; each run has 128 tokens or more. `instruction_mask`: 1 on a prefix of 1 to 64 tokens of each run of pair_flags, 0 elsewhere.
All inputs are finite; a program needn't handle non-finite values.
Results may differ from the reference program's by a relative error of at most 0.015.
Values may be sent and summed in bfloat16 or wider, within the bound.
A program may use at most 256 MiB of HBM per device.

```python
import jax
import jax.numpy as jnp
from jax import lax

MODEL_WIDTH = 768
HEADS = 12
HEAD_DIM = 64
FF = 3072
BUCKETS = 32
SEQUENCE_LENGTH = 512
SEQS = 128
TOKENS = 65536


def split_points(key):
    return jax.random.randint(key, (TOKENS // SEQUENCE_LENGTH, 1), SEQUENCE_LENGTH // 4, 3 * SEQUENCE_LENGTH // 4 + 1, dtype=jnp.int32)


def draw_pair_flags(key, part):
    bounds = split_points(key)
    position = jnp.arange(SEQUENCE_LENGTH, dtype=jnp.int32)[None, :]
    return (position >= bounds).astype(jnp.int32).reshape(TOKENS)


def draw_instruction_mask(key, part):
    bounds = split_points(key)
    key = jax.random.fold_in(key, 7)
    prefixes = jax.random.randint(key, (TOKENS // SEQUENCE_LENGTH, 2), 1, SEQUENCE_LENGTH // 8 + 1, dtype=jnp.int32)
    position = jnp.arange(SEQUENCE_LENGTH, dtype=jnp.int32)[None, :]
    first_run = position < prefixes[:, 0:1]
    second_run = (position >= bounds) & (position < bounds + prefixes[:, 1:2])
    return (first_run | second_run).astype(jnp.int32).reshape(TOKENS)


def steps_of(key, extent, cuts, least, high):
    def one(axis_at, parts):
        steps = jax.random.uniform(jax.random.fold_in(jax.random.fold_in(key, 6), axis_at), (parts,), jnp.float32, least / len(cuts), high / len(cuts))
        return jnp.repeat(jnp.exp(steps), extent[axis_at] // parts).reshape((-1,) + (1,) * (len(extent) - axis_at - 1))

    level = one(*cuts[0])
    for cut in cuts[1:]:
        level = level * one(*cut)
    return level


def bell_draw(rng, dims, spread, limit, split=(), kind=jnp.bfloat16):
    entries = jax.random.normal(rng, dims, jnp.float32) * spread
    if len(split) > 0:
        entries = steps_of(rng, dims, split, -0.22, 0.18) * entries
    return jnp.clip(entries, min=-limit, max=limit).astype(kind)


def setup_inputs(seed: int = 0) -> dict:
    keys = jax.random.split(jax.random.key(seed), 15)
    hidden_in = bell_draw(keys[0], (TOKENS, MODEL_WIDTH), 1.0, 6.0, ((0, 32),))
    out_grad = bell_draw(keys[1], (TOKENS, MODEL_WIDTH), 1.0, 6.0, ((0, 32),))
    pooled_gradient = bell_draw(keys[2], (SEQS, 2, MODEL_WIDTH), (SEQUENCE_LENGTH // 8), 384.0, ((0, 32),), jnp.float32)
    gain_attn = jnp.clip(1.0 + 0.1 * jax.random.normal(keys[3], (MODEL_WIDTH,), jnp.float32), 0.5, 1.5).astype(jnp.bfloat16)
    w_query = bell_draw(keys[4], (MODEL_WIDTH, HEADS * HEAD_DIM), (16 * MODEL_WIDTH) ** -0.5, 0.0546875, ((0, 16),))
    w_key = bell_draw(keys[5], (MODEL_WIDTH, HEADS * HEAD_DIM), MODEL_WIDTH ** -0.5, 0.21875, ((0, 16),))
    w_value = bell_draw(keys[6], (MODEL_WIDTH, HEADS * HEAD_DIM), MODEL_WIDTH ** -0.5, 0.21875, ((0, 16),))
    w_output = bell_draw(keys[7], (HEADS * HEAD_DIM, MODEL_WIDTH), (HEADS * HEAD_DIM // 4) ** -0.5, 0.4375, ((0, 16),))
    rel_table = bell_draw(keys[8], (BUCKETS * HEADS,), 1.0, 4.0, ((0, 16),))
    gain_ffn = jnp.clip(1.0 + 0.1 * jax.random.normal(keys[9], (MODEL_WIDTH,), jnp.float32), 0.5, 1.5).astype(jnp.bfloat16)
    w_in = bell_draw(keys[10], (MODEL_WIDTH, FF), MODEL_WIDTH ** -0.5, 0.21875, ((0, 16),))
    w_out = bell_draw(keys[11], (FF, MODEL_WIDTH), FF ** -0.5, 0.109375, ((0, 16),))
    pair_flags = draw_pair_flags(jax.random.fold_in(keys[14], 71), 0)
    instruction_mask = draw_instruction_mask(jax.random.fold_in(keys[14], 71), 0)
    return {"hidden_in": hidden_in, "out_grad": out_grad, "pooled_gradient": pooled_gradient, "gain_attn": gain_attn, "w_query": w_query, "w_key": w_key, "w_value": w_value, "w_output": w_output, "rel_table": rel_table, "gain_ffn": gain_ffn, "w_in": w_in, "w_out": w_out, "pair_flags": pair_flags, "instruction_mask": instruction_mask}


@jax.custom_vjp
def low(v):
    return lax.optimization_barrier(v.astype(jnp.bfloat16)).astype(jnp.float32)

@jax.custom_vjp
def low_back(v):
    return v

def low_keep(v):
    return (low(v), None)

def low_pass(kept, grad):
    return (grad,)

def back_keep(v):
    return (v, None)

def back_low(kept, grad):
    return (low(grad),)
low.defvjp(low_keep, low_pass)
low_back.defvjp(back_keep, back_low)
EPS = 1e-06
NEG = -1e+30
HIGH_PRECISION = lax.Precision.HIGHEST
LIMITS = (12, 16, 23, 32, 46, 64, 91)

def rounded(tensor):
    return low(low_back(tensor))

def product(matrix, operand):
    return jnp.dot(matrix, operand, precision=HIGH_PRECISION, preferred_element_type=jnp.float32)

def rms_norm(tensor, scale_vec):
    return tensor * lax.rsqrt(lax.optimization_barrier(jnp.mean(tensor * tensor, axis=-1, keepdims=True)) + EPS) * scale_vec

def bucket_of(offset):
    distance = jnp.abs(offset)
    far_bucket = jnp.full(offset.shape, 8, jnp.int32)
    for threshold in LIMITS:
        far_bucket = far_bucket + (distance >= threshold).astype(jnp.int32)
    near_bucket = jnp.where(distance < 8, distance, far_bucket)
    return (near_bucket + BUCKETS // 2 * (offset > 0).astype(jnp.int32)).astype(jnp.int32)

def pooling_weight_rows(flag_values, instruction_tokens):
    kept_tokens = (instruction_tokens.reshape(-1, SEQUENCE_LENGTH) == 0).astype(jnp.float32)
    which_part = (flag_values.reshape(-1, SEQUENCE_LENGTH)[:, None, :] == jnp.arange(2, dtype=jnp.int32)[None, :, None]).astype(jnp.float32)
    chosen = which_part * kept_tokens[:, None, :]
    return chosen / lax.optimization_barrier(jnp.sum(chosen, axis=-1, keepdims=True))

def forward(hidden, gain_attn, w_query, w_key, w_value, w_output, rel_table, gain_ffn, w_in, w_out, flag_values, instruction_tokens):
    width_all = HEADS * HEAD_DIM
    normed = low(rms_norm(hidden, gain_attn))
    queries = rounded(product(normed, w_query))
    keys_proj = rounded(product(normed, w_key))
    values_proj = rounded(product(normed, w_value))
    position = jnp.arange(SEQUENCE_LENGTH, dtype=jnp.int32)
    buckets = bucket_of(position[None, :] - position[:, None])
    onehot = (buckets[:, :, None] == jnp.arange(BUCKETS, dtype=jnp.int32)[None, None, :]).astype(jnp.float32)
    position_bias = jnp.einsum('ijb,bh->hij', onehot, rel_table.reshape(BUCKETS, HEADS), precision=HIGH_PRECISION)

    def one_sequence(pieces):
        seq_query, seq_key, seq_value, seq_flags = pieces
        heads_query = seq_query.reshape(SEQUENCE_LENGTH, HEADS, HEAD_DIM)
        heads_key = seq_key.reshape(SEQUENCE_LENGTH, HEADS, HEAD_DIM)
        heads_value = seq_value.reshape(SEQUENCE_LENGTH, HEADS, HEAD_DIM)
        scores = jnp.einsum('ihd,jhd->hij', heads_query, heads_key, precision=HIGH_PRECISION) + position_bias
        scores = low_back(scores)
        same_part = (seq_flags[:, None] == seq_flags[None, :])[None]
        scores = jnp.where(same_part, scores, NEG)
        highest = lax.optimization_barrier(jnp.max(scores, axis=-1, keepdims=True))
        exponent = jnp.exp(scores - highest)
        probabilities = exponent / lax.optimization_barrier(jnp.sum(exponent, axis=-1, keepdims=True))
        mixture = jnp.einsum('hij,jhd->ihd', low(probabilities), heads_value, precision=HIGH_PRECISION)
        return mixture.reshape(SEQUENCE_LENGTH, width_all)
    mixture = lax.map(jax.checkpoint(one_sequence), (queries.reshape(-1, SEQUENCE_LENGTH, width_all), keys_proj.reshape(-1, SEQUENCE_LENGTH, width_all), values_proj.reshape(-1, SEQUENCE_LENGTH, width_all), flag_values.reshape(-1, SEQUENCE_LENGTH)))
    mixture = rounded(mixture.reshape(-1, width_all))
    middle = hidden + low_back(product(mixture, w_output))
    normed_two = low(rms_norm(middle, gain_ffn))
    inner_value = low_back(product(normed_two, w_in))
    activation = low(jax.nn.gelu(inner_value, approximate=True))
    final_output = middle + low_back(product(activation, w_out))
    pooled = jnp.einsum('qgu,quv->qgv', pooling_weight_rows(flag_values, instruction_tokens), final_output.reshape(-1, SEQUENCE_LENGTH, MODEL_WIDTH), precision=HIGH_PRECISION)
    return (final_output, pooled)

def reference(hidden_in, out_grad, pooled_gradient, gain_attn, w_query, w_key, w_value, w_output, rel_table, gain_ffn, w_in, w_out, pair_flags, instruction_mask):
    floats = [array.astype(jnp.float32) for array in (hidden_in, gain_attn, w_query, w_key, w_value, w_output, rel_table, gain_ffn, w_in, w_out)]

    def apply_layer(*params):
        return forward(*params, pair_flags, instruction_mask)
    (final_output, pooled), pullback = jax.vjp(apply_layer, *floats)
    grads = pullback((out_grad.astype(jnp.float32), pooled_gradient))
    return (final_output.astype(jnp.bfloat16), pooled, grads[0].astype(jnp.bfloat16), grads[1], grads[2], grads[3], grads[4], grads[5], grads[6], grads[7], grads[8], grads[9])
```

```python
from functools import partial

import jax
import jax.numpy as jnp
from jax import lax
from jax.experimental import pallas as pl
from jax.experimental.pallas import tpu as pltpu
from jax.sharding import PartitionSpec as P

HEADS = 12
HEAD_DIM = 64
BUCKETS = 32
LENGTH = 512
BLOCK = 128
BLOCKS = LENGTH // BLOCK
PAIRS = HEADS // 2
BAND = 5 * BLOCK
EPS = 1e-06
NEG = -1e30
LIMITS = (12, 16, 23, 32, 46, 64, 91)
ROOT = 0.7978845608028654
CUBE = 0.044715
F32 = jnp.float32
BF16 = jnp.bfloat16
ANY = pl.BlockSpec(memory_space=pl.ANY)
VMEM_LIMIT = 62 * 1024 * 1024


def bucket_of(offset):
    distance = jnp.abs(offset)
    far_bucket = jnp.full(offset.shape, 8, jnp.int32)
    for threshold in LIMITS:
        far_bucket = far_bucket + (distance >= threshold).astype(jnp.int32)
    near_bucket = jnp.where(distance < 8, distance, far_bucket)
    return near_bucket + BUCKETS // 2 * (offset > 0).astype(jnp.int32)


def dot(a, b):
    return lax.dot_general(a, b, (((1,), (0,)), ((), ())), preferred_element_type=F32)


def dot_nt(a, b):
    return lax.dot_general(a, b, (((1,), (1,)), ((), ())), preferred_element_type=F32)


def dot_tn(a, b):
    return lax.dot_general(a, b, (((0,), (0,)), ((), ())), preferred_element_type=F32)


def iota(shape, axis):
    return lax.broadcasted_iota(jnp.int32, shape, axis)


def whole(shape):
    zeros = (0,) * len(shape)
    return pl.BlockSpec(shape, lambda *_: zeros, pipeline_mode=pl.Buffered(1))


def columns_of(row):
    return (0, BLOCKS - 1) if row == 0 else (1, BLOCKS) if row == BLOCKS - 1 else (0, BLOCKS)


def span(first, last):
    return slice(first * BLOCK, last * BLOCK)


def half_mask(half):
    return (iota((1, BLOCK), 1) // HEAD_DIM == half).astype(F32).astype(BF16)


def pool_terms(flags, instruction):
    kept = (instruction == 0).astype(F32)
    chosen = [kept * (flags == part).astype(F32) for part in range(2)]
    counts = [jnp.sum(one, axis=1, keepdims=True) for one in chosen]
    return chosen, counts


def pool_gradient(chosen, counts, pooled_grad):
    row = iota((16, LENGTH), 0)
    picks = jnp.where(row % 2 == 0, chosen[0], chosen[1])
    picks = jnp.where(row < 6, picks, 0.0).astype(BF16)
    scaled = [pooled_grad[part : part + 1, :] / counts[part] for part in range(2)]
    width = pooled_grad.shape[1]
    line = iota((16, width), 0)
    both = jnp.where(line % 2 == 0, scaled[0], scaled[1])
    high = both.astype(BF16).astype(F32)
    rest = both - high
    middle = rest.astype(BF16).astype(F32)
    low = rest - middle
    parts = jnp.where(line < 2, high, jnp.where(line < 4, middle, jnp.where(line < 6, low, 0.0)))
    return dot_tn(picks, parts.astype(BF16))


def attend_kernel(
    x_ref, og_ref, pg_ref, flags_ref, instr_ref, gain1_ref, gain2_ref, table_ref, wq_ref, wk_ref, wv_ref, wo_ref,
    q_ref, k_ref, v_ref, p_ref, mix_ref, mid_ref, n2_ref, bg_ref,
    band_ref, auxq_ref, auxk_ref,
):
    @pl.when(pl.program_id(0) == 0)
    def _():
        table = table_ref[...]

        def one_head(head, _):
            line = jnp.sum(jnp.where(iota((16, 2 * LENGTH), 0) == head, table, 0.0), axis=0, keepdims=True)
            turned = pltpu.roll(jnp.broadcast_to(line, (BLOCK, 2 * LENGTH)), 0, 1, stride=1, stride_axis=0)
            band_ref[head] = turned[:, BLOCK : BLOCK + BAND]
            return 0

        lax.fori_loop(0, HEADS, one_head, 0)

    flags, instruction = flags_ref[0], instr_ref[0]
    chosen, counts = pool_terms(flags, instruction)
    grad_result = og_ref[...].astype(F32) + pool_gradient(chosen, counts, pg_ref[0])
    bg_ref[...] = grad_result.astype(BF16)

    row = iota((16, LENGTH), 0)
    which = jnp.where(row == 0, 1 - flags, jnp.where(row == 1, flags, 0)).astype(F32).astype(BF16)
    lane, line = iota((16, BLOCK), 1), iota((16, BLOCK), 0)
    own = jnp.where((lane == line) & (line < 2), 1.0, 0.0).astype(BF16)
    other = jnp.where((lane == 1 - line) & (line < 2), NEG, 0.0).astype(BF16)
    auxq_ref[...] = dot_tn(which, own).astype(BF16)
    auxk_ref[...] = dot_tn(which, other).astype(BF16)

    hidden = x_ref[...].astype(F32)
    scale = lax.rsqrt(jnp.mean(hidden * hidden, axis=1, keepdims=True) + EPS)
    normed = (hidden * scale * gain1_ref[...]).astype(BF16)
    q_ref[...] = dot(normed, wq_ref[...]).astype(BF16)
    k_ref[...] = dot(normed, wk_ref[...]).astype(BF16)
    v_ref[...] = dot(normed, wv_ref[...]).astype(BF16)

    def one_pair(pair, _):
        lanes = pl.ds(pl.multiple_of(pair * BLOCK, BLOCK), BLOCK)
        keys = jnp.concatenate([k_ref[:, lanes], auxk_ref[...]], axis=1)
        values = v_ref[:, lanes]
        for index in range(BLOCKS):
            first, last = columns_of(index)
            shift = 2 - index
            total = None
            for half in range(2):
                head = pair * 2 + half
                query = q_ref[span(index, index + 1), lanes] * half_mask(half)
                query = jnp.concatenate([query, auxq_ref[span(index, index + 1), :]], axis=1)
                scores = dot_nt(query, keys[span(first, last)]) + band_ref[head, :, span(first + shift, last + shift)]
                exponent = jnp.exp(scores - jnp.max(scores, axis=1, keepdims=True))
                probability = exponent * (1.0 / jnp.sum(exponent, axis=1, keepdims=True))
                probability = probability.astype(BF16)
                p_ref[0, head, span(index, index + 1), span(first, last)] = probability
                part = dot(probability, values[span(first, last)] * half_mask(half))
                total = part if total is None else total + part
            mix_ref[span(index, index + 1), lanes] = total.astype(BF16)
        return 0

    lax.fori_loop(0, PAIRS, one_pair, 0)

    middle = hidden + dot(mix_ref[...], wo_ref[...])
    mid_ref[...] = middle
    scale = lax.rsqrt(jnp.mean(middle * middle, axis=1, keepdims=True) + EPS)
    n2_ref[...] = (middle * scale * gain2_ref[...]).astype(BF16)


def attend(x, og, pg, flags, instr, gain1, gain2, table, wq, wk, wv, wo):
    tokens, width = x.shape
    seqs = tokens // LENGTH
    rows = pl.BlockSpec((LENGTH, width), lambda s: (s, 0))
    flag_rows = pl.BlockSpec((1, 1, LENGTH), lambda s: (s, 0, 0))
    low = jax.ShapeDtypeStruct((tokens, width), BF16)
    return pl.pallas_call(
        attend_kernel,
        name="attend",
        grid=(seqs,),
        in_specs=[
            rows, rows, pl.BlockSpec((1, 2, width), lambda s: (s, 0, 0)), flag_rows, flag_rows,
            whole((1, width)), whole((1, width)), whole((16, 2 * LENGTH)),
            whole((width, width)), whole((width, width)), whole((width, width)), whole((width, width)),
        ],
        out_specs=[
            rows, rows, rows, pl.BlockSpec((1, HEADS, LENGTH, LENGTH), lambda s: (s, 0, 0, 0)), rows, rows, rows, rows,
        ],
        out_shape=[
            low, low, low, jax.ShapeDtypeStruct((seqs, HEADS, LENGTH, LENGTH), BF16), low,
            jax.ShapeDtypeStruct((tokens, width), F32), low, low,
        ],
        scratch_shapes=[
            pltpu.VMEM((HEADS, BLOCK, BAND), F32), pltpu.VMEM((LENGTH, BLOCK), BF16), pltpu.VMEM((LENGTH, BLOCK), BF16),
        ],
        compiler_params=pltpu.CompilerParams(vmem_limit_bytes=VMEM_LIMIT),
    )(x, og, pg, flags, instr, gain1, gain2, table, wq, wk, wv, wo)


FF_CHUNK = 512


def feed_kernel(
    n2_ref, bg_ref, mid_hbm, flags_ref, instr_ref, win_ref, wout_ref,
    out_ref, pooled_ref, dn2_ref, dwin_ref, dwout_ref,
    res_ref, act_ref, dinner_ref, sem,
):
    step, steps = pl.program_id(0), pl.num_programs(0)
    seqs = n2_ref.shape[0] // LENGTH

    @pl.when(step == 0)
    def _():
        copy = pltpu.make_async_copy(mid_hbm, res_ref, sem)
        copy.start()
        dn2_ref[...] = jnp.zeros_like(dn2_ref)
        copy.wait()

    def one_block(block, _):
        rows = pl.ds(pl.multiple_of(block * LENGTH, LENGTH), LENGTH)
        win, wout = win_ref[...], wout_ref[...]
        inner = dot(n2_ref[rows, :], win)
        square = inner * inner
        half = 0.5 * jnp.tanh(inner * (ROOT + (ROOT * CUBE) * square)) + 0.5
        active = inner * half
        slope = half + active * (1.0 - half) * (2.0 * ROOT + (6.0 * ROOT * CUBE) * square)
        active = active.astype(BF16)
        act_ref[rows, :] = active
        res_ref[rows, :] += dot(active, wout)
        dinner = (dot_nt(bg_ref[rows, :], wout) * slope).astype(BF16)
        dinner_ref[rows, :] = dinner
        dn2_ref[rows, :] += dot_nt(dinner, win)
        return 0

    lax.fori_loop(0, seqs, one_block, 0)
    dwin_ref[...] = dot_tn(n2_ref[...], dinner_ref[...]).astype(dwin_ref.dtype)
    dwout_ref[...] = dot_tn(act_ref[...], bg_ref[...]).astype(dwout_ref.dtype)

    @pl.when(step == steps - 1)
    def _():
        for seq in range(seqs):
            rows = slice(seq * LENGTH, (seq + 1) * LENGTH)
            result = res_ref[rows, :]
            out_ref[rows, :] = result.astype(BF16)
            chosen, counts = pool_terms(flags_ref[seq], instr_ref[seq])
            line = iota((8, LENGTH), 0)
            picks = jnp.where(line == 0, chosen[0], jnp.where(line == 1, chosen[1], 0.0)).astype(BF16)
            high = result.astype(BF16)
            low = (result - high.astype(F32)).astype(BF16)
            total = dot(picks, high) + dot(picks, low)
            side = iota((8, 1), 0)
            total = total / jnp.where(side == 0, counts[0], counts[1])
            pooled_ref[seq] = total[0:2, :]


def feed(n2, bg, mid, flags, instr, win, wout):
    tokens, width = n2.shape
    seqs = tokens // LENGTH
    ff = win.shape[1]
    chunk = FF_CHUNK
    return pl.pallas_call(
        feed_kernel,
        name="feed",
        grid=(ff // chunk,),
        in_specs=[
            whole((tokens, width)), whole((tokens, width)), ANY,
            whole((seqs, 1, LENGTH)), whole((seqs, 1, LENGTH)),
            pl.BlockSpec((width, chunk), lambda c: (0, c)), pl.BlockSpec((chunk, width), lambda c: (c, 0)),
        ],
        out_specs=[
            whole((tokens, width)), whole((seqs, 2, width)), whole((tokens, width)),
            pl.BlockSpec((width, chunk), lambda c: (0, c)), pl.BlockSpec((chunk, width), lambda c: (c, 0)),
        ],
        out_shape=[
            jax.ShapeDtypeStruct((tokens, width), BF16), jax.ShapeDtypeStruct((seqs, 2, width), F32),
            jax.ShapeDtypeStruct((tokens, width), F32),
            jax.ShapeDtypeStruct((width, ff), BF16), jax.ShapeDtypeStruct((ff, width), BF16),
        ],
        scratch_shapes=[
            pltpu.VMEM((tokens, width), F32), pltpu.VMEM((tokens, chunk), BF16), pltpu.VMEM((tokens, chunk), BF16),
            pltpu.SemaphoreType.DMA,
        ],
        compiler_params=pltpu.CompilerParams(vmem_limit_bytes=VMEM_LIMIT),
    )(n2, bg, mid, flags, instr, win, wout)


def norm_back(value, gain, cotangent):
    scale = lax.rsqrt(jnp.mean(value * value, axis=1, keepdims=True) + EPS)
    scaled = cotangent * gain
    inner = jnp.mean(scaled * value, axis=1, keepdims=True)
    unit = value * scale
    return scale * (scaled - unit * (scale * inner)), jnp.sum(cotangent * unit, axis=0, keepdims=True)


def back_kernel(
    x_ref, og_ref, pg_ref, flags_ref, instr_ref, mid_ref, dn2_ref, mix_ref, q_ref, k_ref, v_ref, p_hbm,
    gain1_ref, gain2_ref, wq_ref, wk_ref, wv_ref, wo_ref,
    ig_ref, dqkv_ref, dwo_ref, dgain_ref, diag_ref,
    band_ref, dwo_acc, normed_ref, grads_ref, dmix_ref, gm_ref, p_buf, ds_ref, sems,
):
    seq, seqs = pl.program_id(0), pl.num_programs(0)

    def p_copy(at):
        slot = lax.rem(at, 2)
        return pltpu.make_async_copy(
            p_hbm.at[lax.div(at, PAIRS), pl.ds(lax.rem(at, PAIRS) * 2, 2)], p_buf.at[slot], sems.at[slot]
        )

    @pl.when(seq == 0)
    def _():
        p_copy(0).start()
        band_ref[...] = jnp.zeros_like(band_ref)
        dwo_acc[...] = jnp.zeros_like(dwo_acc)
        dgain_ref[...] = jnp.zeros_like(dgain_ref)

    chosen, counts = pool_terms(flags_ref[0], instr_ref[0])
    grad_result = og_ref[...].astype(F32) + pool_gradient(chosen, counts, pg_ref[0])
    part, gain_part = norm_back(mid_ref[...], gain2_ref[...], dn2_ref[...])
    dgain_ref[1:2, :] += gain_part
    grad_middle = grad_result + part
    gm_ref[...] = grad_middle
    out_low = grad_middle.astype(BF16)
    dmix_ref[...] = dot_nt(out_low, wo_ref[...]).astype(BF16)
    dwo_acc[...] += dot_tn(mix_ref[...], out_low)

    rows = pl.ds(pl.multiple_of(seq * LENGTH, LENGTH), LENGTH)
    width = x_ref.shape[1]

    def one_pair(pair, _):
        at = seq * PAIRS + pair
        slot = lax.rem(at, 2)

        @pl.when(at + 1 < seqs * PAIRS)
        def _():
            p_copy(at + 1).start()

        p_copy(at).wait()
        lanes = pl.ds(pl.multiple_of(pair * BLOCK, BLOCK), BLOCK)
        queries, keys, grads = q_ref[:, lanes], k_ref[:, lanes], dmix_ref[:, lanes]
        values = jnp.concatenate([v_ref[:, lanes], jnp.full((LENGTH, BLOCK), -1.0, BF16)], axis=1)
        product = (grads.astype(F32) * mix_ref[:, lanes].astype(F32)).astype(BF16)
        dq = [None] * BLOCKS
        dk = [None] * BLOCKS
        dv = [None] * BLOCKS

        def add(total, index, part):
            total[index] = part if total[index] is None else total[index] + part

        for half in range(2):
            head = pair * 2 + half
            mask = half_mask(half)
            grad_half = grads * mask
            both = jnp.concatenate([grad_half, product * mask], axis=1)
            key_half, query_half = keys * mask, queries * mask
            for index in range(BLOCKS):
                first, last = columns_of(index)
                shift = 2 - index
                mine = span(index, index + 1)
                grad_prob = dot_nt(both[mine], values[span(first, last)])
                grad_scores = p_buf[slot, half, mine, span(first, last)].astype(F32) * grad_prob
                band_ref[head, :, span(first + shift, last + shift)] += grad_scores
                low = grad_scores.astype(BF16)
                ds_ref[half, mine, span(first, last)] = low
                add(dq, index, dot(low, key_half[span(first, last)]))
            for index in range(BLOCKS):
                first, last = columns_of(index)
                mine = span(index, index + 1)
                seen = span(first, last)
                add(dk, index, dot_tn(ds_ref[half, seen, mine], query_half[seen]))
                add(dv, index, dot_tn(p_buf[slot, half, seen, mine], grad_half[seen]))
        for which, total in enumerate((dq, dk, dv)):
            at_lane = pl.ds(pl.multiple_of(which * width + pair * BLOCK, BLOCK), BLOCK)
            for index in range(BLOCKS):
                at_row = pl.ds(pl.multiple_of(seq * LENGTH + index * BLOCK, BLOCK), BLOCK)
                grads_ref[at_row, at_lane] = total[index].astype(BF16)
        return 0

    lax.fori_loop(0, PAIRS, one_pair, 0)

    hidden = x_ref[...].astype(F32)
    scale = lax.rsqrt(jnp.mean(hidden * hidden, axis=1, keepdims=True) + EPS)
    normed_ref[rows, :] = (hidden * scale * gain1_ref[...]).astype(BF16)
    grad_normed = (
        dot_nt(grads_ref[rows, 0:width], wq_ref[...])
        + dot_nt(grads_ref[rows, width : 2 * width], wk_ref[...])
        + dot_nt(grads_ref[rows, 2 * width : 3 * width], wv_ref[...])
    )
    part, gain_part = norm_back(hidden, gain1_ref[...], grad_normed)
    dgain_ref[0:1, :] += gain_part
    ig_ref[...] = (gm_ref[...] + part).astype(BF16)

    @pl.when(seq == seqs - 1)
    def _():
        dwo_ref[...] = dwo_acc[...].astype(BF16)

        def one_part(part, _):
            lanes = pl.ds(pl.multiple_of(part * 256, 256), 256)
            dqkv_ref[:, lanes] = dot_tn(normed_ref[...], grads_ref[:, lanes]).astype(BF16)
            return 0

        lax.fori_loop(0, 3 * width // 256, one_part, 0)

        def one_head(head, _):
            total = jnp.zeros((8, 6 * BLOCK), F32)
            for group in range(BLOCK // 8):
                wide = band_ref[head, 8 * group : 8 * group + 8, :]
                wide = jnp.concatenate([wide, jnp.zeros((8, 6 * BLOCK - BAND), F32)], axis=1)
                total = total + pltpu.roll(wide, BLOCK - 8 * group, 1)
            line = iota((8, 6 * BLOCK), 0)
            turned = total
            for row in range(1, 8):
                turned = jnp.where(line == row, pltpu.roll(total, 6 * BLOCK - row, 1), turned)
            diag_ref[head] = jnp.broadcast_to(jnp.sum(turned, axis=0, keepdims=True), (8, 6 * BLOCK))
            return 0

        lax.fori_loop(0, HEADS, one_head, 0)


def back(x, og, pg, flags, instr, mid, dn2, mix, q, k, v, p, gain1, gain2, wq, wk, wv, wo):
    tokens, width = x.shape
    seqs = tokens // LENGTH
    rows = pl.BlockSpec((LENGTH, width), lambda s: (s, 0))
    flag_rows = pl.BlockSpec((1, 1, LENGTH), lambda s: (s, 0, 0))
    square = whole((width, width))
    return pl.pallas_call(
        back_kernel,
        name="back",
        grid=(seqs,),
        in_specs=[
            rows, rows, pl.BlockSpec((1, 2, width), lambda s: (s, 0, 0)), flag_rows, flag_rows,
            rows, rows, rows, rows, rows, rows, ANY,
            whole((1, width)), whole((1, width)), square, square, square, square,
        ],
        out_specs=[
            rows, whole((width, 3 * width)), square, whole((8, width)), whole((HEADS, 8, 6 * BLOCK)),
        ],
        out_shape=[
            jax.ShapeDtypeStruct((tokens, width), BF16), jax.ShapeDtypeStruct((width, 3 * width), BF16),
            jax.ShapeDtypeStruct((width, width), BF16), jax.ShapeDtypeStruct((8, width), F32),
            jax.ShapeDtypeStruct((HEADS, 8, 6 * BLOCK), F32),
        ],
        scratch_shapes=[
            pltpu.VMEM((HEADS, BLOCK, BAND), F32), pltpu.VMEM((width, width), F32), pltpu.VMEM((tokens, width), BF16),
            pltpu.VMEM((tokens, 3 * width), BF16), pltpu.VMEM((LENGTH, width), BF16), pltpu.VMEM((LENGTH, width), F32),
            pltpu.VMEM((2, 2, LENGTH, LENGTH), BF16), pltpu.VMEM((2, LENGTH, LENGTH), BF16), pltpu.SemaphoreType.DMA((2,)),
        ],
        compiler_params=pltpu.CompilerParams(vmem_limit_bytes=VMEM_LIMIT),
    )(x, og, pg, flags, instr, mid, dn2, mix, q, k, v, p, gain1, gain2, wq, wk, wv, wo)


DEPTH, WIDE, CORES = 4, 2, 2
MESH_ID = pl.DeviceIdType.MESH
GATHER_PHASES = 7
SCATTER_PHASES = 8
UP0, UP1, UP2, DOWN0, ACROSS_X, ACROSS_Y, ACROSS_C = range(7)


def place():
    grp, at = lax.axis_index("grp"), lax.axis_index("fsdp")
    z, x, core = lax.div(at, WIDE * CORES), lax.rem(lax.div(at, CORES), WIDE), lax.rem(at, CORES)

    def device(grp, z, x, core):
        return (grp, z * (WIDE * CORES) + x * CORES + core)

    edge = (z == 0) | (z == DEPTH - 1)
    low = z < DEPTH // 2
    return dict(
        y=grp, z=z, x=x, core=core, edge=edge, low=low,
        over_y=device(1 - grp, z, x, core),
        over_x=device(grp, z, 1 - x, core),
        over_core=device(grp, z, x, 1 - core),
        inward=device(grp, jnp.where(low, z + 1, z - 1), x, core),
        outward=device(grp, jnp.where(low, 0, DEPTH - 1), x, core),
    )


def greet(here):
    barrier = pltpu.get_barrier_semaphore()
    for name in ("over_y", "over_x", "over_core", "inward"):
        pl.semaphore_signal(barrier, inc=1, device_id=here[name], device_id_type=MESH_ID)

    @pl.when(jnp.logical_not(here["edge"]))
    def _():
        pl.semaphore_signal(barrier, inc=1, device_id=here["outward"], device_id_type=MESH_ID)
        pl.semaphore_wait(barrier, 5)

    @pl.when(here["edge"])
    def _():
        pl.semaphore_wait(barrier, 4)


def gather_phase(phase, piece, here, whole_ref, sent, got):
    y, z, x, core, edge, low = (here[name] for name in ("y", "z", "x", "core", "edge", "low"))
    inner = jnp.logical_not(edge)
    half = whole_ref.shape[-1] // 2
    mine = jnp.where(low, 0, DEPTH - 1)
    next_in = jnp.where(low, z + 1, z - 1)
    other_edge = DEPTH - 1 - mine

    def copy(where, channel, *target):
        ref = whole_ref.at[(piece, *where)]
        return pltpu.make_async_remote_copy(
            src_ref=ref, dst_ref=ref, send_sem=sent.at[channel, piece], recv_sem=got.at[channel, piece],
            device_id=target[0], device_id_type=MESH_ID,
        )

    line = lambda at: (at, x, core)
    x_half = (slice(None), x, core, slice(None), pl.ds(pl.multiple_of(y * half, half), half))
    x_half_in = (slice(None), 1 - x, core, slice(None), pl.ds(pl.multiple_of(y * half, half), half))
    y_half_in = (slice(None), 1 - x, core, slice(None), pl.ds(pl.multiple_of((1 - y) * half, half), half))
    inward, outward = here["inward"], here["outward"]
    if phase == 0:
        @pl.when(edge)
        def _():
            copy(line(z), 8, inward).start()

        @pl.when(inner)
        def _():
            copy(line(z), 0, inward).start()
            copy(line(z), 1, outward).start()
    elif phase == 1:
        @pl.when(inner)
        def _():
            copy(line(z), 0, inward).wait_send()
            copy(line(z), 1, outward).wait_send()
            copy(line(mine), 8, outward).wait_recv()
            copy(line(mine), 2, inward).start()
            copy(line(next_in), 0, inward).wait_recv()
            copy(line(next_in), 3, outward).start()

        @pl.when(edge)
        def _():
            copy(line(z), 8, inward).wait_send()
            copy(line(next_in), 1, inward).wait_recv()
    elif phase == 2:
        @pl.when(inner)
        def _():
            copy(line(mine), 2, inward).wait_send()
            copy(line(next_in), 3, outward).wait_send()
            copy(line(other_edge), 2, inward).wait_recv()
            copy(line(other_edge), 4, outward).start()

        @pl.when(edge)
        def _():
            copy(line(jnp.where(low, 2, 1)), 3, inward).wait_recv()
    elif phase == 3:
        @pl.when(inner)
        def _():
            copy(line(other_edge), 4, outward).wait_send()

        @pl.when(edge)
        def _():
            copy(line(other_edge), 4, inward).wait_recv()

        copy(x_half, 5, here["over_x"]).start()
    elif phase == 4:
        copy(x_half, 5, here["over_x"]).wait_send()
        copy(x_half_in, 5, here["over_x"]).wait_recv()
        copy(x_half_in, 6, here["over_y"]).start()
    elif phase == 5:
        copy(x_half_in, 6, here["over_y"]).wait_send()
        copy(y_half_in, 6, here["over_y"]).wait_recv()
        copy((slice(None), slice(None), core), 7, here["over_core"]).start()
    else:
        copy((slice(None), slice(None), core), 7, here["over_core"]).wait_send()
        copy((slice(None), slice(None), 1 - core), 7, here["over_core"]).wait_recv()


def scatter_phase(phase, piece, here, part_ref, out_ref, own, fromc, fromy, fromx, fromz, last, sent, got, own_sem):
    y, z, x, core, edge, low = (here[name] for name in ("y", "z", "x", "core", "edge", "low"))
    inner = jnp.logical_not(edge)
    half = part_ref.shape[-1] // 2
    slot = lax.rem(piece, 2)
    inward, outward = here["inward"], here["outward"]

    def remote(source, target, channel, device):
        return pltpu.make_async_remote_copy(
            src_ref=source, dst_ref=target, send_sem=sent.at[channel, piece], recv_sem=got.at[channel, piece],
            device_id=device, device_id_type=MESH_ID,
        )

    def lanes(which):
        return pl.ds(pl.multiple_of(which * half, half), half)

    def add(target, source):
        target[...] = (target[...].astype(F32) + source[...].astype(F32)).astype(BF16)

    total = fromc.at[piece]
    over_core = lambda: remote(part_ref.at[piece, :, :, 1 - core], fromc.at[piece], 0, here["over_core"])
    load = lambda: pltpu.make_async_copy(part_ref.at[piece, :, :, core], own.at[slot], own_sem.at[slot])
    over_y = lambda: remote(fromc.at[piece, :, 1 - x, :, lanes(1 - y)], fromy.at[piece], 1, here["over_y"])
    over_x = lambda: remote(fromc.at[piece, :, 1 - x, :, lanes(y)], fromx.at[piece], 2, here["over_x"])
    rest = pl.ds(jnp.where(low, 1, 0), 3)
    edge_in = lambda: remote(fromc.at[piece, rest, x], fromz.at[piece, pl.ds(0, 3)], 3, inward)
    far = pl.ds(jnp.where(low, 2, 0), 2)
    near = pl.ds(jnp.where(low, 0, 2), 2)
    across = lambda: remote(fromc.at[piece, far, x], fromz.at[piece, pl.ds(3, 2)], 4, inward)
    mine = jnp.where(low, 0, DEPTH - 1)
    back = lambda: remote(fromc.at[piece, mine, x], fromz.at[piece, 5], 5, outward)
    final = lambda: remote(fromc.at[piece, z, x], last.at[piece], 6, here["over_y"])

    if phase == 0:
        over_core().start()
        load().start()
    elif phase == 1:
        load().wait()
        over_core().wait()

        def one(at, _):
            for side in range(WIDE):
                add(total.at[at, side], own.at[slot, at, side])
            return 0

        lax.fori_loop(0, DEPTH, one, 0)
        over_y().start()
    elif phase == 2:
        over_y().wait()

        def one(at, _):
            add(total.at[at, 1 - x, :, lanes(y)], fromy.at[piece, at])
            return 0

        lax.fori_loop(0, DEPTH, one, 0)
        over_x().start()
    elif phase == 3:
        over_x().wait()

        def one(at, _):
            add(total.at[at, x, :, lanes(y)], fromx.at[piece, at])
            return 0

        lax.fori_loop(0, DEPTH, one, 0)

        @pl.when(edge)
        def _():
            edge_in().start()
    elif phase == 4:
        @pl.when(edge)
        def _():
            edge_in().wait_send()

        @pl.when(inner)
        def _():
            edge_in().wait_recv()
            for at in range(3):
                add(total.at[jnp.where(low, 1, 0) + at, x], fromz.at[piece, at])
            across().start()
    elif phase == 5:
        @pl.when(inner)
        def _():
            across().wait()
            for at in range(2):
                add(total.at[jnp.where(low, 0, 2) + at, x], fromz.at[piece, 3 + at])
            back().start()
    elif phase == 6:
        @pl.when(inner)
        def _():
            back().wait_send()

        @pl.when(edge)
        def _():
            back().wait_recv()
            add(total.at[z, x], fromz.at[piece, 5])

        final().start()
    else:
        final().wait()
        out_ref[piece] = fromc[piece, z, x].astype(F32) + last[piece].astype(F32)


def run_slot(slot, pieces, phases, stride, delay, act):
    for phase in reversed(range(phases)):
        since = slot - phase * delay
        piece = lax.div(since, stride)

        @pl.when((since >= 0) & (lax.rem(since, stride) == 0) & (piece < pieces))
        def _(phase=phase, piece=piece):
            act(phase, piece)


def gather_sems(pieces):
    return [pltpu.SemaphoreType.DMA((9, pieces)), pltpu.SemaphoreType.DMA((9, pieces))]


def scatter_scratch(pieces, rows, columns):
    return [
        pltpu.VMEM((2, DEPTH, WIDE, rows, columns), BF16),
        pltpu.VMEM((pieces, DEPTH, WIDE, rows, columns), BF16),
        pltpu.VMEM((pieces, DEPTH, rows, columns // 2), BF16),
        pltpu.VMEM((pieces, DEPTH, rows, columns // 2), BF16),
        pltpu.VMEM((pieces, 6, rows, columns), BF16),
        pltpu.VMEM((pieces, rows, columns), BF16),
        pltpu.SemaphoreType.DMA((7, pieces)),
        pltpu.SemaphoreType.DMA((7, pieces)),
        pltpu.SemaphoreType.DMA((2,)),
    ]


def gather_kernel(share_ref, whole_ref, sent, got, own_sem):
    here = place()
    pieces = share_ref.shape[0]
    own = [
        pltpu.make_async_copy(share_ref.at[piece], whole_ref.at[piece, here["z"], here["x"], here["core"]], own_sem.at[piece])
        for piece in range(pieces)
    ]
    for one in own:
        one.start()
    greet(here)
    for one in own:
        one.wait()

    def step(slot, _):
        run_slot(slot, pieces, GATHER_PHASES, 1, 1, lambda f, p: gather_phase(f, p, here, whole_ref, sent, got))
        return 0

    lax.fori_loop(0, pieces + GATHER_PHASES - 1, step, 0)


def gather_all(shares, collective_id):
    pieces, rows, columns = shares.shape
    return pl.pallas_call(
        gather_kernel,
        name="gather",
        in_specs=[ANY],
        out_specs=ANY,
        out_shape=jax.ShapeDtypeStruct((pieces, DEPTH, WIDE, CORES, rows, columns), shares.dtype),
        scratch_shapes=gather_sems(pieces) + [pltpu.SemaphoreType.DMA((pieces,))],
        compiler_params=pltpu.CompilerParams(collective_id=collective_id, has_side_effects=True),
    )(shares)


def scatter_kernel(part_ref, out_ref, *scratch):
    here = place()
    pieces = part_ref.shape[0]
    greet(here)

    def step(slot, _):
        run_slot(slot, pieces, SCATTER_PHASES, 1, 1, lambda f, p: scatter_phase(f, p, here, part_ref, out_ref, *scratch))
        return 0

    lax.fori_loop(0, pieces + SCATTER_PHASES - 1, step, 0)


def scatter_all(parts, collective_id):
    pieces, _, _, _, rows, columns = parts.shape
    return pl.pallas_call(
        scatter_kernel,
        name="scatter",
        in_specs=[ANY],
        out_specs=pl.BlockSpec(memory_space=pltpu.VMEM),
        out_shape=jax.ShapeDtypeStruct((pieces, rows, columns), F32),
        scratch_shapes=scatter_scratch(pieces, rows, columns),
        compiler_params=pltpu.CompilerParams(
            collective_id=collective_id, has_side_effects=True, vmem_limit_bytes=VMEM_LIMIT
        ),
    )(parts)


def shards(
    hidden_in, out_grad, pooled_gradient, gain_attn, w_query, w_key, w_value, w_output, rel_table, gain_ffn, w_in, w_out,
    pair_flags, instruction_mask, *, fast,
):
    width = hidden_in.shape[1]
    ff = w_in.shape[1]
    if fast:
        rows = w_query.shape[0]
        small = jnp.zeros((rows, width), BF16)
        small = small.at[:, 0].set(gain_attn).at[:, 1].set(gain_ffn).at[: rel_table.shape[0], 2].set(rel_table)
        pieces = jnp.concatenate(
            [
                jnp.stack([small, w_query, w_key, w_value, w_output]),
                w_in.reshape(rows, ff // width, width).transpose(1, 0, 2),
                w_out.reshape(ff // width, rows, width),
            ]
        )
        pieces = gather_all(pieces, 1).reshape(-1, width, width)
        small, wq, wk, wv, wo = (pieces[at] for at in range(5))
        win = pieces[5:9].transpose(1, 0, 2).reshape(width, ff)
        wout = pieces[9:13].reshape(ff // width, -1, rows, width).transpose(1, 0, 2, 3).reshape(ff, width)
        gain1, gain2 = small[:, 0], small[:, 1]
        rel = small[:, 2].reshape(-1, rows)[:, : rel_table.shape[0]].reshape(-1)
    else:
        gather = lambda one: lax.all_gather(one, "fsdp", axis=0, tiled=True)
        wq, wk, wv, wo, win, wout = map(gather, (w_query, w_key, w_value, w_output, w_in, w_out))
        gain1, gain2, rel = map(gather, (gain_attn, gain_ffn, rel_table))
    gain1, gain2 = gain1.astype(F32)[None, :], gain2.astype(F32)[None, :]
    position = jnp.arange(2 * LENGTH, dtype=jnp.int32)
    onehot = bucket_of(position - 3 * BLOCK)[None, :] == jnp.arange(BUCKETS, dtype=jnp.int32)[:, None]
    table = lax.dot_general(
        rel.reshape(BUCKETS, HEADS), onehot.astype(BF16), (((0,), (0,)), ((), ())), preferred_element_type=F32
    )
    table = jnp.pad(table, ((0, 16 - HEADS), (0, 0)))
    flags = pair_flags.reshape(-1, 1, LENGTH)
    instr = instruction_mask.reshape(-1, 1, LENGTH)
    q, k, v, p, mix, mid, n2, bg = attend(
        hidden_in, out_grad, pooled_gradient, flags, instr, gain1, gain2, table, wq, wk, wv, wo
    )
    output, pooled, dn2, dwin, dwout = feed(n2, bg, mid, flags, instr, win, wout)
    input_grad, dqkv, dwo, dgain, diag = back(
        hidden_in, out_grad, pooled_gradient, flags, instr, mid, dn2, mix, q, k, v, p, gain1, gain2, wq, wk, wv, wo
    )
    offset = jnp.arange(6 * BLOCK, dtype=jnp.int32) - 3 * BLOCK
    buckets = (bucket_of(offset)[:, None] == jnp.arange(BUCKETS, dtype=jnp.int32)[None, :]).astype(F32)
    grad_table = jnp.dot(diag[:, 0, :], buckets, precision=lax.Precision.HIGHEST).T.reshape(-1)
    if fast:
        devices = width // rows
        small = jnp.zeros((devices, rows, width), F32)
        small = small.at[:, :, 0].set(dgain[0].reshape(devices, rows)).at[:, :, 1].set(dgain[1].reshape(devices, rows))
        small = small.at[:, : rel_table.shape[0], 2].set(grad_table.reshape(devices, -1))
        parts = [small.astype(BF16)[None]]
        parts += [dqkv[:, at * width : (at + 1) * width].reshape(1, devices, rows, width) for at in range(3)]
        parts += [dwo.reshape(1, devices, rows, width)]
        parts += [dwin.reshape(devices, rows, ff // width, width).transpose(2, 0, 1, 3)]
        parts += [dwout.reshape(devices, ff // width, rows, width).transpose(1, 0, 2, 3)]
        sums = scatter_all(jnp.concatenate(parts).reshape(-1, DEPTH, WIDE, CORES, rows, width), 2)
        small = sums[0]
        return (
            output, pooled, input_grad,
            small[:, 0], sums[1], sums[2], sums[3], sums[4], small[: rel_table.shape[0], 2], small[:, 1],
            sums[5:9].transpose(1, 0, 2).reshape(rows, ff), sums[9:13].reshape(-1, width),
        )
    scatter = lambda one: lax.psum(lax.psum_scatter(one, "fsdp", scatter_dimension=0, tiled=True), "grp").astype(F32)
    return (
        output, pooled, input_grad,
        scatter(dgain[0]), scatter(dqkv[:, :width]), scatter(dqkv[:, width : 2 * width]), scatter(dqkv[:, 2 * width :]),
        scatter(dwo), scatter(grad_table), scatter(dgain[1]), scatter(dwin), scatter(dwout),
    )


def solution(mesh):
    tokens, square, line = P(("grp", "fsdp"), None), P("fsdp", None), P("fsdp")
    cube, flat = P(("grp", "fsdp"), None, None), P(("grp", "fsdp"))
    fast = mesh.shape["fsdp"] == DEPTH * WIDE * CORES and mesh.shape["grp"] == 2
    return jax.shard_map(
        partial(shards, fast=fast),
        mesh=mesh,
        in_specs=(tokens, tokens, cube, line, square, square, square, square, line, line, square, square, flat, flat),
        out_specs=(tokens, cube, tokens, line, square, square, square, square, line, line, square, square),
        check_vma=False,
    )
```

```python
from functools import partial

import jax
import jax.numpy as jnp
from jax import lax
from jax.experimental import pallas as pl
from jax.experimental.pallas import tpu as pltpu
from jax.sharding import PartitionSpec as P

HEADS = 12
HEAD_DIM = 64
BUCKETS = 32
LENGTH = 512
BLOCK = 128
BLOCKS = LENGTH // BLOCK
BAND_BLOCKS = 2 * BLOCKS - 1
BAND = BAND_BLOCKS * BLOCK
OFFSETS = BAND + BLOCK
GROUPS = 3
GROUP = HEADS // GROUPS
GROUP_ROWS = GROUP * HEAD_DIM
OWNERS, PARTS, SHARE = 16, 4, 48
TABLE_SHARE = HEADS * BUCKETS // OWNERS
SMALL = 256
EPS = 1e-06
NEG = -1e30
LIMITS = (12, 16, 23, 32, 46, 64, 91)
ROOT = 0.7978845608028654
CUBE = 0.044715
F32 = jnp.float32
BF16 = jnp.bfloat16
ANY = pl.BlockSpec(memory_space=pl.ANY)
VMEM_LIMIT = 63 * 1024 * 1024


def bucket_of(offset):
    distance = jnp.abs(offset)
    far_bucket = jnp.full(offset.shape, 8, jnp.int32)
    for threshold in LIMITS:
        far_bucket = far_bucket + (distance >= threshold).astype(jnp.int32)
    near_bucket = jnp.where(distance < 8, distance, far_bucket)
    return near_bucket + BUCKETS // 2 * (offset > 0).astype(jnp.int32)


def dot(a, b):
    return lax.dot_general(a, b, (((1,), (0,)), ((), ())), preferred_element_type=F32)


def dot_nt(a, b):
    return lax.dot_general(a, b, (((1,), (1,)), ((), ())), preferred_element_type=F32)


def dot_tn(a, b):
    return lax.dot_general(a, b, (((0,), (0,)), ((), ())), preferred_element_type=F32)


def dot_tt(a, b):
    return lax.dot_general(a, b, (((0,), (1,)), ((), ())), preferred_element_type=F32)


def iota(shape, axis):
    return lax.broadcasted_iota(jnp.int32, shape, axis)


def whole(shape):
    zeros = (0,) * len(shape)
    return pl.BlockSpec(shape, lambda *_: zeros, pipeline_mode=pl.Buffered(1))


def span(first, last):
    return slice(first * BLOCK, last * BLOCK)


def pool_terms(flags, instruction):
    kept = (instruction == 0).astype(F32)
    chosen = [kept * (flags == part).astype(F32) for part in range(2)]
    counts = [jnp.sum(one, axis=1, keepdims=True) for one in chosen]
    return chosen, counts


def pool_gradient(chosen, counts, pooled_grad):
    row = iota((16, LENGTH), 0)
    picks = jnp.where(row % 2 == 0, chosen[0], chosen[1])
    picks = jnp.where(row < 6, picks, 0.0).astype(BF16)
    scaled = [pooled_grad[part : part + 1, :] / counts[part] for part in range(2)]
    line = iota((16, pooled_grad.shape[1]), 0)
    both = jnp.where(line % 2 == 0, scaled[0], scaled[1])
    high = both.astype(BF16).astype(F32)
    rest = both - high
    middle = rest.astype(BF16).astype(F32)
    low = rest - middle
    parts = jnp.where(line < 2, high, jnp.where(line < 4, middle, jnp.where(line < 6, low, 0.0)))
    return dot_tn(picks, parts.astype(BF16))


def norm_back(value, gain, cotangent):
    scale = lax.rsqrt(jnp.mean(value * value, axis=1, keepdims=True) + EPS)
    scaled = cotangent * gain
    unit = value * scale
    inner = jnp.mean(scaled * unit, axis=1, keepdims=True)
    return scale * (scaled - unit * inner), jnp.sum(cotangent * unit, axis=0, keepdims=True)


def table_places():
    at = iota((1, OWNERS * SHARE), 1)
    owner = sum((at >= SHARE * one).astype(jnp.int32) for one in range(1, OWNERS))
    inside = at - SHARE * owner
    entry = owner * TABLE_SHARE + inside
    bucket = sum((entry >= HEADS * one).astype(jnp.int32) for one in range(1, BUCKETS))
    return entry - HEADS * bucket, jnp.where(inside < TABLE_SHARE, bucket, -1)


DEPTH, WIDE, CORES = 4, 2, 2
MESH_ID = pl.DeviceIdType.MESH


def place():
    grp, at = lax.axis_index("grp"), lax.axis_index("fsdp")
    z, x, core = lax.div(at, WIDE * CORES), lax.rem(lax.div(at, CORES), WIDE), lax.rem(at, CORES)

    def device(grp, z, x, core):
        return (grp, z * (WIDE * CORES) + x * CORES + core)

    return dict(
        z=z, x=x, core=core,
        over_y=device(1 - grp, z, x, core),
        over_x=device(grp, z, 1 - x, core),
        over_core=device(grp, z, x, 1 - core),
        over_z=[device(grp, lax.rem(z + one, DEPTH), x, core) for one in range(1, DEPTH)],
        ahead=[lax.rem(z + one, DEPTH) for one in range(1, DEPTH)],
        behind=[lax.rem(z + DEPTH - one, DEPTH) for one in range(1, DEPTH)],
    )


def greet(here):
    barrier = pltpu.get_barrier_semaphore()
    for device in (here["over_y"], here["over_x"], here["over_core"], *here["over_z"]):
        pl.semaphore_signal(barrier, inc=1, device_id=device, device_id_type=MESH_ID)
    pl.semaphore_wait(barrier, DEPTH + 2)


def gather_phase(phase, sem, here, share_ref, whole_ref, sent, got, own_sem):
    z, x, core = here["z"], here["x"], here["core"]

    def copy(source, where, channel, device):
        return pltpu.make_async_remote_copy(
            src_ref=source, dst_ref=whole_ref.at[where], send_sem=sent.at[channel, sem], recv_sem=got.at[channel, sem],
            device_id=device, device_id_type=MESH_ID,
        )

    own = lambda: pltpu.make_async_copy(share_ref, whole_ref.at[z, x, core], own_sem.at[sem])
    every = slice(None)
    line_out = lambda one: copy(share_ref, (z, x, core), one, here["over_z"][one])
    line_in = lambda one: copy(share_ref, (here["behind"][one], x, core), one, here["over_z"][one])
    side_out = lambda: copy(whole_ref.at[every, x, core], (every, x, core), 3, here["over_x"])
    side_in = lambda: copy(whole_ref.at[every, x, core], (every, 1 - x, core), 3, here["over_x"])
    core_out = lambda: copy(whole_ref.at[every, every, core], (every, every, core), 4, here["over_core"])
    core_in = lambda: copy(whole_ref.at[every, every, core], (every, every, 1 - core), 4, here["over_core"])
    if phase == 0:
        own().start()
        for one in range(DEPTH - 1):
            line_out(one).start()
    elif phase == 1:
        own().wait()
        for one in range(DEPTH - 1):
            line_in(one).wait_recv()
        side_out().start()
    elif phase == 2:
        side_in().wait_recv()
        core_out().start()
    else:
        for one in range(DEPTH - 1):
            line_out(one).wait_send()
        side_out().wait_send()
        core_out().wait_send()
        core_in().wait_recv()


def scatter_phase(phase, piece, here, part_ref, out_ref, own, fromc, fromx, fromz, last, sent, got, own_sem):
    z, x, core = here["z"], here["x"], here["core"]
    slot = lax.rem(piece, 2)

    def remote(source, target, channel, device):
        return pltpu.make_async_remote_copy(
            src_ref=source, dst_ref=target, send_sem=sent.at[channel, piece], recv_sem=got.at[channel, piece],
            device_id=device, device_id_type=MESH_ID,
        )

    total = fromc.at[piece]
    over_core = lambda: remote(part_ref.at[:, :, 1 - core], total, 0, here["over_core"])
    load = lambda: pltpu.make_async_copy(part_ref.at[:, :, core], own.at[slot], own_sem.at[slot])
    over_x = lambda: remote(fromc.at[piece, :, 1 - x], fromx.at[piece], 1, here["over_x"])
    line_out = lambda one: remote(fromc.at[piece, here["ahead"][one], x], fromz.at[piece, z], 2 + one, here["over_z"][one])
    line_in = lambda one: remote(
        fromc.at[piece, z, x], fromz.at[piece, here["behind"][one]], 2 + one, here["over_z"][one]
    )
    final = lambda: remote(fromc.at[piece, z, x], last.at[piece], 5, here["over_y"])

    if phase == 0:
        over_core().start()
        load().start()
    elif phase == 1:
        load().wait()
        over_core().wait()

        def one(at, _):
            for side in range(WIDE):
                mine = own[slot, at, side].astype(F32) + fromc[piece, at, side].astype(F32)
                fromc[piece, at, side] = mine.astype(BF16)
            return 0

        lax.fori_loop(0, DEPTH, one, 0)
        over_x().start()
    elif phase == 2:
        over_x().wait()

        def one(at, _):
            mine = fromc[piece, at, x].astype(F32) + fromx[piece, at].astype(F32)
            fromc[piece, at, x] = mine.astype(BF16)
            return 0

        lax.fori_loop(0, DEPTH, one, 0)
        for one in range(DEPTH - 1):
            line_out(one).start()
    elif phase == 3:
        mine = fromc[piece, z, x].astype(F32)
        for one in range(DEPTH - 1):
            line_in(one).wait_recv()
            mine = mine + fromz[piece, here["behind"][one]].astype(F32)
        fromc[piece, z, x] = mine.astype(BF16)
        final().start()
    else:
        for one in range(DEPTH - 1):
            line_out(one).wait_send()
        final().wait()
        out_ref[piece] = fromc[piece, z, x].astype(F32) + last[piece].astype(F32)


def run_slot(slot, table, act):
    for phase in reversed(range(max(map(len, table.values())))):
        due, found = False, 0
        for piece, slots in table.items():
            if slots[phase] is not None:
                now = slot == slots[phase]
                due, found = due | now, jnp.where(now, piece, found)
        if due is not False:

            @pl.when(due)
            def _(phase=phase, found=found):
                act(phase, found)


def run_rest(first, tables, travel):
    end = 1 + max(slot for table in tables for slots in table.values() for slot in slots if slot is not None)

    def one(slot, _):
        travel(slot)
        return 0

    if end > first:
        lax.fori_loop(first, end, one, 0)


def gather_sems(pieces):
    return [pltpu.SemaphoreType.DMA((5, pieces)), pltpu.SemaphoreType.DMA((5, pieces)), pltpu.SemaphoreType.DMA((pieces,))]


def scatter_scratch(pieces, rows, columns):
    return [
        pltpu.VMEM((2, DEPTH, WIDE, rows, columns), BF16),
        pltpu.VMEM((pieces, DEPTH, WIDE, rows, columns), BF16),
        pltpu.VMEM((pieces, DEPTH, rows, columns), BF16),
        pltpu.VMEM((pieces, DEPTH, rows, columns), BF16),
        pltpu.VMEM((pieces, rows, columns), BF16),
        pltpu.SemaphoreType.DMA((6, pieces)),
        pltpu.SemaphoreType.DMA((6, pieces)),
        pltpu.SemaphoreType.DMA((2,)),
    ]


ATTEND_PIECES, FEED_PIECES = 8, 4
ATTEND_TABLE = {
    1: (None, 0, 3, 5),
    2: (0, 4, 8, 10),
    3: (3, 8, 12, 14),
    4: (6, 11, 15, 17),
    5: (9, 14, 18, 20),
    6: (12, 17, 21, 23),
    7: (15, 20, 24, 25),
}
FEED_GATHER = {0: (0, 5, 10, 12), 1: (3, 8, 13, 15), 2: (6, 11, 16, 18), 3: (9, 14, 19, 21)}
FEED_SUMS = 5
FEED_SCATTER = {
    0: (8, 10, 15, 20, 23), 1: (11, 13, 18, 23, 26), 2: (16, 18, 23, 28, 31), 3: (19, 21, 26, 31, 34), 4: (24, 26, 31, 36, 39),
}
BACK_BEFORE, BACK_SUMS = 4, 6
BACK_SCATTER = {
    0: (0, 2, 7, 12, 15), 1: (3, 5, 10, 15, 18), 2: (6, 8, 13, 18, 21), 3: (9, 11, 16, 21, 24),
    4: (12, 14, 19, 24, 27), 5: (16, 18, 23, 27, 29),
}
TAIL_SUMS = 4
TAIL_SCATTER = {0: (24, 25, 26, 27, 28), 1: (25, 26, 27, 28, 29), 2: (26, 27, 28, 29, 30), 3: (27, 28, 29, 30, 31)}


def attend_kernel(
    x_ref, og_ref, pg_ref, flags_ref, instr_ref, shares_hbm, small_hbm,
    qkv_ref, p_ref, inv_ref, mix_ref, mid_ref, n2_ref, bg_ref, gains_ref, weights_hbm, smalls_hbm,
    band_ref, aux_ref, normed_ref, wg_ref, wo_ref, small_ref, table_ref, cur_ref, nxt_ref, sa_ref, sb_ref, sems,
    *comm, fast,
):
    group, seq = pl.program_id(0), pl.program_id(1)
    seqs = pl.num_programs(1)
    step = group * seqs + seq
    width = x_ref.shape[1]
    if fast:
        main_sems, first_sems, small_sems = comm[0:3], comm[3:6], comm[6:9]
        here = place()

        def main(phase, piece):
            gather_phase(phase, piece, here, shares_hbm.at[piece], weights_hbm.at[piece], *main_sems)

        def small(phase):
            gather_phase(phase, 0, here, small_hbm.at[0], smalls_hbm.at[0], *small_sems)

        def first(phase, which):
            lanes = pl.ds(which * GROUP_ROWS, GROUP_ROWS)
            every = slice(None)
            gather_phase(
                phase, which, here, shares_hbm.at[0, :, lanes], weights_hbm.at[0, every, every, every, every, lanes], *first_sems
            )

        def travel(slot):
            run_slot(slot, ATTEND_TABLE, main)

        point = lambda at: travel(2 * step + at)
    else:
        point = lambda at: None
    load_small = lambda: pltpu.make_async_copy(smalls_hbm.at[0], small_ref, sems.at[0])
    load_group = lambda at: pltpu.make_async_copy(weights_hbm.at[at], wg_ref, sems.at[1])
    load_output = lambda: pltpu.make_async_copy(weights_hbm.at[GROUPS], wo_ref, sems.at[2])
    square = lambda ref: ref[...].reshape(width, width)

    def prepare(at):
        flags = flags_ref[at]
        chosen, counts = pool_terms(flags, instr_ref[at])
        rows = pl.ds(pl.multiple_of(at * LENGTH, LENGTH), LENGTH)
        grad_result = og_ref[rows, :].astype(F32) + pool_gradient(chosen, counts, pg_ref[at])
        bg_ref[rows, :] = grad_result.astype(BF16)
        row = iota((16, LENGTH), 0)
        aux_ref[0, at] = jnp.where(row == 0, 1 - flags, jnp.where(row == 1, flags, 0)).astype(F32).astype(BF16)
        other = jnp.where(row == 0, flags, jnp.where(row == 1, 1 - flags, 0)).astype(F32) * NEG
        aux_ref[1, at] = other.astype(BF16)
        hidden = x_ref[rows, :].astype(F32)
        scale = lax.rsqrt(jnp.mean(hidden * hidden, axis=1, keepdims=True) + EPS)
        normed_ref[at] = (hidden * scale * gains_ref[0:1, :]).astype(BF16)

    def project(at, target):
        target[...] = dot_tt(square(wg_ref), normed_ref[at]).astype(BF16)

    def part(source, which, head):
        first = which * GROUP_ROWS + head * HEAD_DIM
        return source[first : first + HEAD_DIM, :]

    def score(source, at_group, at, head, target):
        queries = jnp.concatenate([part(source, 0, head), aux_ref[0, at]], axis=0)
        keys = jnp.concatenate([part(source, 1, head), aux_ref[1, at]], axis=0)
        scores = dot_tn(keys, queries)
        for row in range(BLOCKS):
            for column in range(BLOCKS):
                bias = band_ref[at_group * GROUP + head, span(row - column + BLOCKS - 1, row - column + BLOCKS), :]
                target[span(row, row + 1), span(column, column + 1)] = scores[span(row, row + 1), span(column, column + 1)] + bias

    def soften(head, source):
        scores = source[...]
        exponent = jnp.exp(scores - jnp.max(scores, axis=0, keepdims=True)).astype(BF16)
        p_ref[0, 0, head] = exponent
        values = jnp.concatenate([part(cur_ref, 2, head), jnp.ones((16, LENGTH), BF16)], axis=0)
        mixed = dot(values, exponent)
        inverse = 1.0 / mixed[HEAD_DIM : HEAD_DIM + 1, :]
        inv_ref[0, 0, head] = inverse
        mix_ref[group, seq, head * HEAD_DIM : (head + 1) * HEAD_DIM, :] = (mixed[0:HEAD_DIM, :] * inverse).astype(BF16)

    def read_small():
        load_small().start()
        load_small().wait()
        flipped = small_ref[...].reshape(width, SMALL)[:, 0:BLOCK].astype(F32).T
        gains_ref[...] = flipped[0:8, :]
        heads, buckets = table_places()
        entries = jnp.where((iota((16, width), 0) == heads) & (buckets >= 0), flipped[2:3, :], 0.0).astype(BF16)
        onehot = (bucket_of(iota((OFFSETS, 1), 0) - BLOCKS * BLOCK) == buckets).astype(F32).astype(BF16)
        table_ref[...] = dot_nt(entries, onehot)

    def make_bands():
        def one_head(head, _):
            table = table_ref[...]
            line = jnp.sum(jnp.where(iota(table.shape, 0) == head, table, 0.0), axis=0, keepdims=True)
            turned = pltpu.roll(jnp.broadcast_to(line, (BLOCK, OFFSETS)), 0, 1, stride=1, stride_axis=0)
            band_ref[head] = turned[:, BLOCK:].T
            return 0

        lax.fori_loop(0, HEADS, one_head, 0)

    def prepare_all():
        def one_seq(at, _):
            prepare(at)
            return 0

        lax.fori_loop(0, seqs, one_seq, 0)

    @pl.when(step == 0)
    def _():
        if fast:
            greet(here)
            small(0)
            for which in range(3):
                first(0, which)
            small(1)
            first(1, 0)
            small(2)
            first(1, 1)
            small(3)
            read_small()
            first(1, 2)
            main(0, 1)
            first(2, 0)
            prepare_all()
            first(2, 1)
            make_bands()
            first(2, 2)
            for which in range(3):
                first(3, which)
        else:
            read_small()
            prepare_all()
            make_bands()
        load_group(0).start()
        load_group(0).wait()
        project(0, nxt_ref)
        score(nxt_ref, 0, 0, 0, sa_ref)

    last_seq = seq == seqs - 1
    more = step + 1 < GROUPS * seqs
    cur_ref[...] = nxt_ref[...]
    qkv_ref[0, 0] = nxt_ref[...]

    @pl.when(last_seq & more)
    def _():
        load_group(group + 1).start()

    @pl.when((seq == 0) & (group == GROUPS - 1))
    def _():
        load_output().start()
        load_output().wait()

    next_seq = jnp.where(last_seq, 0, seq + 1)
    next_group = jnp.where(last_seq, jnp.minimum(group + 1, GROUPS - 1), group)
    point(0)
    score(cur_ref, group, seq, 1, sb_ref)
    soften(0, sa_ref)
    score(cur_ref, group, seq, 2, sa_ref)
    soften(1, sb_ref)
    point(1)
    score(cur_ref, group, seq, 3, sb_ref)
    soften(2, sa_ref)

    @pl.when(last_seq & more)
    def _():
        load_group(group + 1).wait()

    project(next_seq, nxt_ref)
    score(nxt_ref, next_group, next_seq, 0, sa_ref)
    soften(3, sb_ref)

    @pl.when(group == GROUPS - 1)
    def _():
        rows = pl.ds(pl.multiple_of(seq * LENGTH, LENGTH), LENGTH)
        middle = x_ref[rows, :].astype(F32)
        output = square(wo_ref)
        for one in range(GROUPS):
            middle = middle + dot_tn(mix_ref[one, seq], output[one * GROUP_ROWS : (one + 1) * GROUP_ROWS, :])
        mid_ref[...] = middle
        scale = lax.rsqrt(jnp.mean(middle * middle, axis=1, keepdims=True) + EPS)
        n2_ref[...] = (middle * scale * gains_ref[1:2, :]).astype(BF16)

    if fast:

        @pl.when(step == GROUPS * seqs - 1)
        def _():
            run_rest(2 * GROUPS * (x_ref.shape[0] // LENGTH), [ATTEND_TABLE], travel)


def attend(x, og, pg, flags, instr, shares, small, fast):
    tokens, width = x.shape
    seqs = tokens // LENGTH
    last_rows = pl.BlockSpec((LENGTH, width), lambda g, s: (jnp.where(g == GROUPS - 1, s, 0), 0))
    low = jax.ShapeDtypeStruct((tokens, width), BF16)
    out_specs = [
        pl.BlockSpec((1, 1, width, LENGTH), lambda g, s: (g, s, 0, 0)),
        pl.BlockSpec((1, 1, GROUP, LENGTH, LENGTH), lambda g, s: (g, s, 0, 0, 0)),
        pl.BlockSpec((1, 1, GROUP, 1, LENGTH), lambda g, s: (g, s, 0, 0, 0)),
        whole((GROUPS, seqs, GROUP_ROWS, LENGTH)), last_rows, last_rows, whole((tokens, width)), whole((8, width)),
    ]
    out_shape = [
        jax.ShapeDtypeStruct((GROUPS, seqs, width, LENGTH), BF16),
        jax.ShapeDtypeStruct((GROUPS, seqs, GROUP, LENGTH, LENGTH), BF16),
        jax.ShapeDtypeStruct((GROUPS, seqs, GROUP, 1, LENGTH), F32),
        jax.ShapeDtypeStruct((GROUPS, seqs, GROUP_ROWS, LENGTH), BF16),
        jax.ShapeDtypeStruct((tokens, width), F32), low, low, jax.ShapeDtypeStruct((8, width), F32),
    ]
    scratch = [
        pltpu.VMEM((HEADS, BAND, BLOCK), F32), pltpu.VMEM((2, seqs, 16, LENGTH), BF16),
        pltpu.VMEM((seqs, LENGTH, width), BF16), pltpu.VMEM((DEPTH, WIDE, CORES, SHARE, width), BF16),
        pltpu.VMEM((DEPTH, WIDE, CORES, SHARE, width), BF16), pltpu.VMEM((DEPTH, WIDE, CORES, SHARE, SMALL), BF16), pltpu.VMEM((16, OFFSETS), F32),
        pltpu.VMEM((width, LENGTH), BF16), pltpu.VMEM((width, LENGTH), BF16),
        pltpu.VMEM((LENGTH, LENGTH), F32), pltpu.VMEM((LENGTH, LENGTH), F32), pltpu.SemaphoreType.DMA((3,)),
    ]
    in_specs = [
        whole((tokens, width)), whole((tokens, width)), whole((seqs, 2, width)), whole((seqs, 1, LENGTH)),
        whole((seqs, 1, LENGTH)), ANY, ANY,
    ]
    if fast:
        kernel = partial(attend_kernel, fast=True)
        out_specs += [ANY, ANY]
        out_shape += [
            jax.ShapeDtypeStruct((ATTEND_PIECES, DEPTH, WIDE, CORES, SHARE, width), BF16),
            jax.ShapeDtypeStruct((1, DEPTH, WIDE, CORES, SHARE, SMALL), BF16),
        ]
        scratch += gather_sems(ATTEND_PIECES) + gather_sems(3) + gather_sems(1)
    else:

        def kernel(*refs):
            inputs, outputs, rest = refs[:7], refs[7:15], refs[15:]
            attend_kernel(*inputs, *outputs, inputs[5], inputs[6], *rest, fast=False)

    return pl.pallas_call(
        kernel,
        name="attend",
        grid=(GROUPS, seqs),
        in_specs=in_specs,
        out_specs=out_specs,
        out_shape=out_shape,
        scratch_shapes=scratch,
        compiler_params=pltpu.CompilerParams(
            vmem_limit_bytes=VMEM_LIMIT, collective_id=1 if fast else None, has_side_effects=fast
        ),
    )(x, og, pg, flags, instr, shares, small)


def feed_kernel(
    n2_ref, bg_ref, mid_hbm, flags_ref, instr_ref, pg_ref, gains_ref, og_ref, mid_ref, mix_ref, early_hbm, late_hbm,
    out_ref, pooled_ref, gm_ref, dmix_ref, parts_hbm, *rest, fast,
):
    if fast:
        sums_ref, gathered_hbm = rest[0:2]
        rest = rest[2:]
    res_ref, dn2_ref, act_ref, dinner_ref, win_ref, wout_ref, wo_ref, dwo_ref, staged_ref, sems = rest[:10]
    part, block = pl.program_id(0), pl.program_id(1)
    blocks = pl.num_programs(1)
    step = part * blocks + block
    width = n2_ref.shape[1]
    rows = pl.ds(pl.multiple_of(block * LENGTH, LENGTH), LENGTH)
    if fast:
        sems_of, scratch = rest[10:13], rest[13:]
        here = place()

        def travel(slot):
            def bring(phase, piece):
                share = late_hbm.at[ATTEND_PIECES + piece]
                gather_phase(phase, piece, here, share, gathered_hbm.at[piece], *sems_of)

            def add(phase, piece):
                scatter_phase(phase, piece, here, parts_hbm.at[piece], sums_ref, *scratch)

            run_slot(slot, FEED_GATHER, bring)
            run_slot(slot, FEED_SCATTER, add)

        point = lambda at: travel(2 * step + at)
    else:
        point = lambda at: None
    square = lambda ref: ref[...].reshape(width, width)

    def weights(at, start):
        def both(source, first):
            for which, target in enumerate((win_ref, wout_ref)):
                slot = lax.rem(at, 2)
                copy = pltpu.make_async_copy(source.at[first + which], target.at[slot], sems.at[slot, which])
                copy.start() if start else copy.wait()

        if start:
            pl.when(at < PARTS // 2)(lambda: both(early_hbm, 4 + 2 * at))
            pl.when(at >= PARTS // 2)(lambda: both(gathered_hbm if fast else late_hbm, 2 * at + (-PARTS if fast else 4)))
        else:
            both(early_hbm, 4)

    load_middle = lambda: pltpu.make_async_copy(mid_hbm, res_ref, sems.at[0, 2])
    load_output = lambda: pltpu.make_async_copy(early_hbm.at[GROUPS], wo_ref, sems.at[1, 2])
    keep = lambda at, which: pltpu.make_async_copy(staged_ref.at[which], parts_hbm.at[2 * at + which], sems.at[which, 3])

    @pl.when(step == 0)
    def _():
        load_middle().start()
        load_output().start()
        weights(0, True)
        if fast:
            greet(here)
        dn2_ref[...] = jnp.zeros_like(dn2_ref)
        dwo_ref[...] = jnp.zeros_like(dwo_ref)
        load_middle().wait()
        load_output().wait()

    @pl.when((part < PARTS) & (block == 0))
    def _():
        weights(part, False)

    @pl.when((part > 0) & (block == 0))
    def _():
        keep(part - 1, 0).wait()
        keep(part - 1, 1).wait()

    point(0)

    @pl.when(part < PARTS)
    def _():
        slot = lax.rem(part, 2)
        inner = dot(n2_ref[rows, :], square(win_ref.at[slot]))
        squared = inner * inner
        half = 0.5 * jnp.tanh(inner * (ROOT + (ROOT * CUBE) * squared)) + 0.5
        active = inner * half
        slope = half + active * (1.0 - half) * (2.0 * ROOT + (6.0 * ROOT * CUBE) * squared)
        active = active.astype(BF16)
        act_ref[rows, :] = active
        dinner = (dot_nt(bg_ref[rows, :], square(wout_ref.at[slot])) * slope).astype(BF16)
        dinner_ref[rows, :] = dinner
        res_ref[rows, :] += dot(active, square(wout_ref.at[slot]))
        dn2_ref[rows, :] += dot_nt(dinner, square(win_ref.at[slot]))

    point(1)

    @pl.when((part < PARTS - 1) & (block == blocks - 1))
    def _():
        weights(part + 1, True)

    def stage(which, first, value):
        for owner in range(OWNERS):
            z, x, core = owner // 4, owner // 2 % 2, owner % 2
            staged_ref[which, z, x, core, :, first : first + 256] = value[SHARE * owner : SHARE * (owner + 1), :]

    @pl.when((part < PARTS) & (block == blocks - 1))
    def _():
        for first in range(0, width, 256):
            stage(0, first, dot_tn(n2_ref[...], dinner_ref[:, first : first + 256]).astype(BF16))
        keep(part, 0).start()
        for first in range(0, width, 256):
            stage(1, first, dot_tn(act_ref[...], bg_ref[:, first : first + 256]).astype(BF16))
        keep(part, 1).start()

    @pl.when(part == PARTS)
    def _():
        result = res_ref[rows, :]
        out_ref[...] = result.astype(BF16)
        chosen, counts = pool_terms(flags_ref[block], instr_ref[block])
        line = iota((8, LENGTH), 0)
        picks = jnp.where(line == 0, chosen[0], jnp.where(line == 1, chosen[1], 0.0)).astype(BF16)
        high = result.astype(BF16)
        low = (result - high.astype(F32)).astype(BF16)
        total = dot(picks, high) + dot(picks, low)
        total = total / jnp.where(iota((8, 1), 0) == 0, counts[0], counts[1])
        pooled_ref[block] = total[0:2, :]
        grad_result = og_ref[...].astype(F32) + pool_gradient(chosen, counts, pg_ref[block])
        change, _ = norm_back(mid_ref[...], gains_ref[1:2, :], dn2_ref[rows, :])
        grad_middle = grad_result + change
        gm_ref[...] = grad_middle
        out_low = grad_middle.astype(BF16)
        output = square(wo_ref)
        for group in range(GROUPS):
            mine = slice(group * GROUP_ROWS, (group + 1) * GROUP_ROWS)
            dmix_ref[group, 0] = dot_nt(output[mine, :], out_low).astype(BF16)
            dwo_ref[mine, :] += dot(mix_ref[group, 0], out_low)

    @pl.when(step == (PARTS + 1) * blocks - 1)
    def _():
        for first in range(0, width, 256):
            stage(0, first, dwo_ref[:, first : first + 256].astype(BF16))
        keep(PARTS, 0).start()
        keep(PARTS, 0).wait()


def feed(n2, bg, mid, flags, instr, pg, gains, og, mix, early, late, fast):
    tokens, width = n2.shape
    seqs = tokens // LENGTH
    rows = pl.BlockSpec((LENGTH, width), lambda c, m: (jnp.where(c == PARTS, m, 0), 0))
    heads = pl.BlockSpec((GROUPS, 1, GROUP_ROWS, LENGTH), lambda c, m: (0, jnp.where(c == PARTS, m, 0), 0, 0))
    piece = (DEPTH, WIDE, CORES, SHARE, width)
    sums = FEED_SUMS
    out_specs = [rows, whole((seqs, 2, width)), rows, heads, ANY]
    out_shape = [
        jax.ShapeDtypeStruct((tokens, width), BF16), jax.ShapeDtypeStruct((seqs, 2, width), F32),
        jax.ShapeDtypeStruct((tokens, width), F32), jax.ShapeDtypeStruct((GROUPS, seqs, GROUP_ROWS, LENGTH), BF16),
        jax.ShapeDtypeStruct((2 * PARTS + 1, *piece), BF16),
    ]
    scratch = [
        pltpu.VMEM((tokens, width), F32), pltpu.VMEM((tokens, width), F32), pltpu.VMEM((tokens, width), BF16),
        pltpu.VMEM((tokens, width), BF16), pltpu.VMEM((2, *piece), BF16), pltpu.VMEM((2, *piece), BF16),
        pltpu.VMEM(piece, BF16), pltpu.VMEM((width, width), F32), pltpu.VMEM((2, *piece), BF16), pltpu.SemaphoreType.DMA((2, 4)),
    ]
    if fast:
        out_specs += [whole((sums, SHARE, width)), ANY]
        out_shape += [
            jax.ShapeDtypeStruct((sums, SHARE, width), F32), jax.ShapeDtypeStruct((FEED_PIECES, *piece), BF16)
        ]
        scratch += gather_sems(FEED_PIECES) + scatter_scratch(sums, SHARE, width)
    return pl.pallas_call(
        partial(feed_kernel, fast=fast),
        name="feed",
        grid=(PARTS + 1, seqs),
        in_specs=[
            whole((tokens, width)), whole((tokens, width)), ANY, whole((seqs, 1, LENGTH)), whole((seqs, 1, LENGTH)),
            whole((seqs, 2, width)), whole((8, width)), rows, rows, heads, ANY, ANY,
        ],
        out_specs=out_specs,
        out_shape=out_shape,
        scratch_shapes=scratch,
        compiler_params=pltpu.CompilerParams(
            vmem_limit_bytes=VMEM_LIMIT, collective_id=2 if fast else None, has_side_effects=fast
        ),
    )(n2, bg, mid, flags, instr, pg, gains, og, mid, mix, early, late)


def back_kernel(
    x_ref, gm_ref, gains_ref, wg_ref, qkv_ref, p_ref, inv_ref, mix_ref, dmix_ref, early_hbm,
    ig_ref, parts_hbm, small_ref, *rest, fast,
):
    if fast:
        sums_ref, tail_ref = rest[0:2]
        rest = rest[2:]
    band_ref, flipped_ref, grads_ref, normal_ref, diag_ref, staged_ref, ds_ref, sem = rest[:8]
    group, seq = pl.program_id(0), pl.program_id(1)
    seqs = pl.num_programs(1)
    step = group * seqs + seq
    width = x_ref.shape[1]
    if fast:
        extra = len(scatter_scratch(1, SHARE, width))
        scratch, tail_scratch = rest[8 : 8 + extra], rest[8 + extra :]
        here = place()

        def main(phase, piece):
            if phase > 0:
                scatter_phase(phase, piece, here, early_hbm.at[0], sums_ref, *scratch)
                return

            @pl.when(piece < BACK_BEFORE)
            def _():
                scatter_phase(phase, piece, here, early_hbm.at[FEED_SUMS + piece], sums_ref, *scratch)

            @pl.when(piece >= BACK_BEFORE)
            def _():
                scatter_phase(phase, piece, here, parts_hbm.at[piece - BACK_BEFORE], sums_ref, *scratch)

        def tail(phase, piece):
            if phase > 0:
                scatter_phase(phase, piece, here, small_ref, tail_ref, *tail_scratch)
                return
            for which in range(3):

                @pl.when(piece == which)
                def _(which=which):
                    lanes = slice(which * SMALL, (which + 1) * SMALL)
                    scatter_phase(phase, which, here, staged_ref.at[:, :, :, :, lanes], tail_ref, *tail_scratch)

            @pl.when(piece == 3)
            def _():
                scatter_phase(phase, 3, here, small_ref, tail_ref, *tail_scratch)

        def travel(slot):
            run_slot(slot, BACK_SCATTER, main)
            run_slot(slot, TAIL_SCATTER, tail)

        def point(at):
            ends = 2 * GROUPS * seqs
            travel(jnp.where(group < GROUPS, 2 * step + at, ends + seq + at * 10000))
    else:
        point = lambda at: None
    keep = lambda: pltpu.make_async_copy(staged_ref, parts_hbm.at[group], sem)
    lanes = pl.ds(pl.multiple_of(seq * LENGTH, LENGTH), LENGTH)

    def hidden_terms():
        hidden = x_ref[...].astype(F32)
        scale = lax.rsqrt(jnp.mean(hidden * hidden, axis=1, keepdims=True) + EPS)
        return hidden, scale

    if fast:

        @pl.when(step == 0)
        def _():
            greet(here)

    @pl.when(group == 0)
    def _():
        hidden, scale = hidden_terms()
        flipped_ref[:, lanes] = (hidden * scale * gains_ref[0:1, :]).astype(BF16).T
        normal_ref[seq] = jnp.zeros((width, LENGTH), F32)

    @pl.when((seq == 0) & (group < GROUPS))
    def _():
        band_ref[...] = jnp.zeros_like(band_ref)

    def one_head(head):
        at = head * HEAD_DIM
        rows = lambda which: qkv_ref[0, 0, which * GROUP_ROWS + at : which * GROUP_ROWS + at + HEAD_DIM, :]
        grads = dmix_ref[0, 0, at : at + HEAD_DIM, :].astype(F32) * inv_ref[0, 0, head]
        grads = grads.astype(BF16)
        delta = jnp.sum(grads.astype(F32) * mix_ref[0, 0, at : at + HEAD_DIM, :].astype(F32), axis=0, keepdims=True)
        grad_prob = dot_tn(rows(2), grads)
        for column in range(BLOCKS):
            mine = span(column, column + 1)
            for row in range(BLOCKS):
                seen = span(row, row + 1)
                value = p_ref[0, 0, head, seen, mine].astype(F32) * (grad_prob[seen, mine] - delta[:, mine])
                band_ref[head, span(row - column + BLOCKS - 1, row - column + BLOCKS), :] += value
                ds_ref[head % 2, seen, mine] = value.astype(BF16)
        scores = ds_ref[head % 2]
        grads_ref[at : at + HEAD_DIM, lanes] = dot(rows(1), scores).astype(BF16)
        grads_ref[GROUP_ROWS + at : GROUP_ROWS + at + HEAD_DIM, lanes] = dot_nt(rows(0), scores).astype(BF16)
        grads_ref[2 * GROUP_ROWS + at : 2 * GROUP_ROWS + at + HEAD_DIM, lanes] = dot_nt(grads, p_ref[0, 0, head]).astype(BF16)

    point(0)

    @pl.when(group < GROUPS)
    def _():
        one_head(0)
        one_head(1)

    point(1)

    @pl.when(group < GROUPS)
    def _():
        one_head(2)
        one_head(3)
        normal_ref[seq] += dot(wg_ref[...].reshape(width, width), grads_ref[:, lanes])

    @pl.when((seq == seqs - 1) & (group < GROUPS))
    def _():
        for first in range(0, width, 256):
            value = dot_nt(flipped_ref[...], grads_ref[first : first + 256, :]).astype(BF16)
            for owner in range(OWNERS):
                z, x, core = owner // 4, owner // 2 % 2, owner % 2
                staged_ref[z, x, core, :, first : first + 256] = value[SHARE * owner : SHARE * (owner + 1), :]
        keep().start()
        for head in range(GROUP):
            turned = band_ref[head].T
            total = jnp.zeros((8, OFFSETS), F32)
            for some in range(BLOCK // 8):
                wide = jnp.concatenate([turned[8 * some : 8 * some + 8, :], jnp.zeros((8, BLOCK), F32)], axis=1)
                total = total + pltpu.roll(wide, BLOCK - 8 * some, 1)
            line = iota((8, OFFSETS), 0)
            moved = total
            for row in range(1, 8):
                moved = jnp.where(line == row, pltpu.roll(total, OFFSETS - row, 1), moved)
            diag_ref[pl.ds(group * GROUP + head, 1)] = jnp.sum(moved, axis=0, keepdims=True)[None]
        keep().wait()

    @pl.when((seq == seqs - 1) & (group == GROUPS - 1))
    def _():
        heads, buckets = table_places()
        onehot = (bucket_of(iota((OFFSETS, 1), 0) - BLOCKS * BLOCK) == buckets).astype(F32).astype(BF16)
        row = iota((16, width), 0)
        sums = jnp.concatenate([diag_ref[head] for head in range(HEADS)] + [jnp.zeros((16 - HEADS, OFFSETS), F32)], axis=0)
        high = sums.astype(BF16)
        low = (sums - high.astype(F32)).astype(BF16)
        entries = dot(high, onehot) + dot(low, onehot)
        entries = jnp.sum(jnp.where((row == heads) & (buckets >= 0), entries, 0.0), axis=0, keepdims=True)
        column = jnp.broadcast_to(entries, (BLOCK, width)).T.astype(BF16)
        for owner in range(OWNERS):
            z, x, core = owner // 4, owner // 2 % 2, owner % 2
            mine = column[SHARE * owner : SHARE * (owner + 1), :]
            small_ref[z, x, core, :, 0:BLOCK] = mine
            small_ref[z, x, core, :, BLOCK:SMALL] = mine

    @pl.when(group == GROUPS)
    def _():
        hidden, scale = hidden_terms()
        cotangent = normal_ref[seq].T
        scaled = cotangent * gains_ref[0:1, :]
        unit = hidden * scale
        inner = jnp.mean(scaled * unit, axis=1, keepdims=True)
        ig_ref[...] = (gm_ref[...] + scale * (scaled - unit * inner)).astype(BF16)

    if fast:

        @pl.when(step == (GROUPS + 1) * seqs - 1)
        def _():
            run_rest((2 * GROUPS + 1) * (flipped_ref.shape[1] // LENGTH), [BACK_SCATTER, TAIL_SCATTER], travel)


def back(x, gm, gains, weights, qkv, p, inv, mix, dmix, early, fast):
    tokens, width = x.shape
    seqs = tokens // LENGTH
    piece = (DEPTH, WIDE, CORES, SHARE, width)
    last = GROUPS - 1
    group_at = lambda g: jnp.minimum(g, last)
    seq_at = lambda g, s: jnp.where(g <= last, s, seqs - 1)
    four = lambda rows: pl.BlockSpec((1, 1, rows, LENGTH), lambda g, s: (group_at(g), seq_at(g, s), 0, 0))
    x_rows = pl.BlockSpec((LENGTH, width), lambda g, s: (jnp.where((g == 0) | (g == GROUPS), s, 0), 0))
    end_rows = pl.BlockSpec((LENGTH, width), lambda g, s: (jnp.where(g == GROUPS, s, 0), 0))
    out_specs = [end_rows, ANY, whole((DEPTH, WIDE, CORES, SHARE, SMALL))]
    out_shape = [
        jax.ShapeDtypeStruct((tokens, width), BF16), jax.ShapeDtypeStruct((GROUPS, *piece), BF16),
        jax.ShapeDtypeStruct((DEPTH, WIDE, CORES, SHARE, SMALL), BF16),
    ]
    scratch = [
        pltpu.VMEM((GROUP, BAND, BLOCK), F32), pltpu.VMEM((width, tokens), BF16), pltpu.VMEM((width, tokens), BF16),
        pltpu.VMEM((seqs, width, LENGTH), F32), pltpu.VMEM((HEADS, 1, OFFSETS), F32), pltpu.VMEM(piece, BF16),
        pltpu.VMEM((2, LENGTH, LENGTH), BF16), pltpu.SemaphoreType.DMA,
    ]
    kernel = partial(back_kernel, fast=fast)
    if fast:
        sums = BACK_SUMS
        out_specs += [whole((sums, SHARE, width)), whole((TAIL_SUMS, SHARE, SMALL))]
        out_shape += [jax.ShapeDtypeStruct((sums, SHARE, width), F32), jax.ShapeDtypeStruct((TAIL_SUMS, SHARE, SMALL), F32)]
        scratch += scatter_scratch(sums, SHARE, width) + scatter_scratch(TAIL_SUMS, SHARE, SMALL)
    return pl.pallas_call(
        kernel,
        name="back",
        grid=(GROUPS + 1, seqs),
        in_specs=[
            x_rows, end_rows, whole((8, width)),
            pl.BlockSpec((1, *piece), lambda g, s: (group_at(g), 0, 0, 0, 0, 0)), four(width),
            pl.BlockSpec((1, 1, GROUP, LENGTH, LENGTH), lambda g, s: (group_at(g), seq_at(g, s), 0, 0, 0)),
            pl.BlockSpec((1, 1, GROUP, 1, LENGTH), lambda g, s: (group_at(g), seq_at(g, s), 0, 0, 0)),
            four(GROUP_ROWS), four(GROUP_ROWS), ANY,
        ],
        out_specs=out_specs,
        out_shape=out_shape,
        scratch_shapes=scratch,
        compiler_params=pltpu.CompilerParams(
            vmem_limit_bytes=VMEM_LIMIT, collective_id=3 if fast else None, has_side_effects=fast
        ),
    )(x, gm, gains, weights, qkv, p, inv, mix, dmix, early)


def ordered(rows, w_query, w_key, w_value, w_output, w_in, w_out):
    width = w_query.shape[1]
    groups = [
        jnp.concatenate([one[:, at * GROUP_ROWS : (at + 1) * GROUP_ROWS] for one in (w_query, w_key, w_value)], axis=1)
        for at in range(GROUPS)
    ]
    inner = w_in.reshape(rows, OWNERS, PARTS, SHARE).transpose(2, 0, 1, 3).reshape(PARTS, rows, width)
    outer = w_out.reshape(-1, PARTS, SHARE, width).transpose(1, 0, 2, 3).reshape(PARTS, rows, width)
    parts = [one for at in range(PARTS) for one in (inner[at], outer[at])]
    return jnp.stack(groups + [w_output] + parts)


def small_of(rows, gain_attn, gain_ffn, rel_table):
    entries = jnp.pad(rel_table.reshape(-1, TABLE_SHARE), ((0, 0), (0, SHARE - TABLE_SHARE))).reshape(rows)
    return jnp.pad(jnp.stack([gain_attn, gain_ffn, entries], axis=1), ((0, 0), (0, SMALL - 3)))


def shards(
    hidden_in, out_grad, pooled_gradient, gain_attn, w_query, w_key, w_value, w_output, rel_table, gain_ffn, w_in, w_out,
    pair_flags, instruction_mask, *, fast,
):
    width = hidden_in.shape[1]
    own = (w_query, w_key, w_value, w_output, w_in, w_out)
    if fast:
        shares = ordered(w_query.shape[0], *own)
        small = small_of(w_query.shape[0], gain_attn, gain_ffn, rel_table)[None]
    else:
        gather = lambda one: lax.all_gather(one, "fsdp", axis=0, tiled=True)
        shares = ordered(width, *map(gather, own)).reshape(-1, DEPTH, WIDE, CORES, SHARE, width)
        small = small_of(width, *map(gather, (gain_attn, gain_ffn, rel_table))).reshape(1, DEPTH, WIDE, CORES, SHARE, SMALL)
    flags = pair_flags.reshape(-1, 1, LENGTH)
    instr = instruction_mask.reshape(-1, 1, LENGTH)
    qkv, p, inv, mix, mid, n2, bg, gains, *rest = attend(
        hidden_in, out_grad, pooled_gradient, flags, instr, shares, small, fast
    )
    early = rest[0] if fast else shares
    output, pooled, gm, dmix, parts, *rest = feed(
        n2, bg, mid, flags, instr, pooled_gradient, gains, out_grad, mix, early, shares, fast
    )
    early_sums = rest[0] if fast else None
    input_grad, group_parts, small_parts, *rest = back(hidden_in, gm, gains, early, qkv, p, inv, mix, dmix, parts, fast)
    if fast:
        last = rest[1][:GROUPS].transpose(1, 0, 2).reshape(1, SHARE, width)
        sums = jnp.concatenate([early_sums, rest[0], last])
        table = rest[1][GROUPS, :TABLE_SHARE, 0]
        rows = SHARE
    else:
        sums = jnp.concatenate([parts, group_parts]).reshape(-1, width, width)
        table = small_parts.reshape(OWNERS, SHARE, SMALL)[:, :TABLE_SHARE, 0].reshape(-1)
        rows = width
    groups = [sums[2 * PARTS + 1 + at] for at in range(GROUPS)]
    grad_query, grad_key, grad_value = (
        jnp.concatenate([one[:, at * GROUP_ROWS : (at + 1) * GROUP_ROWS] for one in groups], axis=1) for at in range(3)
    )
    grad_output = sums[2 * PARTS]
    grad_in = sums[0 : 2 * PARTS : 2].reshape(PARTS, rows, OWNERS, SHARE).transpose(1, 2, 0, 3).reshape(rows, -1)
    grad_out = sums[1 : 2 * PARTS : 2].reshape(PARTS, -1, SHARE, width).transpose(1, 0, 2, 3).reshape(-1, width)
    if not fast:
        scatter = lambda one: lax.psum(lax.psum_scatter(one, "fsdp", scatter_dimension=0, tiled=True), "grp").astype(F32)
        grad_query, grad_key, grad_value, grad_output, grad_in, grad_out, table = map(
            scatter, (grad_query, grad_key, grad_value, grad_output, grad_in, grad_out, table)
        )
    weigh = lambda weight, grad: jnp.sum(weight.astype(F32) * grad, axis=1)
    grad_gain = weigh(w_query, grad_query) + weigh(w_key, grad_key) + weigh(w_value, grad_value)
    return (
        output, pooled, input_grad, grad_gain / gain_attn.astype(F32),
        grad_query, grad_key, grad_value, grad_output, table.astype(F32),
        weigh(w_in, grad_in) / gain_ffn.astype(F32), grad_in, grad_out,
    )


def solution(mesh):
    tokens, square, line = P(("grp", "fsdp"), None), P("fsdp", None), P("fsdp")
    cube, flat = P(("grp", "fsdp"), None, None), P(("grp", "fsdp"))
    fast = mesh.shape["fsdp"] == OWNERS and mesh.shape["grp"] == 2
    return jax.shard_map(
        partial(shards, fast=fast),
        mesh=mesh,
        in_specs=(tokens, tokens, cube, line, square, square, square, square, line, line, square, square, flat, flat),
        out_specs=(tokens, cube, tokens, line, square, square, square, square, line, line, square, square),
        check_vma=False,
    )
```

```python
from functools import partial

import jax
import jax.numpy as jnp
from jax import lax
from jax.experimental import pallas as pl
from jax.experimental.pallas import tpu as pltpu
from jax.sharding import PartitionSpec as P

HEADS = 12
HEAD_DIM = 64
BUCKETS = 32
LENGTH = 512
BLOCK = 128
BLOCKS = LENGTH // BLOCK
BAND_BLOCKS = 2 * BLOCKS - 1
BAND = BAND_BLOCKS * BLOCK
OFFSETS = BAND + BLOCK
GROUPS = 3
GROUP = HEADS // GROUPS
GROUP_ROWS = GROUP * HEAD_DIM
OWNERS, PARTS, SHARE = 16, 4, 48
TABLE_SHARE = HEADS * BUCKETS // OWNERS
SMALL = 256
EPS = 1e-06
NEG = -1e30
LIMITS = (12, 16, 23, 32, 46, 64, 91)
ROOT = 0.7978845608028654
CUBE = 0.044715
F32 = jnp.float32
BF16 = jnp.bfloat16
ANY = pl.BlockSpec(memory_space=pl.ANY)
VMEM_LIMIT = 63 * 1024 * 1024


def bucket_of(offset):
    distance = jnp.abs(offset)
    far_bucket = jnp.full(offset.shape, 8, jnp.int32)
    for threshold in LIMITS:
        far_bucket = far_bucket + (distance >= threshold).astype(jnp.int32)
    near_bucket = jnp.where(distance < 8, distance, far_bucket)
    return near_bucket + BUCKETS // 2 * (offset > 0).astype(jnp.int32)


def dot(a, b):
    return lax.dot_general(a, b, (((1,), (0,)), ((), ())), preferred_element_type=F32)


def dot_nt(a, b):
    return lax.dot_general(a, b, (((1,), (1,)), ((), ())), preferred_element_type=F32)


def dot_tn(a, b):
    return lax.dot_general(a, b, (((0,), (0,)), ((), ())), preferred_element_type=F32)


def dot_tt(a, b):
    return lax.dot_general(a, b, (((0,), (1,)), ((), ())), preferred_element_type=F32)


def iota(shape, axis):
    return lax.broadcasted_iota(jnp.int32, shape, axis)


def whole(shape):
    zeros = (0,) * len(shape)
    return pl.BlockSpec(shape, lambda *_: zeros, pipeline_mode=pl.Buffered(1))


def span(first, last):
    return slice(first * BLOCK, last * BLOCK)


def pool_terms(flags, instruction):
    kept = (instruction == 0).astype(F32)
    chosen = [kept * (flags == part).astype(F32) for part in range(2)]
    counts = [jnp.sum(one, axis=1, keepdims=True) for one in chosen]
    return chosen, counts


def pool_gradient(chosen, counts, pooled_grad):
    row = iota((16, LENGTH), 0)
    picks = jnp.where(row % 2 == 0, chosen[0], chosen[1])
    picks = jnp.where(row < 6, picks, 0.0).astype(BF16)
    scaled = [pooled_grad[part : part + 1, :] / counts[part] for part in range(2)]
    line = iota((16, pooled_grad.shape[1]), 0)
    both = jnp.where(line % 2 == 0, scaled[0], scaled[1])
    high = both.astype(BF16).astype(F32)
    rest = both - high
    middle = rest.astype(BF16).astype(F32)
    low = rest - middle
    parts = jnp.where(line < 2, high, jnp.where(line < 4, middle, jnp.where(line < 6, low, 0.0)))
    return dot_tn(picks, parts.astype(BF16))


def norm_back(value, gain, cotangent):
    scale = lax.rsqrt(jnp.mean(value * value, axis=1, keepdims=True) + EPS)
    scaled = cotangent * gain
    unit = value * scale
    inner = jnp.mean(scaled * unit, axis=1, keepdims=True)
    return scale * (scaled - unit * inner), jnp.sum(cotangent * unit, axis=0, keepdims=True)


def owners_of():
    at = iota((1, OWNERS * SHARE), 1)
    owner = sum((at >= SHARE * one).astype(jnp.int32) for one in range(1, OWNERS))
    return owner, at - SHARE * owner


def table_places():
    owner, inside = owners_of()
    entry = owner * TABLE_SHARE + inside
    bucket = sum((entry >= HEADS * one).astype(jnp.int32) for one in range(1, BUCKETS))
    return entry - HEADS * bucket, jnp.where(inside < TABLE_SHARE, bucket, -1)


DEPTH, WIDE, CORES = 4, 2, 2
MESH_ID = pl.DeviceIdType.MESH


def place():
    grp, at = lax.axis_index("grp"), lax.axis_index("fsdp")
    z, x, core = lax.div(at, WIDE * CORES), lax.rem(lax.div(at, CORES), WIDE), lax.rem(at, CORES)

    def device(grp, z, x, core):
        return (grp, z * (WIDE * CORES) + x * CORES + core)

    return dict(
        at=at, y=grp, z=z, x=x, core=core,
        over_y=device(1 - grp, z, x, core),
        over_x=device(grp, z, 1 - x, core),
        over_core=device(grp, z, x, 1 - core),
        over_z=[device(grp, lax.rem(z + one, DEPTH), x, core) for one in range(1, DEPTH)],
        ahead=[lax.rem(z + one, DEPTH) for one in range(1, DEPTH)],
        behind=[lax.rem(z + DEPTH - one, DEPTH) for one in range(1, DEPTH)],
    )


def greet(here):
    barrier = pltpu.get_barrier_semaphore()
    for device in (here["over_y"], here["over_x"], here["over_core"], *here["over_z"]):
        pl.semaphore_signal(barrier, inc=1, device_id=device, device_id_type=MESH_ID)
    pl.semaphore_wait(barrier, DEPTH + 2)


def others(here):
    at = here["at"]
    for one in range(1, OWNERS):
        yield one, (here["y"], lax.rem(at + one, OWNERS)), lax.rem(at + OWNERS - one, OWNERS)


def greet_all(here):
    barrier = pltpu.get_barrier_semaphore()
    pl.semaphore_signal(barrier, inc=1, device_id=here["over_y"], device_id_type=MESH_ID)
    for _, device, _ in others(here):
        pl.semaphore_signal(barrier, inc=1, device_id=device, device_id_type=MESH_ID)
    pl.semaphore_wait(barrier, OWNERS)


def gather_phase(phase, sem, here, share_ref, whole_ref, sent, got, own_sem, shared=False):
    z, x, core = here["z"], here["x"], here["core"]
    every = slice(None)
    half = share_ref.shape[-1] // 2
    lanes = pl.ds(pl.multiple_of(here["y"] * half, half), half) if shared else every
    other = pl.ds(pl.multiple_of((1 - here["y"]) * half, half), half) if shared else every
    mine = share_ref.at[:, lanes] if shared else share_ref

    def copy(source, where, channel, device):
        return pltpu.make_async_remote_copy(
            src_ref=source, dst_ref=whole_ref.at[where], send_sem=sent.at[channel, sem], recv_sem=got.at[channel, sem],
            device_id=device, device_id_type=MESH_ID,
        )

    def same(where, channel, device):
        return copy(whole_ref.at[where], where, channel, device)

    own = lambda: pltpu.make_async_copy(mine, whole_ref.at[z, x, core, every, lanes], own_sem.at[sem])
    line_out = lambda one: copy(mine, (z, x, core, every, lanes), one, here["over_z"][one])
    line_in = lambda one: copy(mine, (here["behind"][one], x, core, every, lanes), one, here["over_z"][one])
    side_out = lambda: same((every, x, core, every, lanes), 3, here["over_x"])
    side_in = lambda: same((every, 1 - x, core, every, lanes), 3, here["over_x"])
    group_out = lambda: same((every, every, core, every, lanes), 5, here["over_y"])
    group_in = lambda: same((every, every, core, every, other), 5, here["over_y"])
    core_out = lambda: same((every, every, core), 4, here["over_core"])
    core_in = lambda: same((every, every, 1 - core), 4, here["over_core"])
    if phase == 0:
        own().start()
        for one in range(DEPTH - 1):
            line_out(one).start()
    elif phase == 1:
        own().wait()
        for one in range(DEPTH - 1):
            line_in(one).wait_recv()
        side_out().start()
    elif phase == 2:
        side_in().wait_recv()
        group_out().start()
    elif phase == 3:
        if shared:
            group_in().wait_recv()
        else:
            side_in().wait_recv()
        core_out().start()
    else:
        for one in range(DEPTH - 1):
            line_out(one).wait_send()
        side_out().wait_send()
        if shared:
            group_out().wait_send()
        core_out().wait_send()
        core_in().wait_recv()


def scatter_phase(phase, piece, here, part_ref, out_ref, own, fromc, fromx, fromz, last, sent, got, own_sem):
    z, x, core = here["z"], here["x"], here["core"]
    slot = lax.rem(piece, own.shape[0])

    def remote(source, target, channel, device):
        return pltpu.make_async_remote_copy(
            src_ref=source, dst_ref=target, send_sem=sent.at[channel, piece], recv_sem=got.at[channel, piece],
            device_id=device, device_id_type=MESH_ID,
        )

    total = fromc.at[piece]
    over_core = lambda: remote(part_ref.at[:, :, 1 - core], total, 0, here["over_core"])
    load = lambda: pltpu.make_async_copy(part_ref.at[:, :, core], own.at[slot], own_sem.at[slot])
    over_x = lambda: remote(fromc.at[piece, :, 1 - x], fromx.at[piece], 1, here["over_x"])
    line_out = lambda one: remote(fromc.at[piece, here["ahead"][one], x], fromz.at[piece, z], 2 + one, here["over_z"][one])
    line_in = lambda one: remote(
        fromc.at[piece, z, x], fromz.at[piece, here["behind"][one]], 2 + one, here["over_z"][one]
    )
    final = lambda: remote(fromc.at[piece, z, x], last.at[piece], 5, here["over_y"])

    if phase == 0:
        over_core().start()
        load().start()
    elif phase == 1:
        load().wait()
        over_core().wait()

        def one(at, _):
            for side in range(WIDE):
                fromc[piece, at, side] = own[slot, at, side] + fromc[piece, at, side]
            return 0

        lax.fori_loop(0, DEPTH, one, 0)
        over_x().start()
    elif phase == 2:
        over_x().wait()

        def one(at, _):
            fromc[piece, at, x] = fromc[piece, at, x] + fromx[piece, at]
            return 0

        lax.fori_loop(0, DEPTH, one, 0)
        for one in range(DEPTH - 1):
            line_out(one).start()
    elif phase == 3:
        mine = fromc[piece, z, x].astype(F32)
        for one in range(DEPTH - 1):
            line_in(one).wait_recv()
            mine = mine + fromz[piece, here["behind"][one]].astype(F32)
        fromc[piece, z, x] = mine.astype(BF16)
        final().start()
    else:
        for one in range(DEPTH - 1):
            line_out(one).wait_send()
        final().wait()
        out_ref[piece] = fromc[piece, z, x].astype(F32) + last[piece].astype(F32)


def run_slot(slot, table, act):
    for phase in reversed(range(max(map(len, table.values())))):
        due, found = False, 0
        for piece, slots in table.items():
            if slots[phase] is not None:
                now = slot == slots[phase]
                due, found = due | now, jnp.where(now, piece, found)
        if due is not False:

            @pl.when(due)
            def _(phase=phase, found=found):
                act(phase, found)


def run_rest(first, tables, travel):
    end = 1 + max(slot for table in tables for slots in table.values() for slot in slots if slot is not None)

    def one(slot, _):
        travel(slot)
        return 0

    if end > first:
        lax.fori_loop(first, end, one, 0)


def gather_sems(pieces):
    return [pltpu.SemaphoreType.DMA((6, pieces)), pltpu.SemaphoreType.DMA((6, pieces)), pltpu.SemaphoreType.DMA((pieces,))]


def scatter_scratch(pieces, rows, columns, places=2):
    return [
        pltpu.VMEM((places, DEPTH, WIDE, rows, columns), BF16),
        pltpu.VMEM((pieces, DEPTH, WIDE, rows, columns), BF16),
        pltpu.VMEM((pieces, DEPTH, rows, columns), BF16),
        pltpu.VMEM((pieces, DEPTH, rows, columns), BF16),
        pltpu.VMEM((pieces, rows, columns), BF16),
        pltpu.SemaphoreType.DMA((6, pieces)),
        pltpu.SemaphoreType.DMA((6, pieces)),
        pltpu.SemaphoreType.DMA((places,)),
    ]


ATTEND_PIECES, FEED_PIECES = 8, 4
ATTEND_DIRECT = {1: (None, 0, None, 3, 5), 3: (2, 7, None, 12, 14), 6: (8, 13, None, 18, 20)}
ATTEND_SHARED = {2: (0, 4, 7, 11, 13), 4: (4, 8, 12, 16, 18), 5: (6, 10, 15, 19, 21), 7: (11, 15, 19, 23, 25)}
FEED_GATHER = {0: (0, 5, None, 10, 12), 1: (3, 8, None, 13, 15), 2: (6, 11, None, 16, 18), 3: (9, 14, None, 19, 21)}
FEED_SUMS = 5
FEED_SCATTER = {
    0: (8, 10, 15, 20, 23), 1: (11, 13, 18, 23, 26), 2: (16, 18, 23, 28, 31), 3: (19, 21, 26, 31, 34), 4: (24, 26, 31, 36, 39),
}
BACK_BEFORE, BACK_SUMS = 4, 6
BACK_SCATTER = {
    0: (0, 2, 7, 12, 15), 1: (3, 5, 10, 15, 18), 2: (6, 8, 13, 18, 21), 3: (9, 11, 16, 21, 24),
    4: (12, 14, 19, 24, 27), 5: (16, 18, 23, 27, 29),
}
TAIL_SUMS = 4
TAIL_SCATTER = {0: (None, 24, 26, 28, 30), 1: (None, 25, 27, 29, 31), 2: (None, 26, 28, 30, 32), 3: (24, 27, 29, 31, 33)}


def attend_kernel(
    x_hbm, og_hbm, pg_ref, flags_ref, instr_ref, shares_hbm, small_hbm,
    qkv_ref, p_ref, inv_ref, mix_ref, mid_ref, n2_ref, bg_hbm, gains_ref, weights_hbm,
    x_ref, bg_ref, mixed_ref, band_ref, aux_ref, normed_ref, wg_ref, wo_ref, small_ref, table_ref, cur_ref, nxt_ref, sa_ref, sb_ref,
    sems, *comm, fast,
):
    group, seq = pl.program_id(0), pl.program_id(1)
    seqs = pl.num_programs(1)
    step = group * seqs + seq
    width = x_ref.shape[1]
    if fast:
        main_sems, first_sems, small_sent, small_got = comm[0:3], comm[3:6], comm[6], comm[7]
        here = place()

        def main(phase, piece, shared=False):
            gather_phase(phase, piece, here, shares_hbm.at[piece], weights_hbm.at[piece], *main_sems, shared=shared)

        def small(start):
            for one, device, source in others(here):
                copy = lambda where: pltpu.make_async_remote_copy(
                    src_ref=small_hbm, dst_ref=small_ref.at[where], send_sem=small_sent.at[one], recv_sem=small_got.at[one],
                    device_id=device, device_id_type=MESH_ID,
                )
                if start:
                    copy(here["at"]).start()
                else:
                    copy(source).wait_recv()
                    copy(here["at"]).wait_send()

        def first(phase, which):
            lanes = pl.ds(which * GROUP_ROWS, GROUP_ROWS)
            every = slice(None)
            gather_phase(
                phase, which, here, shares_hbm.at[0, :, lanes], weights_hbm.at[0, every, every, every, every, lanes], *first_sems
            )

        def travel(slot):
            run_slot(slot, ATTEND_DIRECT, main)
            run_slot(slot, ATTEND_SHARED, partial(main, shared=True))

        point = lambda at: travel(2 * step + at)
    else:
        point = lambda at: None
    small_own = small_ref.at[here["at"]] if fast else small_ref
    load_small = lambda: pltpu.make_async_copy(small_hbm, small_own, sems.at[0])
    load_hidden = lambda: pltpu.make_async_copy(x_hbm, x_ref, sems.at[3])
    load_grad = lambda: pltpu.make_async_copy(og_hbm, bg_ref, sems.at[4])
    keep_grad = lambda: pltpu.make_async_copy(bg_ref, bg_hbm, sems.at[4])
    load_group = lambda at: pltpu.make_async_copy(weights_hbm.at[at], wg_ref, sems.at[1])
    load_output = lambda: pltpu.make_async_copy(weights_hbm.at[GROUPS], wo_ref, sems.at[2])
    square = lambda ref: ref[...].reshape(width, width)

    def prepare(at):
        flags = flags_ref[at]
        chosen, counts = pool_terms(flags, instr_ref[at])
        rows = pl.ds(pl.multiple_of(at * LENGTH, LENGTH), LENGTH)
        bg_ref[rows, :] = (bg_ref[rows, :].astype(F32) + pool_gradient(chosen, counts, pg_ref[at])).astype(BF16)
        row = iota((16, LENGTH), 0)
        aux_ref[0, at] = jnp.where(row == 0, 1 - flags, jnp.where(row == 1, flags, 0)).astype(F32).astype(BF16)
        other = jnp.where(row == 0, flags, jnp.where(row == 1, 1 - flags, 0)).astype(F32) * NEG
        aux_ref[1, at] = other.astype(BF16)

    def normalize(at):
        rows = pl.ds(pl.multiple_of(at * LENGTH, LENGTH), LENGTH)
        hidden = x_ref[rows, :].astype(F32)
        scale = lax.rsqrt(jnp.mean(hidden * hidden, axis=1, keepdims=True) + EPS)
        normed_ref[at] = (hidden * scale * gains_ref[0:1, :]).astype(BF16)

    def every_seq(act):
        def one_seq(at, _):
            act(at)
            return 0

        lax.fori_loop(0, seqs, one_seq, 0)

    def project(at, target):
        target[...] = dot_tt(square(wg_ref), normed_ref[at]).astype(BF16)

    def part(source, which, head):
        first = which * GROUP_ROWS + head * HEAD_DIM
        return source[first : first + HEAD_DIM, :]

    def score(source, at_group, at, head, target):
        queries = jnp.concatenate([part(source, 0, head), aux_ref[0, at]], axis=0)
        keys = jnp.concatenate([part(source, 1, head), aux_ref[1, at]], axis=0)
        scores = dot_tn(keys, queries)
        for row in range(BLOCKS):
            for column in range(BLOCKS):
                bias = band_ref[at_group * GROUP + head, span(row - column + BLOCKS - 1, row - column + BLOCKS), :]
                target[span(row, row + 1), span(column, column + 1)] = scores[span(row, row + 1), span(column, column + 1)] + bias

    def soften(head, source):
        scores = source[...]
        exponent = jnp.exp(scores - jnp.max(scores, axis=0, keepdims=True)).astype(BF16)
        p_ref[0, 0, head] = exponent
        values = jnp.concatenate([part(cur_ref, 2, head), jnp.ones((16, LENGTH), BF16)], axis=0)
        mixed = dot(values, exponent)
        inverse = 1.0 / mixed[HEAD_DIM : HEAD_DIM + 1, :]
        inv_ref[0, 0, head] = inverse
        mixed = (mixed[0:HEAD_DIM, :] * inverse).astype(BF16)
        mix_ref[0, 0, head * HEAD_DIM : (head + 1) * HEAD_DIM, :] = mixed
        mixed_ref[seq, pl.ds(pl.multiple_of(group * GROUP_ROWS + head * HEAD_DIM, HEAD_DIM), HEAD_DIM), :] = mixed

    def read_small():
        owner, inside = owners_of()
        spread = (iota((BLOCK, width), 0) == inside).astype(F32).astype(BF16)
        shares = small_ref[...].astype(F32)

        def line(which):
            placed = dot(shares[:, which, :].astype(BF16), spread)
            return jnp.sum(jnp.where(iota((OWNERS, width), 0) == owner, placed, 0.0), axis=0, keepdims=True)

        row = iota((8, width), 0)
        gains_ref[...] = jnp.where(row == 0, line(0), line(1))
        table_row = line(2)
        heads, buckets = table_places()
        entries = jnp.where((iota((16, width), 0) == heads) & (buckets >= 0), table_row, 0.0).astype(BF16)
        onehot = (bucket_of(iota((OFFSETS, 1), 0) - BLOCKS * BLOCK) == buckets).astype(F32).astype(BF16)
        table_ref[...] = dot_nt(entries, onehot)

    def make_bands(at_group):
        def one_head(head, _):
            table = table_ref[...]
            line = jnp.sum(jnp.where(iota(table.shape, 0) == head, table, 0.0), axis=0, keepdims=True)
            turned = pltpu.roll(jnp.broadcast_to(line, (BLOCK, OFFSETS)), 0, 1, stride=1, stride_axis=0)
            band_ref[head] = turned[:, BLOCK:].T
            return 0

        lax.fori_loop(at_group * GROUP, (at_group + 1) * GROUP, one_head, 0)

    @pl.when(step == 0)
    def _():
        load_grad().start()
        load_hidden().start()
        load_small().start()
        if fast:
            greet_all(here)
            small(True)
            for which in range(3):
                first(0, which)
        load_grad().wait()
        every_seq(prepare)
        keep_grad().start()
        load_hidden().wait()
        load_small().wait()
        if fast:
            small(False)
            first(1, 0)
            read_small()
            first(1, 1)
            normalize(0)
            normalize(1)
            first(1, 2)
            main(0, 1)
            normalize(2)
            normalize(3)
            first(3, 0)
            make_bands(0)
            first(3, 1)
            make_bands(1)
            first(3, 2)
            make_bands(2)
            for which in range(3):
                first(4, which)
        else:
            read_small()
            every_seq(normalize)
            for one in range(GROUPS):
                make_bands(one)
        load_group(0).start()
        load_group(0).wait()
        project(0, nxt_ref)
        score(nxt_ref, 0, 0, 0, sa_ref)

    last_seq = seq == seqs - 1
    more = step + 1 < GROUPS * seqs
    cur_ref[...] = nxt_ref[...]
    qkv_ref[0, 0] = nxt_ref[...]

    @pl.when(last_seq & more)
    def _():
        load_group(group + 1).start()

    @pl.when((seq == 0) & (group == GROUPS - 1))
    def _():
        load_output().start()
        load_output().wait()

    next_seq = jnp.where(last_seq, 0, seq + 1)
    next_group = jnp.where(last_seq, jnp.minimum(group + 1, GROUPS - 1), group)
    point(0)
    score(cur_ref, group, seq, 1, sb_ref)
    soften(0, sa_ref)
    score(cur_ref, group, seq, 2, sa_ref)
    soften(1, sb_ref)
    point(1)
    score(cur_ref, group, seq, 3, sb_ref)
    soften(2, sa_ref)

    @pl.when(last_seq & more)
    def _():
        load_group(group + 1).wait()

    project(next_seq, nxt_ref)
    score(nxt_ref, next_group, next_seq, 0, sa_ref)
    soften(3, sb_ref)

    @pl.when(group == GROUPS - 1)
    def _():
        rows = pl.ds(pl.multiple_of(seq * LENGTH, LENGTH), LENGTH)
        middle = x_ref[rows, :].astype(F32) + dot_tn(mixed_ref[seq], square(wo_ref))
        mid_ref[...] = middle
        scale = lax.rsqrt(jnp.mean(middle * middle, axis=1, keepdims=True) + EPS)
        n2_ref[...] = (middle * scale * gains_ref[1:2, :]).astype(BF16)

    @pl.when(step == GROUPS * seqs - 1)
    def _():
        keep_grad().wait()
        if fast:
            run_rest(2 * GROUPS * (x_ref.shape[0] // LENGTH), [ATTEND_DIRECT, ATTEND_SHARED], travel)


def attend(x, og, pg, flags, instr, shares, small, fast):
    tokens, width = x.shape
    seqs = tokens // LENGTH
    last_rows = pl.BlockSpec((LENGTH, width), lambda g, s: (jnp.where(g == GROUPS - 1, s, 0), 0))
    low = jax.ShapeDtypeStruct((tokens, width), BF16)
    out_specs = [
        pl.BlockSpec((1, 1, width, LENGTH), lambda g, s: (g, s, 0, 0)),
        pl.BlockSpec((1, 1, GROUP, LENGTH, LENGTH), lambda g, s: (g, s, 0, 0, 0)),
        pl.BlockSpec((1, 1, GROUP, 1, LENGTH), lambda g, s: (g, s, 0, 0, 0)),
        pl.BlockSpec((1, 1, GROUP_ROWS, LENGTH), lambda g, s: (g, s, 0, 0)), last_rows, last_rows, ANY, whole((8, width)),
    ]
    out_shape = [
        jax.ShapeDtypeStruct((GROUPS, seqs, width, LENGTH), BF16),
        jax.ShapeDtypeStruct((GROUPS, seqs, GROUP, LENGTH, LENGTH), BF16),
        jax.ShapeDtypeStruct((GROUPS, seqs, GROUP, 1, LENGTH), F32),
        jax.ShapeDtypeStruct((GROUPS, seqs, GROUP_ROWS, LENGTH), BF16),
        jax.ShapeDtypeStruct((tokens, width), F32), low, low, jax.ShapeDtypeStruct((8, width), F32),
    ]
    scratch = [
        pltpu.VMEM((tokens, width), BF16), pltpu.VMEM((tokens, width), BF16), pltpu.VMEM((seqs, width, LENGTH), BF16),
        pltpu.VMEM((HEADS, BAND, BLOCK), F32), pltpu.VMEM((2, seqs, 16, LENGTH), BF16),
        pltpu.VMEM((seqs, LENGTH, width), BF16), pltpu.VMEM((DEPTH, WIDE, CORES, SHARE, width), BF16),
        pltpu.VMEM((DEPTH, WIDE, CORES, SHARE, width), BF16), pltpu.VMEM((OWNERS, 16, BLOCK), BF16), pltpu.VMEM((16, OFFSETS), F32),
        pltpu.VMEM((width, LENGTH), BF16), pltpu.VMEM((width, LENGTH), BF16),
        pltpu.VMEM((LENGTH, LENGTH), F32), pltpu.VMEM((LENGTH, LENGTH), F32), pltpu.SemaphoreType.DMA((5,)),
    ]
    in_specs = [
        ANY, ANY, whole((seqs, 2, width)), whole((seqs, 1, LENGTH)), whole((seqs, 1, LENGTH)), ANY, ANY,
    ]
    if fast:
        kernel = partial(attend_kernel, fast=True)
        out_specs += [ANY]
        out_shape += [jax.ShapeDtypeStruct((ATTEND_PIECES, DEPTH, WIDE, CORES, SHARE, width), BF16)]
        scratch += gather_sems(ATTEND_PIECES) + gather_sems(3) + [pltpu.SemaphoreType.DMA((OWNERS,)), pltpu.SemaphoreType.DMA((OWNERS,))]
    else:

        def kernel(*refs):
            inputs, outputs, rest = refs[:7], refs[7:15], refs[15:]
            attend_kernel(*inputs, *outputs, inputs[5], *rest, fast=False)

    return pl.pallas_call(
        kernel,
        name="attend",
        grid=(GROUPS, seqs),
        in_specs=in_specs,
        out_specs=out_specs,
        out_shape=out_shape,
        scratch_shapes=scratch,
        compiler_params=pltpu.CompilerParams(
            vmem_limit_bytes=VMEM_LIMIT, collective_id=1 if fast else None, has_side_effects=fast
        ),
    )(x, og, pg, flags, instr, shares, small)


def feed_kernel(
    n2_hbm, bg_hbm, mid_hbm, flags_ref, instr_ref, gains_ref, mid_ref, mix_ref, early_hbm, late_hbm,
    out_ref, pooled_ref, gm_ref, dmix_ref, parts_hbm, *rest, fast,
):
    if fast:
        sums_ref, gathered_hbm = rest[0:2]
        rest = rest[2:]
    n2_ref, bg_ref, res_ref, dn2_ref, act_ref, dinner_ref, win_ref, wout_ref, wo_ref, dwo_ref, staged_ref, sems, block_sems = rest[:13]
    part, block = pl.program_id(0), pl.program_id(1)
    blocks = pl.num_programs(1)
    step = part * blocks + block
    width = res_ref.shape[1]
    rows = pl.ds(pl.multiple_of(block * LENGTH, LENGTH), LENGTH)
    if fast:
        sems_of, scratch = rest[13:16], rest[16:]
        here = place()

        def travel(slot):
            def bring(phase, piece):
                share = late_hbm.at[ATTEND_PIECES + piece]
                gather_phase(phase, piece, here, share, gathered_hbm.at[piece], *sems_of)

            def add(phase, piece):
                scatter_phase(phase, piece, here, parts_hbm.at[piece], sums_ref, *scratch)

            run_slot(slot, FEED_GATHER, bring)
            run_slot(slot, FEED_SCATTER, add)

        point = lambda at: travel(2 * step + at)
    else:
        point = lambda at: None
    square = lambda ref: ref[...].reshape(width, width)

    def weights(at, start):
        def both(source, first):
            for which, target in enumerate((win_ref, wout_ref)):
                slot = lax.rem(at, 2)
                copy = pltpu.make_async_copy(source.at[first + which], target.at[slot], sems.at[slot, which])
                copy.start() if start else copy.wait()

        if start:
            pl.when(at < PARTS // 2)(lambda: both(early_hbm, 4 + 2 * at))
            pl.when(at >= PARTS // 2)(lambda: both(gathered_hbm if fast else late_hbm, 2 * at + (-PARTS if fast else 4)))
        else:
            both(early_hbm, 4)


    def load_block(at, start):
        mine = pl.ds(pl.multiple_of(at * LENGTH, LENGTH), LENGTH)
        for which, (source, target) in enumerate(((n2_hbm, n2_ref), (bg_hbm, bg_ref), (mid_hbm, res_ref))):
            copy = pltpu.make_async_copy(source.at[mine], target.at[mine], block_sems.at[which, at])
            copy.start() if start else copy.wait()

    load_output = lambda: pltpu.make_async_copy(early_hbm.at[GROUPS], wo_ref, sems.at[1, 2])
    keep = lambda at, which: pltpu.make_async_copy(staged_ref.at[which], parts_hbm.at[2 * at + which], sems.at[which, 3])

    @pl.when(step == 0)
    def _():
        weights(0, True)
        for at in range(res_ref.shape[0] // LENGTH):
            load_block(at, True)
        load_output().start()
        if fast:
            greet(here)
        dwo_ref[...] = jnp.zeros_like(dwo_ref)
        load_output().wait()

    @pl.when(part == 0)
    def _():
        dn2_ref[rows, :] = jnp.zeros((LENGTH, width), F32)
        load_block(block, False)

    @pl.when((part < PARTS) & (block == 0))
    def _():
        weights(part, False)

    @pl.when((part > 0) & (block == 0))
    def _():
        keep(part - 1, 0).wait()
        keep(part - 1, 1).wait()

    point(0)

    @pl.when(part < PARTS)
    def _():
        slot = lax.rem(part, 2)
        inner = dot(n2_ref[rows, :], square(win_ref.at[slot]))
        squared = inner * inner
        half = 0.5 * jnp.tanh(inner * (ROOT + (ROOT * CUBE) * squared)) + 0.5
        active = inner * half
        slope = half + active * (1.0 - half) * (2.0 * ROOT + (6.0 * ROOT * CUBE) * squared)
        active = active.astype(BF16)
        act_ref[rows, :] = active
        dinner = (dot_nt(bg_ref[rows, :], square(wout_ref.at[slot])) * slope).astype(BF16)
        dinner_ref[rows, :] = dinner
        res_ref[rows, :] += dot(active, square(wout_ref.at[slot]))
        dn2_ref[rows, :] += dot_nt(dinner, square(win_ref.at[slot]))

    point(1)

    @pl.when((part < PARTS - 1) & (block == blocks - 1))
    def _():
        weights(part + 1, True)

    def stage(which, first, value):
        for owner in range(OWNERS):
            z, x, core = owner // 4, owner // 2 % 2, owner % 2
            staged_ref[which, z, x, core, :, first : first + 256] = value[SHARE * owner : SHARE * (owner + 1), :]

    @pl.when((part < PARTS) & (block == blocks - 1))
    def _():
        for first in range(0, width, 256):
            stage(0, first, dot_tn(n2_ref[...], dinner_ref[:, first : first + 256]).astype(BF16))
        keep(part, 0).start()
        for first in range(0, width, 256):
            stage(1, first, dot_tn(act_ref[...], bg_ref[:, first : first + 256]).astype(BF16))
        keep(part, 1).start()

    @pl.when(part == PARTS)
    def _():
        result = res_ref[rows, :]
        out_ref[...] = result.astype(BF16)
        chosen, counts = pool_terms(flags_ref[block], instr_ref[block])
        line = iota((8, LENGTH), 0)
        picks = jnp.where(line == 0, chosen[0], jnp.where(line == 1, chosen[1], 0.0)).astype(BF16)
        high = result.astype(BF16)
        low = (result - high.astype(F32)).astype(BF16)
        total = dot(picks, high) + dot(picks, low)
        total = total / jnp.where(iota((8, 1), 0) == 0, counts[0], counts[1])
        pooled_ref[block] = total[0:2, :]
        change, _ = norm_back(mid_ref[...], gains_ref[1:2, :], dn2_ref[rows, :])
        out_low = (bg_ref[rows, :].astype(F32) + change).astype(BF16)
        gm_ref[...] = out_low
        output = square(wo_ref)
        for group in range(GROUPS):
            mine = slice(group * GROUP_ROWS, (group + 1) * GROUP_ROWS)
            dmix_ref[group, 0] = dot_nt(output[mine, :], out_low).astype(BF16)
            dwo_ref[mine, :] += dot(mix_ref[group, 0], out_low)

    @pl.when(step == (PARTS + 1) * blocks - 1)
    def _():
        for first in range(0, width, 256):
            stage(0, first, dwo_ref[:, first : first + 256].astype(BF16))
        keep(PARTS, 0).start()
        keep(PARTS, 0).wait()


def feed(n2, bg, mid, flags, instr, gains, mix, early, late, fast):
    tokens, width = n2.shape
    seqs = tokens // LENGTH
    rows = pl.BlockSpec((LENGTH, width), lambda c, m: (jnp.where(c == PARTS, m, 0), 0))
    heads = pl.BlockSpec((GROUPS, 1, GROUP_ROWS, LENGTH), lambda c, m: (0, jnp.where(c == PARTS, m, 0), 0, 0))
    piece = (DEPTH, WIDE, CORES, SHARE, width)
    sums = FEED_SUMS
    out_specs = [rows, whole((seqs, 2, width)), rows, heads, ANY]
    out_shape = [
        jax.ShapeDtypeStruct((tokens, width), BF16), jax.ShapeDtypeStruct((seqs, 2, width), F32),
        jax.ShapeDtypeStruct((tokens, width), BF16), jax.ShapeDtypeStruct((GROUPS, seqs, GROUP_ROWS, LENGTH), BF16),
        jax.ShapeDtypeStruct((2 * PARTS + 1, *piece), BF16),
    ]
    scratch = [
        pltpu.VMEM((tokens, width), BF16), pltpu.VMEM((tokens, width), BF16),
        pltpu.VMEM((tokens, width), F32), pltpu.VMEM((tokens, width), F32), pltpu.VMEM((tokens, width), BF16),
        pltpu.VMEM((tokens, width), BF16), pltpu.VMEM((2, *piece), BF16), pltpu.VMEM((2, *piece), BF16),
        pltpu.VMEM(piece, BF16), pltpu.VMEM((width, width), F32), pltpu.VMEM((2, *piece), BF16), pltpu.SemaphoreType.DMA((2, 4)),
        pltpu.SemaphoreType.DMA((3, seqs)),
    ]
    if fast:
        out_specs += [whole((sums, SHARE, width)), ANY]
        out_shape += [
            jax.ShapeDtypeStruct((sums, SHARE, width), F32), jax.ShapeDtypeStruct((FEED_PIECES, *piece), BF16)
        ]
        scratch += gather_sems(FEED_PIECES) + scatter_scratch(sums, SHARE, width)
    return pl.pallas_call(
        partial(feed_kernel, fast=fast),
        name="feed",
        grid=(PARTS + 1, seqs),
        in_specs=[
            ANY, ANY, ANY, whole((seqs, 1, LENGTH)), whole((seqs, 1, LENGTH)), whole((8, width)), rows, heads, ANY, ANY,
        ],
        out_specs=out_specs,
        out_shape=out_shape,
        scratch_shapes=scratch,
        compiler_params=pltpu.CompilerParams(
            vmem_limit_bytes=VMEM_LIMIT, collective_id=2 if fast else None, has_side_effects=fast
        ),
    )(n2, bg, mid, flags, instr, gains, mid, mix, early, late)


def back_kernel(
    x_ref, gm_ref, gains_ref, weights_hbm, qkv_ref, p_ref, inv_ref, mix_ref, dmix_ref, early_hbm,
    ig_ref, parts_hbm, small_ref, *rest, fast,
):
    if fast:
        sums_ref, tail_ref = rest[0:2]
        rest = rest[2:]
    band_ref, flipped_ref, grads_ref, wg_ref, diag_ref, staged_ref, ds_ref, sem, weight_sem = rest[:9]
    group, seq = pl.program_id(0), pl.program_id(1)
    seqs = pl.num_programs(1)
    step = group * seqs + seq
    width = x_ref.shape[1]
    if fast:
        extra = len(scatter_scratch(1, SHARE, width))
        scratch, tail_scratch = rest[9 : 9 + extra], rest[9 + extra :]
        here = place()

        def main(phase, piece):
            if phase > 0:
                scatter_phase(phase, piece, here, early_hbm.at[0], sums_ref, *scratch)
                return

            @pl.when(piece < BACK_BEFORE)
            def _():
                scatter_phase(phase, piece, here, early_hbm.at[FEED_SUMS + piece], sums_ref, *scratch)

            @pl.when(piece >= BACK_BEFORE)
            def _():
                scatter_phase(phase, piece, here, parts_hbm.at[piece - BACK_BEFORE], sums_ref, *scratch)

        def tail(phase, piece):
            if phase > 0:
                scatter_phase(phase, piece, here, small_ref, tail_ref, *tail_scratch)
                return
            scatter_phase(phase, GROUPS, here, small_ref, tail_ref, *tail_scratch)

        def tail_start(which):
            mine = slice(which * SMALL, (which + 1) * SMALL)
            scatter_phase(0, which, here, staged_ref.at[:, :, :, :, mine], tail_ref, *tail_scratch)

        def travel(slot):
            run_slot(slot, BACK_SCATTER, main)
            run_slot(slot, TAIL_SCATTER, tail)

        def point(at):
            travel(2 * step + at)
    else:
        point = lambda at: None
    keep = lambda: pltpu.make_async_copy(staged_ref, parts_hbm.at[group], sem)
    lanes = pl.ds(pl.multiple_of(seq * LENGTH, LENGTH), LENGTH)

    def hidden_terms():
        hidden = x_ref[...].astype(F32)
        scale = lax.rsqrt(jnp.mean(hidden * hidden, axis=1, keepdims=True) + EPS)
        return hidden, scale

    load_weights = lambda: pltpu.make_async_copy(weights_hbm.at[0:GROUPS], wg_ref, weight_sem)

    @pl.when(step == 0)
    def _():
        load_weights().start()

    if fast:

        @pl.when(step == 0)
        def _():
            greet(here)

    @pl.when(group == 0)
    def _():
        hidden, scale = hidden_terms()
        flipped_ref[:, lanes] = (hidden * scale * gains_ref[0:1, :]).astype(BF16).T

    @pl.when((seq == 0) & (group < GROUPS))
    def _():
        band_ref[...] = jnp.zeros_like(band_ref)

    def one_head(head):
        at = head * HEAD_DIM
        rows = lambda which: qkv_ref[0, 0, which * GROUP_ROWS + at : which * GROUP_ROWS + at + HEAD_DIM, :]
        grads = dmix_ref[0, 0, at : at + HEAD_DIM, :].astype(F32) * inv_ref[0, 0, head]
        grads = grads.astype(BF16)
        delta = jnp.sum(grads.astype(F32) * mix_ref[0, 0, at : at + HEAD_DIM, :].astype(F32), axis=0, keepdims=True)
        grad_prob = dot_tn(rows(2), grads)
        for column in range(BLOCKS):
            mine = span(column, column + 1)
            for row in range(BLOCKS):
                seen = span(row, row + 1)
                value = p_ref[0, 0, head, seen, mine].astype(F32) * (grad_prob[seen, mine] - delta[:, mine])
                band_ref[head, span(row - column + BLOCKS - 1, row - column + BLOCKS), :] += value
                ds_ref[head % 2, seen, mine] = value.astype(BF16)
        scores = ds_ref[head % 2]
        grads_ref[group, at : at + HEAD_DIM, lanes] = dot(rows(1), scores).astype(BF16)
        grads_ref[group, GROUP_ROWS + at : GROUP_ROWS + at + HEAD_DIM, lanes] = dot_nt(rows(0), scores).astype(BF16)
        grads_ref[group, 2 * GROUP_ROWS + at : 2 * GROUP_ROWS + at + HEAD_DIM, lanes] = dot_nt(grads, p_ref[0, 0, head]).astype(BF16)

    point(0)

    @pl.when(group < GROUPS)
    def _():
        one_head(0)
        one_head(1)

    @pl.when(group < GROUPS)
    def _():
        point(1)

    @pl.when(group < GROUPS)
    def _():
        one_head(2)
        one_head(3)

    @pl.when((seq == seqs - 1) & (group < GROUPS))
    def _():
        for first in range(0, width, 256):
            value = dot_nt(flipped_ref[...], grads_ref[group, first : first + 256, :]).astype(BF16)
            for owner in range(OWNERS):
                z, x, core = owner // 4, owner // 2 % 2, owner % 2
                staged_ref[z, x, core, :, first : first + 256] = value[SHARE * owner : SHARE * (owner + 1), :]
        last_fast = fast & (group == GROUPS - 1)

        @pl.when(jnp.logical_not(last_fast))
        def _():
            keep().start()

        if fast:

            @pl.when(last_fast)
            def _():
                for which in range(3):
                    tail_start(which)

        for head in range(GROUP):
            turned = band_ref[head].T
            total = jnp.zeros((8, OFFSETS), F32)
            for some in range(BLOCK // 8):
                wide = jnp.concatenate([turned[8 * some : 8 * some + 8, :], jnp.zeros((8, BLOCK), F32)], axis=1)
                total = total + pltpu.roll(wide, BLOCK - 8 * some, 1)
            line = iota((8, OFFSETS), 0)
            moved = total
            for row in range(1, 8):
                moved = jnp.where(line == row, pltpu.roll(total, OFFSETS - row, 1), moved)
            diag_ref[pl.ds(group * GROUP + head, 1)] = jnp.sum(moved, axis=0, keepdims=True)[None]
        @pl.when(jnp.logical_not(last_fast))
        def _():
            keep().wait()

    @pl.when((seq == seqs - 1) & (group == GROUPS - 1))
    def _():
        heads, buckets = table_places()
        onehot = (bucket_of(iota((OFFSETS, 1), 0) - BLOCKS * BLOCK) == buckets).astype(F32).astype(BF16)
        row = iota((16, width), 0)
        sums = jnp.concatenate([diag_ref[head] for head in range(HEADS)] + [jnp.zeros((16 - HEADS, OFFSETS), F32)], axis=0)
        high = sums.astype(BF16)
        low = (sums - high.astype(F32)).astype(BF16)
        entries = dot(high, onehot) + dot(low, onehot)
        entries = jnp.sum(jnp.where((row == heads) & (buckets >= 0), entries, 0.0), axis=0, keepdims=True)
        column = jnp.broadcast_to(entries, (BLOCK, width)).T.astype(BF16)
        for owner in range(OWNERS):
            z, x, core = owner // 4, owner // 2 % 2, owner % 2
            mine = column[SHARE * owner : SHARE * (owner + 1), :]
            small_ref[z, x, core, :, 0:BLOCK] = mine
            small_ref[z, x, core, :, BLOCK:SMALL] = mine

    @pl.when((group == GROUPS) & (seq == 0))
    def _():
        load_weights().wait()

    @pl.when(group == GROUPS)
    def _():
        hidden, scale = hidden_terms()
        flat = wg_ref[...].reshape(GROUPS, width, width)
        cotangent = sum(dot(flat[one], grads_ref[one, :, lanes]) for one in range(GROUPS)).T
        scaled = cotangent * gains_ref[0:1, :]
        unit = hidden * scale
        inner = jnp.mean(scaled * unit, axis=1, keepdims=True)
        ig_ref[...] = (gm_ref[...].astype(F32) + scale * (scaled - unit * inner)).astype(BF16)

    @pl.when(group == GROUPS)
    def _():
        point(1)

    if fast:

        @pl.when(step == (GROUPS + 1) * seqs - 1)
        def _():
            run_rest((2 * GROUPS + 2) * (flipped_ref.shape[1] // LENGTH), [BACK_SCATTER, TAIL_SCATTER], travel)


def back(x, gm, gains, weights, qkv, p, inv, mix, dmix, early, fast):
    tokens, width = x.shape
    seqs = tokens // LENGTH
    piece = (DEPTH, WIDE, CORES, SHARE, width)
    last = GROUPS - 1
    group_at = lambda g: jnp.minimum(g, last)
    seq_at = lambda g, s: jnp.where(g <= last, s, seqs - 1)
    four = lambda rows: pl.BlockSpec((1, 1, rows, LENGTH), lambda g, s: (group_at(g), seq_at(g, s), 0, 0))
    x_rows = pl.BlockSpec((LENGTH, width), lambda g, s: (jnp.where((g == 0) | (g == GROUPS), s, 0), 0))
    end_rows = pl.BlockSpec((LENGTH, width), lambda g, s: (jnp.where(g == GROUPS, s, 0), 0))
    out_specs = [end_rows, ANY, whole((DEPTH, WIDE, CORES, SHARE, SMALL))]
    out_shape = [
        jax.ShapeDtypeStruct((tokens, width), BF16), jax.ShapeDtypeStruct((GROUPS, *piece), BF16),
        jax.ShapeDtypeStruct((DEPTH, WIDE, CORES, SHARE, SMALL), BF16),
    ]
    scratch = [
        pltpu.VMEM((GROUP, BAND, BLOCK), F32), pltpu.VMEM((width, tokens), BF16), pltpu.VMEM((GROUPS, width, tokens), BF16),
        pltpu.VMEM((GROUPS, *piece), BF16), pltpu.VMEM((HEADS, 1, OFFSETS), F32), pltpu.VMEM(piece, BF16),
        pltpu.VMEM((2, LENGTH, LENGTH), BF16), pltpu.SemaphoreType.DMA,
        pltpu.SemaphoreType.DMA,
    ]
    kernel = partial(back_kernel, fast=fast)
    if fast:
        sums = BACK_SUMS
        out_specs += [whole((sums, SHARE, width)), whole((TAIL_SUMS, SHARE, SMALL))]
        out_shape += [jax.ShapeDtypeStruct((sums, SHARE, width), F32), jax.ShapeDtypeStruct((TAIL_SUMS, SHARE, SMALL), F32)]
        scratch += scatter_scratch(sums, SHARE, width) + scatter_scratch(TAIL_SUMS, SHARE, SMALL, TAIL_SUMS)
    return pl.pallas_call(
        kernel,
        name="back",
        grid=(GROUPS + 1, seqs),
        in_specs=[
            x_rows, end_rows, whole((8, width)),
            ANY, four(width),
            pl.BlockSpec((1, 1, GROUP, LENGTH, LENGTH), lambda g, s: (group_at(g), seq_at(g, s), 0, 0, 0)),
            pl.BlockSpec((1, 1, GROUP, 1, LENGTH), lambda g, s: (group_at(g), seq_at(g, s), 0, 0, 0)),
            four(GROUP_ROWS), four(GROUP_ROWS), ANY,
        ],
        out_specs=out_specs,
        out_shape=out_shape,
        scratch_shapes=scratch,
        compiler_params=pltpu.CompilerParams(
            vmem_limit_bytes=VMEM_LIMIT, collective_id=3 if fast else None, has_side_effects=fast
        ),
    )(x, gm, gains, weights, qkv, p, inv, mix, dmix, early)


def ordered(rows, w_query, w_key, w_value, w_output, w_in, w_out):
    width = w_query.shape[1]
    groups = [
        jnp.concatenate([one[:, at * GROUP_ROWS : (at + 1) * GROUP_ROWS] for one in (w_query, w_key, w_value)], axis=1)
        for at in range(GROUPS)
    ]
    inner = w_in.reshape(rows, OWNERS, PARTS, SHARE).transpose(2, 0, 1, 3).reshape(PARTS, rows, width)
    outer = w_out.reshape(-1, PARTS, SHARE, width).transpose(1, 0, 2, 3).reshape(PARTS, rows, width)
    parts = [one for at in range(PARTS) for one in (inner[at], outer[at])]
    return jnp.stack(groups + [w_output] + parts)


def small_of(gain_attn, gain_ffn, rel_table):
    lines = [one.reshape(-1, 1, share) for one, share in ((gain_attn, SHARE), (gain_ffn, SHARE), (rel_table, TABLE_SHARE))]
    padded = [jnp.pad(one, ((0, 0), (0, 0), (0, BLOCK - one.shape[2]))) for one in lines]
    return jnp.pad(jnp.concatenate(padded, axis=1), ((0, 0), (0, 13), (0, 0)))


def shards(
    hidden_in, out_grad, pooled_gradient, gain_attn, w_query, w_key, w_value, w_output, rel_table, gain_ffn, w_in, w_out,
    pair_flags, instruction_mask, *, fast,
):
    width = hidden_in.shape[1]
    own = (w_query, w_key, w_value, w_output, w_in, w_out)
    if fast:
        shares = ordered(w_query.shape[0], *own)
        small = small_of(gain_attn, gain_ffn, rel_table)[0]
    else:
        gather = lambda one: lax.all_gather(one, "fsdp", axis=0, tiled=True)
        shares = ordered(width, *map(gather, own)).reshape(-1, DEPTH, WIDE, CORES, SHARE, width)
        small = small_of(*map(gather, (gain_attn, gain_ffn, rel_table)))
    flags = pair_flags.reshape(-1, 1, LENGTH)
    instr = instruction_mask.reshape(-1, 1, LENGTH)
    qkv, p, inv, mix, mid, n2, bg, gains, *rest = attend(
        hidden_in, out_grad, pooled_gradient, flags, instr, shares, small, fast
    )
    early = rest[0] if fast else shares
    output, pooled, gm, dmix, parts, *rest = feed(
        n2, bg, mid, flags, instr, gains, mix, early, shares, fast
    )
    early_sums = rest[0] if fast else None
    input_grad, group_parts, small_parts, *rest = back(hidden_in, gm, gains, early, qkv, p, inv, mix, dmix, parts, fast)
    if fast:
        last = rest[1][:GROUPS].transpose(1, 0, 2).reshape(1, SHARE, width)
        sums = jnp.concatenate([early_sums, rest[0], last])
        table = rest[1][GROUPS, :TABLE_SHARE, 0]
        rows = SHARE
    else:
        sums = jnp.concatenate([parts, group_parts]).reshape(-1, width, width)
        table = small_parts.reshape(OWNERS, SHARE, SMALL)[:, :TABLE_SHARE, 0].reshape(-1)
        rows = width
    groups = [sums[2 * PARTS + 1 + at] for at in range(GROUPS)]
    grad_query, grad_key, grad_value = (
        jnp.concatenate([one[:, at * GROUP_ROWS : (at + 1) * GROUP_ROWS] for one in groups], axis=1) for at in range(3)
    )
    grad_output = sums[2 * PARTS]
    grad_in = sums[0 : 2 * PARTS : 2].reshape(PARTS, rows, OWNERS, SHARE).transpose(1, 2, 0, 3).reshape(rows, -1)
    grad_out = sums[1 : 2 * PARTS : 2].reshape(PARTS, -1, SHARE, width).transpose(1, 0, 2, 3).reshape(-1, width)
    if not fast:
        scatter = lambda one: lax.psum(lax.psum_scatter(one, "fsdp", scatter_dimension=0, tiled=True), "grp").astype(F32)
        grad_query, grad_key, grad_value, grad_output, grad_in, grad_out, table = map(
            scatter, (grad_query, grad_key, grad_value, grad_output, grad_in, grad_out, table)
        )
    weigh = lambda weight, grad: jnp.sum(weight.astype(F32) * grad, axis=1)
    grad_gain = weigh(w_query, grad_query) + weigh(w_key, grad_key) + weigh(w_value, grad_value)
    return (
        output, pooled, input_grad, grad_gain / gain_attn.astype(F32),
        grad_query, grad_key, grad_value, grad_output, table.astype(F32),
        weigh(w_in, grad_in) / gain_ffn.astype(F32), grad_in, grad_out,
    )


def solution(mesh):
    tokens, square, line = P(("grp", "fsdp"), None), P("fsdp", None), P("fsdp")
    cube, flat = P(("grp", "fsdp"), None, None), P(("grp", "fsdp"))
    fast = mesh.shape["fsdp"] == OWNERS and mesh.shape["grp"] == 2
    return jax.shard_map(
        partial(shards, fast=fast),
        mesh=mesh,
        in_specs=(tokens, tokens, cube, line, square, square, square, square, line, line, square, square, flat, flat),
        out_specs=(tokens, cube, tokens, line, square, square, square, square, line, line, square, square),
        check_vma=False,
    )
```

```python
from functools import partial

import jax
import jax.numpy as jnp
from jax import lax
from jax.experimental import pallas as pl
from jax.experimental.pallas import tpu as pltpu
from jax.sharding import PartitionSpec as P

HEADS = 12
HEAD_DIM = 64
BUCKETS = 32
LENGTH = 512
BLOCK = 128
BLOCKS = LENGTH // BLOCK
BAND_BLOCKS = 2 * BLOCKS - 1
BAND = BAND_BLOCKS * BLOCK
OFFSETS = BAND + BLOCK
GROUPS = 3
GROUP = HEADS // GROUPS
GROUP_ROWS = GROUP * HEAD_DIM
OWNERS, PARTS, SHARE = 16, 4, 48
TABLE_SHARE = HEADS * BUCKETS // OWNERS
SMALL = 256
EPS = 1e-06
NEG = -1e30
LIMITS = (12, 16, 23, 32, 46, 64, 91)
ROOT = 0.7978845608028654
CUBE = 0.044715
F32 = jnp.float32
BF16 = jnp.bfloat16
ANY = pl.BlockSpec(memory_space=pl.ANY)
VMEM_LIMIT = 63 * 1024 * 1024


def bucket_of(offset):
    distance = jnp.abs(offset)
    far_bucket = jnp.full(offset.shape, 8, jnp.int32)
    for threshold in LIMITS:
        far_bucket = far_bucket + (distance >= threshold).astype(jnp.int32)
    near_bucket = jnp.where(distance < 8, distance, far_bucket)
    return near_bucket + BUCKETS // 2 * (offset > 0).astype(jnp.int32)


def dot(a, b):
    return lax.dot_general(a, b, (((1,), (0,)), ((), ())), preferred_element_type=F32)


def dot_nt(a, b):
    return lax.dot_general(a, b, (((1,), (1,)), ((), ())), preferred_element_type=F32)


def dot_tn(a, b):
    return lax.dot_general(a, b, (((0,), (0,)), ((), ())), preferred_element_type=F32)


def dot_tt(a, b):
    return lax.dot_general(a, b, (((0,), (1,)), ((), ())), preferred_element_type=F32)


def iota(shape, axis):
    return lax.broadcasted_iota(jnp.int32, shape, axis)


def whole(shape):
    zeros = (0,) * len(shape)
    return pl.BlockSpec(shape, lambda *_: zeros, pipeline_mode=pl.Buffered(1))


def span(first, last):
    return slice(first * BLOCK, last * BLOCK)


def pool_terms(flags, instruction):
    kept = (instruction == 0).astype(F32)
    chosen = [kept * (flags == part).astype(F32) for part in range(2)]
    counts = [jnp.sum(one, axis=1, keepdims=True) for one in chosen]
    return chosen, counts


def pool_gradient(chosen, counts, pooled_grad):
    row = iota((16, LENGTH), 0)
    picks = jnp.where(row % 2 == 0, chosen[0], chosen[1])
    picks = jnp.where(row < 6, picks, 0.0).astype(BF16)
    scaled = [pooled_grad[part : part + 1, :] / counts[part] for part in range(2)]
    line = iota((16, pooled_grad.shape[1]), 0)
    both = jnp.where(line % 2 == 0, scaled[0], scaled[1])
    high = both.astype(BF16).astype(F32)
    rest = both - high
    middle = rest.astype(BF16).astype(F32)
    low = rest - middle
    parts = jnp.where(line < 2, high, jnp.where(line < 4, middle, jnp.where(line < 6, low, 0.0)))
    return dot_tn(picks, parts.astype(BF16))


def norm_back(value, gain, cotangent):
    scale = lax.rsqrt(jnp.mean(value * value, axis=1, keepdims=True) + EPS)
    scaled = cotangent * gain
    unit = value * scale
    inner = jnp.mean(scaled * unit, axis=1, keepdims=True)
    return scale * (scaled - unit * inner), jnp.sum(cotangent * unit, axis=0, keepdims=True)


def owners_of():
    at = iota((1, OWNERS * SHARE), 1)
    owner = sum((at >= SHARE * one).astype(jnp.int32) for one in range(1, OWNERS))
    return owner, at - SHARE * owner


def table_places():
    owner, inside = owners_of()
    entry = owner * TABLE_SHARE + inside
    bucket = sum((entry >= HEADS * one).astype(jnp.int32) for one in range(1, BUCKETS))
    return entry - HEADS * bucket, jnp.where(inside < TABLE_SHARE, bucket, -1)


DEPTH, WIDE, CORES = 4, 2, 2
MESH_ID = pl.DeviceIdType.MESH


def place():
    grp, at = lax.axis_index("grp"), lax.axis_index("fsdp")
    z, x, core = lax.div(at, WIDE * CORES), lax.rem(lax.div(at, CORES), WIDE), lax.rem(at, CORES)

    def device(grp, z, x, core):
        return (grp, z * (WIDE * CORES) + x * CORES + core)

    return dict(
        at=at, y=grp, z=z, x=x, core=core,
        over_y=device(1 - grp, z, x, core),
        over_x=device(grp, z, 1 - x, core),
        over_core=device(grp, z, x, 1 - core),
        over_z=[device(grp, lax.rem(z + one, DEPTH), x, core) for one in range(1, DEPTH)],
        ahead=[lax.rem(z + one, DEPTH) for one in range(1, DEPTH)],
        behind=[lax.rem(z + DEPTH - one, DEPTH) for one in range(1, DEPTH)],
    )


def greet(here):
    barrier = pltpu.get_barrier_semaphore()
    for device in (here["over_y"], here["over_x"], here["over_core"], *here["over_z"]):
        pl.semaphore_signal(barrier, inc=1, device_id=device, device_id_type=MESH_ID)
    pl.semaphore_wait(barrier, DEPTH + 2)


def others(here):
    at = here["at"]
    for one in range(1, OWNERS):
        yield one, (here["y"], lax.rem(at + one, OWNERS)), lax.rem(at + OWNERS - one, OWNERS)


def greet_all(here):
    barrier = pltpu.get_barrier_semaphore()
    pl.semaphore_signal(barrier, inc=1, device_id=here["over_y"], device_id_type=MESH_ID)
    for _, device, _ in others(here):
        pl.semaphore_signal(barrier, inc=1, device_id=device, device_id_type=MESH_ID)
    pl.semaphore_wait(barrier, OWNERS)


def gather_phase(phase, sem, here, share_ref, whole_ref, sent, got, own_sem, shared=False):
    z, x, core = here["z"], here["x"], here["core"]
    every = slice(None)
    half = share_ref.shape[-1] // 2
    lanes = pl.ds(pl.multiple_of(here["y"] * half, half), half) if shared else every
    other = pl.ds(pl.multiple_of((1 - here["y"]) * half, half), half) if shared else every
    mine = share_ref.at[:, lanes] if shared else share_ref

    def copy(source, where, channel, device):
        return pltpu.make_async_remote_copy(
            src_ref=source, dst_ref=whole_ref.at[where], send_sem=sent.at[channel, sem], recv_sem=got.at[channel, sem],
            device_id=device, device_id_type=MESH_ID,
        )

    def same(where, channel, device):
        return copy(whole_ref.at[where], where, channel, device)

    own = lambda: pltpu.make_async_copy(mine, whole_ref.at[z, x, core, every, lanes], own_sem.at[sem])
    line_out = lambda one: copy(mine, (z, x, core, every, lanes), one, here["over_z"][one])
    line_in = lambda one: copy(mine, (here["behind"][one], x, core, every, lanes), one, here["over_z"][one])
    side_out = lambda: same((every, x, core, every, lanes), 3, here["over_x"])
    side_in = lambda: same((every, 1 - x, core, every, lanes), 3, here["over_x"])
    group_out = lambda: same((every, every, core, every, lanes), 5, here["over_y"])
    group_in = lambda: same((every, every, core, every, other), 5, here["over_y"])
    core_out = lambda: same((every, every, core), 4, here["over_core"])
    core_in = lambda: same((every, every, 1 - core), 4, here["over_core"])
    if phase == 0:
        own().start()
        for one in range(DEPTH - 1):
            line_out(one).start()
    elif phase == 1:
        own().wait()
        for one in range(DEPTH - 1):
            line_in(one).wait_recv()
        side_out().start()
    elif phase == 2:
        side_in().wait_recv()
        group_out().start()
    elif phase == 3:
        if shared:
            group_in().wait_recv()
        else:
            side_in().wait_recv()
        core_out().start()
    else:
        for one in range(DEPTH - 1):
            line_out(one).wait_send()
        side_out().wait_send()
        if shared:
            group_out().wait_send()
        core_out().wait_send()
        core_in().wait_recv()


def scatter_phase(phase, piece, here, part_ref, out_ref, own, fromc, fromx, fromz, last, sent, got, own_sem):
    z, x, core = here["z"], here["x"], here["core"]
    slot = lax.rem(piece, own.shape[0])

    def remote(source, target, channel, device):
        return pltpu.make_async_remote_copy(
            src_ref=source, dst_ref=target, send_sem=sent.at[channel, piece], recv_sem=got.at[channel, piece],
            device_id=device, device_id_type=MESH_ID,
        )

    total = fromc.at[piece]
    over_core = lambda: remote(part_ref.at[:, :, 1 - core], total, 0, here["over_core"])
    load = lambda: pltpu.make_async_copy(part_ref.at[:, :, core], own.at[slot], own_sem.at[slot])
    over_x = lambda: remote(fromc.at[piece, :, 1 - x], fromx.at[piece], 1, here["over_x"])
    line_out = lambda one: remote(fromc.at[piece, here["ahead"][one], x], fromz.at[piece, z], 2 + one, here["over_z"][one])
    line_in = lambda one: remote(
        fromc.at[piece, z, x], fromz.at[piece, here["behind"][one]], 2 + one, here["over_z"][one]
    )
    final = lambda: remote(fromc.at[piece, z, x], last.at[piece], 5, here["over_y"])

    if phase == 0:
        over_core().start()
        load().start()
    elif phase == 1:
        load().wait()
        over_core().wait()

        def one(at, _):
            for side in range(WIDE):
                fromc[piece, at, side] = own[slot, at, side] + fromc[piece, at, side]
            return 0

        lax.fori_loop(0, DEPTH, one, 0)
        over_x().start()
    elif phase == 2:
        over_x().wait()

        def one(at, _):
            fromc[piece, at, x] = fromc[piece, at, x] + fromx[piece, at]
            return 0

        lax.fori_loop(0, DEPTH, one, 0)
        for one in range(DEPTH - 1):
            line_out(one).start()
    elif phase == 3:
        mine = fromc[piece, z, x].astype(F32)
        for one in range(DEPTH - 1):
            line_in(one).wait_recv()
            mine = mine + fromz[piece, here["behind"][one]].astype(F32)
        fromc[piece, z, x] = mine.astype(BF16)
        final().start()
    else:
        for one in range(DEPTH - 1):
            line_out(one).wait_send()
        final().wait()
        out_ref[piece] = fromc[piece, z, x].astype(F32) + last[piece].astype(F32)


def run_slot(slot, table, act):
    for phase in reversed(range(max(map(len, table.values())))):
        due, found = False, 0
        for piece, slots in table.items():
            if slots[phase] is not None:
                now = slot == slots[phase]
                due, found = due | now, jnp.where(now, piece, found)
        if due is not False:

            @pl.when(due)
            def _(phase=phase, found=found):
                act(phase, found)


def run_rest(first, tables, travel):
    end = 1 + max(slot for table in tables for slots in table.values() for slot in slots if slot is not None)

    def one(slot, _):
        travel(slot)
        return 0

    if end > first:
        lax.fori_loop(first, end, one, 0)


def gather_sems(pieces):
    return [pltpu.SemaphoreType.DMA((6, pieces)), pltpu.SemaphoreType.DMA((6, pieces)), pltpu.SemaphoreType.DMA((pieces,))]


def scatter_scratch(pieces, rows, columns, places=2):
    return [
        pltpu.VMEM((places, DEPTH, WIDE, rows, columns), BF16),
        pltpu.VMEM((pieces, DEPTH, WIDE, rows, columns), BF16),
        pltpu.VMEM((pieces, DEPTH, rows, columns), BF16),
        pltpu.VMEM((pieces, DEPTH, rows, columns), BF16),
        pltpu.VMEM((pieces, rows, columns), BF16),
        pltpu.SemaphoreType.DMA((6, pieces)),
        pltpu.SemaphoreType.DMA((6, pieces)),
        pltpu.SemaphoreType.DMA((places,)),
    ]


ATTEND_PIECES, FEED_PIECES = 8, 4
ATTEND_DIRECT = {1: (None, 0, None, 3, 5), 3: (2, 7, None, 12, 14), 6: (8, 13, None, 18, 20)}
ATTEND_SHARED = {2: (0, 4, 7, 11, 13), 4: (4, 8, 12, 16, 18), 5: (6, 10, 15, 19, 21), 7: (11, 15, 19, 23, 25)}
FEED_GATHER = {0: (0, 5, None, 10, 12), 1: (3, 8, None, 13, 15), 2: (6, 11, None, 16, 18), 3: (9, 14, None, 19, 21)}
FEED_SUMS = 5
FEED_SCATTER = {
    0: (8, 10, 15, 20, 23), 1: (11, 13, 18, 23, 26), 2: (16, 18, 23, 28, 31), 3: (19, 21, 26, 31, 34), 4: (24, 26, 31, 36, 39),
}
BACK_BEFORE, BACK_SUMS = 4, 6
BACK_SCATTER = {
    0: (0, 2, 7, 12, 15), 1: (3, 5, 10, 15, 18), 2: (6, 8, 13, 18, 21), 3: (9, 11, 16, 21, 24),
    4: (12, 14, 19, 24, 27), 5: (16, 18, 23, 27, 29),
}
TAIL_SUMS = 4
TAIL_SCATTER = {0: (None, 24, 26, 28, 30), 1: (None, 25, 27, 29, 31), 2: (None, 26, 28, 30, 32), 3: (24, 27, 29, 31, 33)}


def arrange_kernel(wq_ref, wk_ref, wv_ref, wo_ref, win_ref, wout_ref, shares_ref, line_ref):
    for group in range(GROUPS):
        mine = slice(group * GROUP_ROWS, (group + 1) * GROUP_ROWS)
        for which, one in enumerate((wq_ref, wk_ref, wv_ref)):
            shares_ref[group, :, which * GROUP_ROWS : (which + 1) * GROUP_ROWS] = one[:, mine]
    shares_ref[GROUPS] = wo_ref[...]
    for part in range(PARTS):
        for owner in range(OWNERS):
            at = (owner * PARTS + part) * SHARE
            line_ref[:, owner * SHARE : (owner + 1) * SHARE] = win_ref[:, at : at + SHARE].astype(F32)
        shares_ref[GROUPS + 1 + 2 * part] = line_ref[...].astype(BF16)
        shares_ref[GROUPS + 2 + 2 * part] = wout_ref[part * SHARE : (part + 1) * SHARE, :]


def arrange(*weights):
    width = weights[0].shape[1]
    return pl.pallas_call(
        arrange_kernel,
        name="arrange",
        out_shape=jax.ShapeDtypeStruct((GROUPS + 1 + 2 * PARTS, SHARE, width), BF16),
        scratch_shapes=[pltpu.VMEM((SHARE, width), F32)],
    )(*weights)


def attend_kernel(
    x_hbm, og_hbm, pg_ref, flags_ref, instr_ref, shares_hbm, small_hbm,
    qkv_ref, p_ref, inv_ref, mix_ref, mid_ref, n2_ref, bg_hbm, gains_ref, weights_hbm,
    x_ref, bg_ref, mixed_ref, band_ref, aux_ref, normed_ref, wg_ref, wo_ref, small_ref, table_ref, cur_ref, nxt_ref, sa_ref, sb_ref,
    sems, *comm, fast,
):
    group, seq = pl.program_id(0), pl.program_id(1)
    seqs = pl.num_programs(1)
    step = group * seqs + seq
    width = x_ref.shape[1]
    if fast:
        main_sems, first_sems, small_sent, small_got = comm[0:3], comm[3:6], comm[6], comm[7]
        here = place()

        def main(phase, piece, shared=False):
            gather_phase(phase, piece, here, shares_hbm.at[piece], weights_hbm.at[piece], *main_sems, shared=shared)

        def small(start):
            for one, device, source in others(here):
                copy = lambda where: pltpu.make_async_remote_copy(
                    src_ref=small_hbm, dst_ref=small_ref.at[where], send_sem=small_sent.at[one], recv_sem=small_got.at[one],
                    device_id=device, device_id_type=MESH_ID,
                )
                if start:
                    copy(here["at"]).start()
                else:
                    copy(source).wait_recv()
                    copy(here["at"]).wait_send()

        def first(phase, which):
            lanes = pl.ds(which * GROUP_ROWS, GROUP_ROWS)
            every = slice(None)
            gather_phase(
                phase, which, here, shares_hbm.at[0, :, lanes], weights_hbm.at[0, every, every, every, every, lanes], *first_sems
            )

        def travel(slot):
            run_slot(slot, ATTEND_DIRECT, main)
            run_slot(slot, ATTEND_SHARED, partial(main, shared=True))

        point = lambda at: travel(2 * step + at)
    else:
        point = lambda at: None
    small_own = small_ref.at[here["at"]] if fast else small_ref
    load_small = lambda: pltpu.make_async_copy(small_hbm, small_own, sems.at[0])
    load_hidden = lambda: pltpu.make_async_copy(x_hbm, x_ref, sems.at[3])
    load_grad = lambda: pltpu.make_async_copy(og_hbm, bg_ref, sems.at[4])
    keep_grad = lambda: pltpu.make_async_copy(bg_ref, bg_hbm, sems.at[4])
    load_group = lambda at: pltpu.make_async_copy(weights_hbm.at[at], wg_ref, sems.at[1])
    load_output = lambda: pltpu.make_async_copy(weights_hbm.at[GROUPS], wo_ref, sems.at[2])
    square = lambda ref: ref[...].reshape(width, width)

    def prepare(at):
        flags = flags_ref[at]
        chosen, counts = pool_terms(flags, instr_ref[at])
        rows = pl.ds(pl.multiple_of(at * LENGTH, LENGTH), LENGTH)
        bg_ref[rows, :] = (bg_ref[rows, :].astype(F32) + pool_gradient(chosen, counts, pg_ref[at])).astype(BF16)
        row = iota((16, LENGTH), 0)
        aux_ref[0, at] = jnp.where(row == 0, 1 - flags, jnp.where(row == 1, flags, 0)).astype(F32).astype(BF16)
        other = jnp.where(row == 0, flags, jnp.where(row == 1, 1 - flags, 0)).astype(F32) * NEG
        aux_ref[1, at] = other.astype(BF16)

    def normalize(at):
        rows = pl.ds(pl.multiple_of(at * LENGTH, LENGTH), LENGTH)
        hidden = x_ref[rows, :].astype(F32)
        scale = lax.rsqrt(jnp.mean(hidden * hidden, axis=1, keepdims=True) + EPS)
        normed_ref[at] = (hidden * scale * gains_ref[0:1, :]).astype(BF16)

    def every_seq(act):
        def one_seq(at, _):
            act(at)
            return 0

        lax.fori_loop(0, seqs, one_seq, 0)

    def project(at, target):
        target[...] = dot_tt(square(wg_ref), normed_ref[at]).astype(BF16)

    def part(source, which, head):
        first = which * GROUP_ROWS + head * HEAD_DIM
        return source[first : first + HEAD_DIM, :]

    def score(source, at_group, at, head, target):
        queries = jnp.concatenate([part(source, 0, head), aux_ref[0, at]], axis=0)
        keys = jnp.concatenate([part(source, 1, head), aux_ref[1, at]], axis=0)
        scores = dot_tn(keys, queries)
        for row in range(BLOCKS):
            for column in range(BLOCKS):
                bias = band_ref[at_group * GROUP + head, span(row - column + BLOCKS - 1, row - column + BLOCKS), :]
                target[span(row, row + 1), span(column, column + 1)] = scores[span(row, row + 1), span(column, column + 1)] + bias

    def soften(head, source):
        scores = source[...]
        exponent = jnp.exp(scores - jnp.max(scores, axis=0, keepdims=True)).astype(BF16)
        p_ref[0, 0, head] = exponent
        values = jnp.concatenate([part(cur_ref, 2, head), jnp.ones((16, LENGTH), BF16)], axis=0)
        mixed = dot(values, exponent)
        inverse = 1.0 / mixed[HEAD_DIM : HEAD_DIM + 1, :]
        inv_ref[0, 0, head] = inverse
        mixed = (mixed[0:HEAD_DIM, :] * inverse).astype(BF16)
        mix_ref[0, 0, head * HEAD_DIM : (head + 1) * HEAD_DIM, :] = mixed
        mixed_ref[seq, pl.ds(pl.multiple_of(group * GROUP_ROWS + head * HEAD_DIM, HEAD_DIM), HEAD_DIM), :] = mixed

    def read_small():
        owner, inside = owners_of()
        spread = (iota((BLOCK, width), 0) == inside).astype(F32).astype(BF16)
        shares = small_ref[...].astype(F32)

        def line(which):
            placed = dot(shares[:, which, :].astype(BF16), spread)
            return jnp.sum(jnp.where(iota((OWNERS, width), 0) == owner, placed, 0.0), axis=0, keepdims=True)

        row = iota((8, width), 0)
        gains_ref[...] = jnp.where(row == 0, line(0), line(1))
        table_row = line(2)
        heads, buckets = table_places()
        entries = jnp.where((iota((16, width), 0) == heads) & (buckets >= 0), table_row, 0.0).astype(BF16)
        onehot = (bucket_of(iota((OFFSETS, 1), 0) - BLOCKS * BLOCK) == buckets).astype(F32).astype(BF16)
        table_ref[...] = dot_nt(entries, onehot)

    def make_bands(at_group):
        def one_head(head, _):
            table = table_ref[...]
            line = jnp.sum(jnp.where(iota(table.shape, 0) == head, table, 0.0), axis=0, keepdims=True)
            turned = pltpu.roll(jnp.broadcast_to(line, (BLOCK, OFFSETS)), 0, 1, stride=1, stride_axis=0)
            band_ref[head] = turned[:, BLOCK:].T
            return 0

        lax.fori_loop(at_group * GROUP, (at_group + 1) * GROUP, one_head, 0)

    @pl.when(step == 0)
    def _():
        load_grad().start()
        load_hidden().start()
        load_small().start()
        if fast:
            greet_all(here)
            small(True)
            for which in range(3):
                first(0, which)
        load_grad().wait()
        every_seq(prepare)
        keep_grad().start()
        load_hidden().wait()
        load_small().wait()
        if fast:
            small(False)
            first(1, 0)
            read_small()
            first(1, 1)
            normalize(0)
            normalize(1)
            first(1, 2)
            main(0, 1)
            normalize(2)
            normalize(3)
            first(3, 0)
            make_bands(0)
            first(3, 1)
            make_bands(1)
            first(3, 2)
            make_bands(2)
            for which in range(3):
                first(4, which)
        else:
            read_small()
            every_seq(normalize)
            for one in range(GROUPS):
                make_bands(one)
        load_group(0).start()
        load_group(0).wait()
        project(0, nxt_ref)
        score(nxt_ref, 0, 0, 0, sa_ref)

    last_seq = seq == seqs - 1
    more = step + 1 < GROUPS * seqs
    cur_ref[...] = nxt_ref[...]
    qkv_ref[0, 0] = nxt_ref[...]

    @pl.when(last_seq & more)
    def _():
        load_group(group + 1).start()

    @pl.when((seq == 0) & (group == GROUPS - 1))
    def _():
        load_output().start()
        load_output().wait()

    next_seq = jnp.where(last_seq, 0, seq + 1)
    next_group = jnp.where(last_seq, jnp.minimum(group + 1, GROUPS - 1), group)
    point(0)
    score(cur_ref, group, seq, 1, sb_ref)
    soften(0, sa_ref)
    score(cur_ref, group, seq, 2, sa_ref)
    soften(1, sb_ref)
    point(1)
    score(cur_ref, group, seq, 3, sb_ref)
    soften(2, sa_ref)

    @pl.when(last_seq & more)
    def _():
        load_group(group + 1).wait()

    project(next_seq, nxt_ref)
    score(nxt_ref, next_group, next_seq, 0, sa_ref)
    soften(3, sb_ref)

    @pl.when(group == GROUPS - 1)
    def _():
        rows = pl.ds(pl.multiple_of(seq * LENGTH, LENGTH), LENGTH)
        middle = x_ref[rows, :].astype(F32) + dot_tn(mixed_ref[seq], square(wo_ref))
        mid_ref[...] = middle
        scale = lax.rsqrt(jnp.mean(middle * middle, axis=1, keepdims=True) + EPS)
        n2_ref[...] = (middle * scale * gains_ref[1:2, :]).astype(BF16)

    @pl.when(step == GROUPS * seqs - 1)
    def _():
        keep_grad().wait()
        if fast:
            run_rest(2 * GROUPS * (x_ref.shape[0] // LENGTH), [ATTEND_DIRECT, ATTEND_SHARED], travel)


def attend(x, og, pg, flags, instr, shares, small, fast):
    tokens, width = x.shape
    seqs = tokens // LENGTH
    last_rows = pl.BlockSpec((LENGTH, width), lambda g, s: (jnp.where(g == GROUPS - 1, s, 0), 0))
    low = jax.ShapeDtypeStruct((tokens, width), BF16)
    out_specs = [
        pl.BlockSpec((1, 1, width, LENGTH), lambda g, s: (g, s, 0, 0)),
        pl.BlockSpec((1, 1, GROUP, LENGTH, LENGTH), lambda g, s: (g, s, 0, 0, 0)),
        pl.BlockSpec((1, 1, GROUP, 1, LENGTH), lambda g, s: (g, s, 0, 0, 0)),
        pl.BlockSpec((1, 1, GROUP_ROWS, LENGTH), lambda g, s: (g, s, 0, 0)), last_rows, last_rows, ANY, whole((8, width)),
    ]
    out_shape = [
        jax.ShapeDtypeStruct((GROUPS, seqs, width, LENGTH), BF16),
        jax.ShapeDtypeStruct((GROUPS, seqs, GROUP, LENGTH, LENGTH), BF16),
        jax.ShapeDtypeStruct((GROUPS, seqs, GROUP, 1, LENGTH), F32),
        jax.ShapeDtypeStruct((GROUPS, seqs, GROUP_ROWS, LENGTH), BF16),
        jax.ShapeDtypeStruct((tokens, width), F32), low, low, jax.ShapeDtypeStruct((8, width), F32),
    ]
    scratch = [
        pltpu.VMEM((tokens, width), BF16), pltpu.VMEM((tokens, width), BF16), pltpu.VMEM((seqs, width, LENGTH), BF16),
        pltpu.VMEM((HEADS, BAND, BLOCK), F32), pltpu.VMEM((2, seqs, 16, LENGTH), BF16),
        pltpu.VMEM((seqs, LENGTH, width), BF16), pltpu.VMEM((DEPTH, WIDE, CORES, SHARE, width), BF16),
        pltpu.VMEM((DEPTH, WIDE, CORES, SHARE, width), BF16), pltpu.VMEM((OWNERS, 16, BLOCK), BF16), pltpu.VMEM((16, OFFSETS), F32),
        pltpu.VMEM((width, LENGTH), BF16), pltpu.VMEM((width, LENGTH), BF16),
        pltpu.VMEM((LENGTH, LENGTH), F32), pltpu.VMEM((LENGTH, LENGTH), F32), pltpu.SemaphoreType.DMA((5,)),
    ]
    in_specs = [
        ANY, ANY, whole((seqs, 2, width)), whole((seqs, 1, LENGTH)), whole((seqs, 1, LENGTH)), ANY, ANY,
    ]
    if fast:
        kernel = partial(attend_kernel, fast=True)
        out_specs += [ANY]
        out_shape += [jax.ShapeDtypeStruct((ATTEND_PIECES, DEPTH, WIDE, CORES, SHARE, width), BF16)]
        scratch += gather_sems(ATTEND_PIECES) + gather_sems(3) + [pltpu.SemaphoreType.DMA((OWNERS,)), pltpu.SemaphoreType.DMA((OWNERS,))]
    else:

        def kernel(*refs):
            inputs, outputs, rest = refs[:7], refs[7:15], refs[15:]
            attend_kernel(*inputs, *outputs, inputs[5], *rest, fast=False)

    return pl.pallas_call(
        kernel,
        name="attend",
        grid=(GROUPS, seqs),
        in_specs=in_specs,
        out_specs=out_specs,
        out_shape=out_shape,
        scratch_shapes=scratch,
        compiler_params=pltpu.CompilerParams(
            vmem_limit_bytes=VMEM_LIMIT, collective_id=1 if fast else None, has_side_effects=fast
        ),
    )(x, og, pg, flags, instr, shares, small)


def feed_kernel(
    n2_hbm, bg_hbm, mid_hbm, flags_ref, instr_ref, gains_ref, mid_ref, mix_ref, early_hbm, late_hbm,
    out_ref, pooled_ref, gm_ref, dmix_ref, parts_hbm, *rest, fast,
):
    if fast:
        sums_ref, gathered_hbm = rest[0:2]
        rest = rest[2:]
    n2_ref, bg_ref, res_ref, dn2_ref, act_ref, dinner_ref, win_ref, wout_ref, wo_ref, dwo_ref, staged_ref, sems, block_sems = rest[:13]
    part, block = pl.program_id(0), pl.program_id(1)
    blocks = pl.num_programs(1)
    step = part * blocks + block
    width = res_ref.shape[1]
    rows = pl.ds(pl.multiple_of(block * LENGTH, LENGTH), LENGTH)
    if fast:
        sems_of, scratch = rest[13:16], rest[16:]
        here = place()

        def travel(slot):
            def bring(phase, piece):
                share = late_hbm.at[ATTEND_PIECES + piece]
                gather_phase(phase, piece, here, share, gathered_hbm.at[piece], *sems_of)

            def add(phase, piece):
                scatter_phase(phase, piece, here, parts_hbm.at[piece], sums_ref, *scratch)

            run_slot(slot, FEED_GATHER, bring)
            run_slot(slot, FEED_SCATTER, add)

        point = lambda at: travel(2 * step + at)
    else:
        point = lambda at: None
    square = lambda ref: ref[...].reshape(width, width)

    def weights(at, start):
        def both(source, first):
            for which, target in enumerate((win_ref, wout_ref)):
                slot = lax.rem(at, 2)
                copy = pltpu.make_async_copy(source.at[first + which], target.at[slot], sems.at[slot, which])
                copy.start() if start else copy.wait()

        if start:
            pl.when(at < PARTS // 2)(lambda: both(early_hbm, 4 + 2 * at))
            pl.when(at >= PARTS // 2)(lambda: both(gathered_hbm if fast else late_hbm, 2 * at + (-PARTS if fast else 4)))
        else:
            both(early_hbm, 4)


    def load_block(at, start):
        mine = pl.ds(pl.multiple_of(at * LENGTH, LENGTH), LENGTH)
        for which, (source, target) in enumerate(((n2_hbm, n2_ref), (bg_hbm, bg_ref), (mid_hbm, res_ref))):
            copy = pltpu.make_async_copy(source.at[mine], target.at[mine], block_sems.at[which, at])
            copy.start() if start else copy.wait()

    load_output = lambda: pltpu.make_async_copy(early_hbm.at[GROUPS], wo_ref, sems.at[1, 2])
    keep = lambda at, which: pltpu.make_async_copy(staged_ref.at[which], parts_hbm.at[2 * at + which], sems.at[which, 3])

    @pl.when(step == 0)
    def _():
        weights(0, True)
        for at in range(res_ref.shape[0] // LENGTH):
            load_block(at, True)
        load_output().start()
        if fast:
            greet(here)
        dwo_ref[...] = jnp.zeros_like(dwo_ref)

    @pl.when((part == PARTS) & (block == 0))
    def _():
        load_output().wait()

    @pl.when(part == 0)
    def _():
        dn2_ref[rows, :] = jnp.zeros((LENGTH, width), F32)
        load_block(block, False)

    @pl.when((part < PARTS) & (block == 0))
    def _():
        weights(part, False)

    @pl.when((part > 0) & (block == 0))
    def _():
        keep(part - 1, 0).wait()
        keep(part - 1, 1).wait()

    point(0)

    @pl.when(part < PARTS)
    def _():
        slot = lax.rem(part, 2)
        inner = dot(n2_ref[rows, :], square(win_ref.at[slot]))
        grad_active = dot_nt(bg_ref[rows, :], square(wout_ref.at[slot]))
        squared = inner * inner
        half = 0.5 * jnp.tanh(inner * (ROOT + (ROOT * CUBE) * squared)) + 0.5
        active = inner * half
        slope = half + active * (1.0 - half) * (2.0 * ROOT + (6.0 * ROOT * CUBE) * squared)
        active = active.astype(BF16)
        act_ref[rows, :] = active
        dinner = (grad_active * slope).astype(BF16)
        dinner_ref[rows, :] = dinner
        res_ref[rows, :] += dot(active, square(wout_ref.at[slot]))
        dn2_ref[rows, :] += dot_nt(dinner, square(win_ref.at[slot]))

    point(1)

    @pl.when((part < PARTS - 1) & (block == blocks - 1))
    def _():
        weights(part + 1, True)

    def stage(which, first, value):
        for owner in range(OWNERS):
            z, x, core = owner // 4, owner // 2 % 2, owner % 2
            staged_ref[which, z, x, core, :, first : first + 256] = value[SHARE * owner : SHARE * (owner + 1), :]

    @pl.when((part < PARTS) & (block == blocks - 1))
    def _():
        for first in range(0, width, 256):
            stage(0, first, dot_tn(n2_ref[...], dinner_ref[:, first : first + 256]).astype(BF16))
        keep(part, 0).start()
        for first in range(0, width, 256):
            stage(1, first, dot_tn(act_ref[...], bg_ref[:, first : first + 256]).astype(BF16))
        keep(part, 1).start()

    @pl.when(part == PARTS)
    def _():
        result = res_ref[rows, :]
        out_ref[...] = result.astype(BF16)
        chosen, counts = pool_terms(flags_ref[block], instr_ref[block])
        line = iota((8, LENGTH), 0)
        picks = jnp.where(line == 0, chosen[0], jnp.where(line == 1, chosen[1], 0.0)).astype(BF16)
        high = result.astype(BF16)
        low = (result - high.astype(F32)).astype(BF16)
        total = dot(picks, high) + dot(picks, low)
        total = total / jnp.where(iota((8, 1), 0) == 0, counts[0], counts[1])
        pooled_ref[block] = total[0:2, :]
        change, _ = norm_back(mid_ref[...], gains_ref[1:2, :], dn2_ref[rows, :])
        out_low = (bg_ref[rows, :].astype(F32) + change).astype(BF16)
        gm_ref[...] = out_low
        output = square(wo_ref)
        for group in range(GROUPS):
            mine = slice(group * GROUP_ROWS, (group + 1) * GROUP_ROWS)
            dmix_ref[group, 0] = dot_nt(output[mine, :], out_low).astype(BF16)
            dwo_ref[mine, :] += dot(mix_ref[group, 0], out_low)

    @pl.when(step == (PARTS + 1) * blocks - 1)
    def _():
        for first in range(0, width, 256):
            stage(0, first, dwo_ref[:, first : first + 256].astype(BF16))
        keep(PARTS, 0).start()
        keep(PARTS, 0).wait()


def feed(n2, bg, mid, flags, instr, gains, mix, early, late, fast):
    tokens, width = n2.shape
    seqs = tokens // LENGTH
    rows = pl.BlockSpec((LENGTH, width), lambda c, m: (jnp.where(c == PARTS, m, 0), 0))
    heads = pl.BlockSpec((GROUPS, 1, GROUP_ROWS, LENGTH), lambda c, m: (0, jnp.where(c == PARTS, m, 0), 0, 0))
    piece = (DEPTH, WIDE, CORES, SHARE, width)
    sums = FEED_SUMS
    out_specs = [rows, whole((seqs, 2, width)), rows, heads, ANY]
    out_shape = [
        jax.ShapeDtypeStruct((tokens, width), BF16), jax.ShapeDtypeStruct((seqs, 2, width), F32),
        jax.ShapeDtypeStruct((tokens, width), BF16), jax.ShapeDtypeStruct((GROUPS, seqs, GROUP_ROWS, LENGTH), BF16),
        jax.ShapeDtypeStruct((2 * PARTS + 1, *piece), BF16),
    ]
    scratch = [
        pltpu.VMEM((tokens, width), BF16), pltpu.VMEM((tokens, width), BF16),
        pltpu.VMEM((tokens, width), F32), pltpu.VMEM((tokens, width), F32), pltpu.VMEM((tokens, width), BF16),
        pltpu.VMEM((tokens, width), BF16), pltpu.VMEM((2, *piece), BF16), pltpu.VMEM((2, *piece), BF16),
        pltpu.VMEM(piece, BF16), pltpu.VMEM((width, width), F32), pltpu.VMEM((2, *piece), BF16), pltpu.SemaphoreType.DMA((2, 4)),
        pltpu.SemaphoreType.DMA((3, seqs)),
    ]
    if fast:
        out_specs += [whole((sums, SHARE, width)), ANY]
        out_shape += [
            jax.ShapeDtypeStruct((sums, SHARE, width), F32), jax.ShapeDtypeStruct((FEED_PIECES, *piece), BF16)
        ]
        scratch += gather_sems(FEED_PIECES) + scatter_scratch(sums, SHARE, width)
    return pl.pallas_call(
        partial(feed_kernel, fast=fast),
        name="feed",
        grid=(PARTS + 1, seqs),
        in_specs=[
            ANY, ANY, ANY, whole((seqs, 1, LENGTH)), whole((seqs, 1, LENGTH)), whole((8, width)), rows, heads, ANY, ANY,
        ],
        out_specs=out_specs,
        out_shape=out_shape,
        scratch_shapes=scratch,
        compiler_params=pltpu.CompilerParams(
            vmem_limit_bytes=VMEM_LIMIT, collective_id=2 if fast else None, has_side_effects=fast
        ),
    )(n2, bg, mid, flags, instr, gains, mid, mix, early, late)


def back_kernel(
    x_ref, gm_ref, gains_ref, weights_hbm, qkv_ref, p_ref, inv_ref, mix_ref, dmix_ref, early_hbm,
    ig_ref, parts_hbm, small_ref, *rest, fast,
):
    if fast:
        sums_ref, tail_ref = rest[0:2]
        rest = rest[2:]
    band_ref, flipped_ref, grads_ref, wg_ref, diag_ref, staged_ref, ds_ref, sem, weight_sem = rest[:9]
    group, seq = pl.program_id(0), pl.program_id(1)
    seqs = pl.num_programs(1)
    step = group * seqs + seq
    width = x_ref.shape[1]
    if fast:
        extra = len(scatter_scratch(1, SHARE, width))
        scratch, tail_scratch = rest[9 : 9 + extra], rest[9 + extra :]
        here = place()

        def main(phase, piece):
            if phase > 0:
                scatter_phase(phase, piece, here, early_hbm.at[0], sums_ref, *scratch)
                return

            @pl.when(piece < BACK_BEFORE)
            def _():
                scatter_phase(phase, piece, here, early_hbm.at[FEED_SUMS + piece], sums_ref, *scratch)

            @pl.when(piece >= BACK_BEFORE)
            def _():
                scatter_phase(phase, piece, here, parts_hbm.at[piece - BACK_BEFORE], sums_ref, *scratch)

        def tail(phase, piece):
            if phase > 0:
                scatter_phase(phase, piece, here, small_ref, tail_ref, *tail_scratch)
                return
            scatter_phase(phase, GROUPS, here, small_ref, tail_ref, *tail_scratch)

        def tail_start(which):
            mine = slice(which * SMALL, (which + 1) * SMALL)
            scatter_phase(0, which, here, staged_ref.at[:, :, :, :, mine], tail_ref, *tail_scratch)

        def travel(slot):
            run_slot(slot, BACK_SCATTER, main)
            run_slot(slot, TAIL_SCATTER, tail)

        def point(at):
            travel(2 * step + at)
    else:
        point = lambda at: None
    keep = lambda: pltpu.make_async_copy(staged_ref, parts_hbm.at[group], sem)
    lanes = pl.ds(pl.multiple_of(seq * LENGTH, LENGTH), LENGTH)

    def hidden_terms():
        hidden = x_ref[...].astype(F32)
        scale = lax.rsqrt(jnp.mean(hidden * hidden, axis=1, keepdims=True) + EPS)
        return hidden, scale

    load_weights = lambda: pltpu.make_async_copy(weights_hbm.at[0:GROUPS], wg_ref, weight_sem)

    @pl.when(step == 0)
    def _():
        load_weights().start()

    if fast:

        @pl.when(step == 0)
        def _():
            greet(here)

    @pl.when(group == 0)
    def _():
        hidden, scale = hidden_terms()
        flipped_ref[:, lanes] = (hidden * scale * gains_ref[0:1, :]).astype(BF16).T

    @pl.when((seq == 0) & (group < GROUPS))
    def _():
        band_ref[...] = jnp.zeros_like(band_ref)

    def one_head(head):
        at = head * HEAD_DIM
        rows = lambda which: qkv_ref[0, 0, which * GROUP_ROWS + at : which * GROUP_ROWS + at + HEAD_DIM, :]
        grads = dmix_ref[0, 0, at : at + HEAD_DIM, :].astype(F32) * inv_ref[0, 0, head]
        grads = grads.astype(BF16)
        delta = jnp.sum(grads.astype(F32) * mix_ref[0, 0, at : at + HEAD_DIM, :].astype(F32), axis=0, keepdims=True)
        grad_prob = dot_tn(rows(2), grads)
        for column in range(BLOCKS):
            mine = span(column, column + 1)
            for row in range(BLOCKS):
                seen = span(row, row + 1)
                value = p_ref[0, 0, head, seen, mine].astype(F32) * (grad_prob[seen, mine] - delta[:, mine])
                band_ref[head, span(row - column + BLOCKS - 1, row - column + BLOCKS), :] += value
                ds_ref[head % 2, seen, mine] = value.astype(BF16)
        scores = ds_ref[head % 2]
        grads_ref[group, at : at + HEAD_DIM, lanes] = dot(rows(1), scores).astype(BF16)
        grads_ref[group, GROUP_ROWS + at : GROUP_ROWS + at + HEAD_DIM, lanes] = dot_nt(rows(0), scores).astype(BF16)
        grads_ref[group, 2 * GROUP_ROWS + at : 2 * GROUP_ROWS + at + HEAD_DIM, lanes] = dot_nt(grads, p_ref[0, 0, head]).astype(BF16)

    point(0)

    @pl.when(group < GROUPS)
    def _():
        one_head(0)
        one_head(1)

    @pl.when(group < GROUPS)
    def _():
        point(1)

    @pl.when(group < GROUPS)
    def _():
        one_head(2)
        one_head(3)

    @pl.when((seq == seqs - 1) & (group < GROUPS))
    def _():
        for first in range(0, width, 256):
            value = dot_nt(flipped_ref[...], grads_ref[group, first : first + 256, :]).astype(BF16)
            for owner in range(OWNERS):
                z, x, core = owner // 4, owner // 2 % 2, owner % 2
                staged_ref[z, x, core, :, first : first + 256] = value[SHARE * owner : SHARE * (owner + 1), :]
        last_fast = fast & (group == GROUPS - 1)

        @pl.when(jnp.logical_not(last_fast))
        def _():
            keep().start()

        if fast:

            @pl.when(last_fast)
            def _():
                for which in range(3):
                    tail_start(which)

        for head in range(GROUP):
            turned = band_ref[head].T
            total = jnp.zeros((8, OFFSETS), F32)
            for some in range(BLOCK // 8):
                wide = jnp.concatenate([turned[8 * some : 8 * some + 8, :], jnp.zeros((8, BLOCK), F32)], axis=1)
                total = total + pltpu.roll(wide, BLOCK - 8 * some, 1)
            line = iota((8, OFFSETS), 0)
            moved = total
            for row in range(1, 8):
                moved = jnp.where(line == row, pltpu.roll(total, OFFSETS - row, 1), moved)
            diag_ref[pl.ds(group * GROUP + head, 1)] = jnp.sum(moved, axis=0, keepdims=True)[None]
        @pl.when(jnp.logical_not(last_fast))
        def _():
            keep().wait()

    @pl.when((seq == seqs - 1) & (group == GROUPS - 1))
    def _():
        heads, buckets = table_places()
        onehot = (bucket_of(iota((OFFSETS, 1), 0) - BLOCKS * BLOCK) == buckets).astype(F32).astype(BF16)
        row = iota((16, width), 0)
        sums = jnp.concatenate([diag_ref[head] for head in range(HEADS)] + [jnp.zeros((16 - HEADS, OFFSETS), F32)], axis=0)
        high = sums.astype(BF16)
        low = (sums - high.astype(F32)).astype(BF16)
        entries = dot(high, onehot) + dot(low, onehot)
        entries = jnp.sum(jnp.where((row == heads) & (buckets >= 0), entries, 0.0), axis=0, keepdims=True)
        column = jnp.broadcast_to(entries, (BLOCK, width)).T.astype(BF16)
        for owner in range(OWNERS):
            z, x, core = owner // 4, owner // 2 % 2, owner % 2
            mine = column[SHARE * owner : SHARE * (owner + 1), :]
            small_ref[z, x, core, :, 0:BLOCK] = mine
            small_ref[z, x, core, :, BLOCK:SMALL] = mine

    @pl.when((group == GROUPS) & (seq == 0))
    def _():
        load_weights().wait()

    @pl.when(group == GROUPS)
    def _():
        hidden, scale = hidden_terms()
        flat = wg_ref[...].reshape(GROUPS, width, width)
        cotangent = sum(dot(flat[one], grads_ref[one, :, lanes]) for one in range(GROUPS)).T
        scaled = cotangent * gains_ref[0:1, :]
        unit = hidden * scale
        inner = jnp.mean(scaled * unit, axis=1, keepdims=True)
        ig_ref[...] = (gm_ref[...].astype(F32) + scale * (scaled - unit * inner)).astype(BF16)

    @pl.when(group == GROUPS)
    def _():
        point(1)

    if fast:

        @pl.when(step == (GROUPS + 1) * seqs - 1)
        def _():
            run_rest((2 * GROUPS + 2) * (flipped_ref.shape[1] // LENGTH), [BACK_SCATTER, TAIL_SCATTER], travel)


def back(x, gm, gains, weights, qkv, p, inv, mix, dmix, early, fast):
    tokens, width = x.shape
    seqs = tokens // LENGTH
    piece = (DEPTH, WIDE, CORES, SHARE, width)
    last = GROUPS - 1
    group_at = lambda g: jnp.minimum(g, last)
    seq_at = lambda g, s: jnp.where(g <= last, s, seqs - 1)
    four = lambda rows: pl.BlockSpec((1, 1, rows, LENGTH), lambda g, s: (group_at(g), seq_at(g, s), 0, 0))
    x_rows = pl.BlockSpec((LENGTH, width), lambda g, s: (jnp.where((g == 0) | (g == GROUPS), s, 0), 0))
    end_rows = pl.BlockSpec((LENGTH, width), lambda g, s: (jnp.where(g == GROUPS, s, 0), 0))
    out_specs = [end_rows, ANY, whole((DEPTH, WIDE, CORES, SHARE, SMALL))]
    out_shape = [
        jax.ShapeDtypeStruct((tokens, width), BF16), jax.ShapeDtypeStruct((GROUPS, *piece), BF16),
        jax.ShapeDtypeStruct((DEPTH, WIDE, CORES, SHARE, SMALL), BF16),
    ]
    scratch = [
        pltpu.VMEM((GROUP, BAND, BLOCK), F32), pltpu.VMEM((width, tokens), BF16), pltpu.VMEM((GROUPS, width, tokens), BF16),
        pltpu.VMEM((GROUPS, *piece), BF16), pltpu.VMEM((HEADS, 1, OFFSETS), F32), pltpu.VMEM(piece, BF16),
        pltpu.VMEM((2, LENGTH, LENGTH), BF16), pltpu.SemaphoreType.DMA,
        pltpu.SemaphoreType.DMA,
    ]
    kernel = partial(back_kernel, fast=fast)
    if fast:
        sums = BACK_SUMS
        out_specs += [whole((sums, SHARE, width)), whole((TAIL_SUMS, SHARE, SMALL))]
        out_shape += [jax.ShapeDtypeStruct((sums, SHARE, width), F32), jax.ShapeDtypeStruct((TAIL_SUMS, SHARE, SMALL), F32)]
        scratch += scatter_scratch(sums, SHARE, width) + scatter_scratch(TAIL_SUMS, SHARE, SMALL, TAIL_SUMS)
    return pl.pallas_call(
        kernel,
        name="back",
        grid=(GROUPS + 1, seqs),
        in_specs=[
            x_rows, end_rows, whole((8, width)),
            ANY, four(width),
            pl.BlockSpec((1, 1, GROUP, LENGTH, LENGTH), lambda g, s: (group_at(g), seq_at(g, s), 0, 0, 0)),
            pl.BlockSpec((1, 1, GROUP, 1, LENGTH), lambda g, s: (group_at(g), seq_at(g, s), 0, 0, 0)),
            four(GROUP_ROWS), four(GROUP_ROWS), ANY,
        ],
        out_specs=out_specs,
        out_shape=out_shape,
        scratch_shapes=scratch,
        compiler_params=pltpu.CompilerParams(
            vmem_limit_bytes=VMEM_LIMIT, collective_id=3 if fast else None, has_side_effects=fast
        ),
    )(x, gm, gains, weights, qkv, p, inv, mix, dmix, early)


def finish_kernel(
    out_ref, ig_ref, early_ref, late_ref, tail_ref, wq_ref, wk_ref, wv_ref, win_ref, gains_ref,
    output_ref, input_grad_ref, gq_ref, gk_ref, gv_ref, go_ref, gin_ref, gout_ref, gains_out_ref, table_ref,
):
    output_ref[...] = out_ref[...]
    input_grad_ref[...] = ig_ref[...]
    step = pl.program_id(0)

    @pl.when(step == 0)
    def _():
        for which, target in enumerate((gq_ref, gk_ref, gv_ref)):
            mine = slice(which * GROUP_ROWS, (which + 1) * GROUP_ROWS)
            for group in range(GROUPS):
                value = tail_ref[which] if group == GROUPS - 1 else late_ref[BACK_BEFORE + group, :, mine]
                target[:, group * GROUP_ROWS : (group + 1) * GROUP_ROWS] = value
        go_ref[...] = late_ref[2 * PARTS - FEED_SUMS]

    @pl.when(step == 1)
    def _():
        for part in range(PARTS):
            piece = 2 * part + 1
            gout_ref[part * SHARE : (part + 1) * SHARE, :] = (
                early_ref[piece] if piece < FEED_SUMS else late_ref[piece - FEED_SUMS]
            )

    @pl.when(step == 2)
    def _():
        for part in range(PARTS):
            piece = 2 * part
            value = early_ref[piece] if piece < FEED_SUMS else late_ref[piece - FEED_SUMS]
            for owner in range(OWNERS):
                at = (owner * PARTS + part) * SHARE
                gin_ref[:, at : at + SHARE] = value[:, owner * SHARE : (owner + 1) * SHARE]

    @pl.when(step == pl.num_programs(0) - 1)
    def _():
        def weigh(weight_ref, grad_ref):
            return jnp.sum(weight_ref[...].astype(F32) * grad_ref[...], axis=1, keepdims=True)

        first = weigh(wq_ref, gq_ref) + weigh(wk_ref, gk_ref) + weigh(wv_ref, gv_ref)
        second = weigh(win_ref, gin_ref)
        column = iota((SHARE, BLOCK), 1)
        lines = jnp.where(column == 0, first, jnp.where(column == 1, second, tail_ref[GROUPS, :, 0:BLOCK])).T
        gains_out_ref[...] = lines[0:2, 0:SHARE] / gains_ref[0:2, 0:SHARE].astype(F32)
        table_ref[...] = lines[2:3, 0:TABLE_SHARE]


def finish(out, ig, early, late, tail, wq, wk, wv, win, gains):
    tokens, width = out.shape
    ff = win.shape[1]
    rows = pl.BlockSpec((LENGTH, width), lambda s: (s, 0))
    low = jax.ShapeDtypeStruct((tokens, width), BF16)
    square = whole((SHARE, width))
    table = lambda *shape: jax.ShapeDtypeStruct(shape, F32)
    return pl.pallas_call(
        finish_kernel,
        name="finish",
        grid=(tokens // LENGTH,),
        in_specs=[
            rows, rows, whole(early.shape), whole(late.shape), whole(tail.shape), square, square, square, whole((SHARE, ff)),
            whole(gains.shape),
        ],
        out_specs=[
            rows, rows, square, square, square, square, whole((SHARE, ff)), whole((ff // OWNERS, width)), whole((2, SHARE)),
            whole((1, TABLE_SHARE)),
        ],
        out_shape=[
            low, low, table(SHARE, width), table(SHARE, width), table(SHARE, width), table(SHARE, width), table(SHARE, ff),
            table(ff // OWNERS, width), table(2, SHARE), table(1, TABLE_SHARE),
        ],
        compiler_params=pltpu.CompilerParams(vmem_limit_bytes=VMEM_LIMIT),
    )(out, ig, early, late, tail, wq, wk, wv, win, gains)


def ordered(rows, w_query, w_key, w_value, w_output, w_in, w_out):
    width = w_query.shape[1]
    groups = [
        jnp.concatenate([one[:, at * GROUP_ROWS : (at + 1) * GROUP_ROWS] for one in (w_query, w_key, w_value)], axis=1)
        for at in range(GROUPS)
    ]
    inner = w_in.reshape(rows, OWNERS, PARTS, SHARE).transpose(2, 0, 1, 3).reshape(PARTS, rows, width)
    outer = w_out.reshape(-1, PARTS, SHARE, width).transpose(1, 0, 2, 3).reshape(PARTS, rows, width)
    parts = [one for at in range(PARTS) for one in (inner[at], outer[at])]
    return jnp.stack(groups + [w_output] + parts)


def small_of(gain_attn, gain_ffn, rel_table):
    lines = [one.reshape(-1, 1, share) for one, share in ((gain_attn, SHARE), (gain_ffn, SHARE), (rel_table, TABLE_SHARE))]
    padded = [jnp.pad(one, ((0, 0), (0, 0), (0, BLOCK - one.shape[2]))) for one in lines]
    return jnp.pad(jnp.concatenate(padded, axis=1), ((0, 0), (0, 13), (0, 0)))


def shards(
    hidden_in, out_grad, pooled_gradient, gain_attn, w_query, w_key, w_value, w_output, rel_table, gain_ffn, w_in, w_out,
    pair_flags, instruction_mask, *, fast,
):
    width = hidden_in.shape[1]
    own = (w_query, w_key, w_value, w_output, w_in, w_out)
    if fast:
        shares = arrange(*own)
        small = small_of(gain_attn, gain_ffn, rel_table)[0]
    else:
        gather = lambda one: lax.all_gather(one, "fsdp", axis=0, tiled=True)
        shares = ordered(width, *map(gather, own)).reshape(-1, DEPTH, WIDE, CORES, SHARE, width)
        small = small_of(*map(gather, (gain_attn, gain_ffn, rel_table)))
    flags = pair_flags.reshape(-1, 1, LENGTH)
    instr = instruction_mask.reshape(-1, 1, LENGTH)
    qkv, p, inv, mix, mid, n2, bg, gains, *rest = attend(
        hidden_in, out_grad, pooled_gradient, flags, instr, shares, small, fast
    )
    early = rest[0] if fast else shares
    output, pooled, gm, dmix, parts, *rest = feed(
        n2, bg, mid, flags, instr, gains, mix, early, shares, fast
    )
    early_sums = rest
    input_grad, group_parts, small_parts, *rest = back(hidden_in, gm, gains, early, qkv, p, inv, mix, dmix, parts, fast)
    if fast:
        output, input_grad, *grads, gains, table = finish(
            output, input_grad, early_sums[0], *rest, w_query, w_key, w_value, w_in, small
        )
        return (output, pooled, input_grad, gains[0], *grads[:4], table[0], gains[1], *grads[4:])
    sums = jnp.concatenate([parts, group_parts]).reshape(-1, width, width)
    table = small_parts.reshape(OWNERS, SHARE, SMALL)[:, :TABLE_SHARE, 0].reshape(-1)
    rows = width
    groups = [sums[2 * PARTS + 1 + at] for at in range(GROUPS)]
    grad_query, grad_key, grad_value = (
        jnp.concatenate([one[:, at * GROUP_ROWS : (at + 1) * GROUP_ROWS] for one in groups], axis=1) for at in range(3)
    )
    grad_output = sums[2 * PARTS]
    grad_in = sums[0 : 2 * PARTS : 2].reshape(PARTS, rows, OWNERS, SHARE).transpose(1, 2, 0, 3).reshape(rows, -1)
    grad_out = sums[1 : 2 * PARTS : 2].reshape(PARTS, -1, SHARE, width).transpose(1, 0, 2, 3).reshape(-1, width)
    scatter = lambda one: lax.psum(lax.psum_scatter(one, "fsdp", scatter_dimension=0, tiled=True), "grp").astype(F32)
    grad_query, grad_key, grad_value, grad_output, grad_in, grad_out, table = map(
        scatter, (grad_query, grad_key, grad_value, grad_output, grad_in, grad_out, table)
    )
    weigh = lambda weight, grad: jnp.sum(weight.astype(F32) * grad, axis=1)
    grad_gain = weigh(w_query, grad_query) + weigh(w_key, grad_key) + weigh(w_value, grad_value)
    return (
        output, pooled, input_grad, grad_gain / gain_attn.astype(F32),
        grad_query, grad_key, grad_value, grad_output, table.astype(F32),
        weigh(w_in, grad_in) / gain_ffn.astype(F32), grad_in, grad_out,
    )


def solution(mesh):
    tokens, square, line = P(("grp", "fsdp"), None), P("fsdp", None), P("fsdp")
    cube, flat = P(("grp", "fsdp"), None, None), P(("grp", "fsdp"))
    fast = mesh.shape["fsdp"] == OWNERS and mesh.shape["grp"] == 2
    return jax.shard_map(
        partial(shards, fast=fast),
        mesh=mesh,
        in_specs=(tokens, tokens, cube, line, square, square, square, square, line, line, square, square, flat, flat),
        out_specs=(tokens, cube, tokens, line, square, square, square, square, line, line, square, square),
        check_vma=False,
    )
```

```python
from functools import partial

import jax
import jax.numpy as jnp
from jax import lax
from jax.experimental import pallas as pl
from jax.experimental.pallas import tpu as pltpu
from jax.sharding import PartitionSpec as P

HEADS = 12
HEAD_DIM = 64
BUCKETS = 32
LENGTH = 512
BLOCK = 128
BLOCKS = LENGTH // BLOCK
BAND_BLOCKS = 2 * BLOCKS - 1
BAND = BAND_BLOCKS * BLOCK
OFFSETS = BAND + BLOCK
GROUPS = 3
GROUP = HEADS // GROUPS
GROUP_ROWS = GROUP * HEAD_DIM
OWNERS, PARTS, SHARE = 16, 4, 48
TABLE_SHARE = HEADS * BUCKETS // OWNERS
SMALL = 256
EPS = 1e-06
NEG = -1e30
LIMITS = (12, 16, 23, 32, 46, 64, 91)
ROOT = 0.7978845608028654
CUBE = 0.044715
F32 = jnp.float32
BF16 = jnp.bfloat16
ANY = pl.BlockSpec(memory_space=pl.ANY)
VMEM_LIMIT = 63 * 1024 * 1024


def bucket_of(offset):
    distance = jnp.abs(offset)
    far_bucket = jnp.full(offset.shape, 8, jnp.int32)
    for threshold in LIMITS:
        far_bucket = far_bucket + (distance >= threshold).astype(jnp.int32)
    near_bucket = jnp.where(distance < 8, distance, far_bucket)
    return near_bucket + BUCKETS // 2 * (offset > 0).astype(jnp.int32)


def dot(a, b):
    return lax.dot_general(a, b, (((1,), (0,)), ((), ())), preferred_element_type=F32)


def dot_nt(a, b):
    return lax.dot_general(a, b, (((1,), (1,)), ((), ())), preferred_element_type=F32)


def dot_tn(a, b):
    return lax.dot_general(a, b, (((0,), (0,)), ((), ())), preferred_element_type=F32)


def dot_tt(a, b):
    return lax.dot_general(a, b, (((0,), (1,)), ((), ())), preferred_element_type=F32)


def iota(shape, axis):
    return lax.broadcasted_iota(jnp.int32, shape, axis)


def whole(shape):
    zeros = (0,) * len(shape)
    return pl.BlockSpec(shape, lambda *_: zeros, pipeline_mode=pl.Buffered(1))


def span(first, last):
    return slice(first * BLOCK, last * BLOCK)


def pool_terms(flags, instruction):
    kept = (instruction == 0).astype(F32)
    chosen = [kept * (flags == part).astype(F32) for part in range(2)]
    counts = [jnp.sum(one, axis=1, keepdims=True) for one in chosen]
    return chosen, counts


def pool_gradient(chosen, counts, pooled_grad):
    row = iota((16, LENGTH), 0)
    picks = jnp.where(row % 2 == 0, chosen[0], chosen[1])
    picks = jnp.where(row < 6, picks, 0.0).astype(BF16)
    scaled = [pooled_grad[part : part + 1, :] / counts[part] for part in range(2)]
    line = iota((16, pooled_grad.shape[1]), 0)
    both = jnp.where(line % 2 == 0, scaled[0], scaled[1])
    high = both.astype(BF16).astype(F32)
    rest = both - high
    middle = rest.astype(BF16).astype(F32)
    low = rest - middle
    parts = jnp.where(line < 2, high, jnp.where(line < 4, middle, jnp.where(line < 6, low, 0.0)))
    return dot_tn(picks, parts.astype(BF16))


def norm_back(value, gain, cotangent):
    scale = lax.rsqrt(jnp.mean(value * value, axis=1, keepdims=True) + EPS)
    scaled = cotangent * gain
    unit = value * scale
    inner = jnp.mean(scaled * unit, axis=1, keepdims=True)
    return scale * (scaled - unit * inner), jnp.sum(cotangent * unit, axis=0, keepdims=True)


def owners_of():
    at = iota((1, OWNERS * SHARE), 1)
    owner = sum((at >= SHARE * one).astype(jnp.int32) for one in range(1, OWNERS))
    return owner, at - SHARE * owner


def table_places():
    owner, inside = owners_of()
    entry = owner * TABLE_SHARE + inside
    bucket = sum((entry >= HEADS * one).astype(jnp.int32) for one in range(1, BUCKETS))
    return entry - HEADS * bucket, jnp.where(inside < TABLE_SHARE, bucket, -1)


DEPTH, WIDE, CORES = 4, 2, 2
MESH_ID = pl.DeviceIdType.MESH


def place():
    grp, at = lax.axis_index("grp"), lax.axis_index("fsdp")
    z, x, core = lax.div(at, WIDE * CORES), lax.rem(lax.div(at, CORES), WIDE), lax.rem(at, CORES)

    def device(grp, z, x, core):
        return (grp, z * (WIDE * CORES) + x * CORES + core)

    return dict(
        at=at, y=grp, z=z, x=x, core=core,
        over_y=device(1 - grp, z, x, core),
        over_x=device(grp, z, 1 - x, core),
        over_core=device(grp, z, x, 1 - core),
        over_z=[device(grp, lax.rem(z + one, DEPTH), x, core) for one in range(1, DEPTH)],
        ahead=[lax.rem(z + one, DEPTH) for one in range(1, DEPTH)],
        behind=[lax.rem(z + DEPTH - one, DEPTH) for one in range(1, DEPTH)],
    )


def greet(here):
    barrier = pltpu.get_barrier_semaphore()
    for device in (here["over_y"], here["over_x"], here["over_core"], *here["over_z"]):
        pl.semaphore_signal(barrier, inc=1, device_id=device, device_id_type=MESH_ID)
    pl.semaphore_wait(barrier, DEPTH + 2)


def others(here):
    at = here["at"]
    for one in range(1, OWNERS):
        yield one, (here["y"], lax.rem(at + one, OWNERS)), lax.rem(at + OWNERS - one, OWNERS)


def greet_all(here):
    barrier = pltpu.get_barrier_semaphore()
    pl.semaphore_signal(barrier, inc=1, device_id=here["over_y"], device_id_type=MESH_ID)
    for _, device, _ in others(here):
        pl.semaphore_signal(barrier, inc=1, device_id=device, device_id_type=MESH_ID)
    pl.semaphore_wait(barrier, OWNERS)


def gather_phase(phase, sem, here, share_ref, whole_ref, sent, got, own_sem, shared=False):
    z, x, core = here["z"], here["x"], here["core"]
    every = slice(None)
    half = share_ref.shape[-1] // 2
    lanes = pl.ds(pl.multiple_of(here["y"] * half, half), half) if shared else every
    other = pl.ds(pl.multiple_of((1 - here["y"]) * half, half), half) if shared else every
    mine = share_ref.at[:, lanes] if shared else share_ref

    def copy(source, where, channel, device):
        return pltpu.make_async_remote_copy(
            src_ref=source, dst_ref=whole_ref.at[where], send_sem=sent.at[channel, sem], recv_sem=got.at[channel, sem],
            device_id=device, device_id_type=MESH_ID,
        )

    def same(where, channel, device):
        return copy(whole_ref.at[where], where, channel, device)

    own = lambda: pltpu.make_async_copy(mine, whole_ref.at[z, x, core, every, lanes], own_sem.at[sem])
    line_out = lambda one: copy(mine, (z, x, core, every, lanes), one, here["over_z"][one])
    line_in = lambda one: copy(mine, (here["behind"][one], x, core, every, lanes), one, here["over_z"][one])
    side_out = lambda: same((every, x, core, every, lanes), 3, here["over_x"])
    side_in = lambda: same((every, 1 - x, core, every, lanes), 3, here["over_x"])
    group_out = lambda: same((every, every, core, every, lanes), 5, here["over_y"])
    group_in = lambda: same((every, every, core, every, other), 5, here["over_y"])
    core_out = lambda: same((every, every, core), 4, here["over_core"])
    core_in = lambda: same((every, every, 1 - core), 4, here["over_core"])
    if phase == 0:
        own().start()
        for one in range(DEPTH - 1):
            line_out(one).start()
    elif phase == 1:
        own().wait()
        for one in range(DEPTH - 1):
            line_in(one).wait_recv()
        side_out().start()
    elif phase == 2:
        side_in().wait_recv()
        group_out().start()
    elif phase == 3:
        if shared:
            group_in().wait_recv()
        else:
            side_in().wait_recv()
        core_out().start()
    else:
        for one in range(DEPTH - 1):
            line_out(one).wait_send()
        side_out().wait_send()
        if shared:
            group_out().wait_send()
        core_out().wait_send()
        core_in().wait_recv()


def scatter_phase(phase, piece, here, part_ref, out_ref, own, fromc, fromx, fromz, last, sent, got, own_sem):
    z, x, core = here["z"], here["x"], here["core"]
    slot = lax.rem(piece, own.shape[0])

    def remote(source, target, channel, device):
        return pltpu.make_async_remote_copy(
            src_ref=source, dst_ref=target, send_sem=sent.at[channel, piece], recv_sem=got.at[channel, piece],
            device_id=device, device_id_type=MESH_ID,
        )

    total = fromc.at[piece]
    over_core = lambda: remote(part_ref.at[:, :, 1 - core], total, 0, here["over_core"])
    load = lambda: pltpu.make_async_copy(part_ref.at[:, :, core], own.at[slot], own_sem.at[slot])
    over_x = lambda: remote(fromc.at[piece, :, 1 - x], fromx.at[piece], 1, here["over_x"])
    line_out = lambda one: remote(fromc.at[piece, here["ahead"][one], x], fromz.at[piece, z], 2 + one, here["over_z"][one])
    line_in = lambda one: remote(
        fromc.at[piece, z, x], fromz.at[piece, here["behind"][one]], 2 + one, here["over_z"][one]
    )
    final = lambda: remote(fromc.at[piece, z, x], last.at[piece], 5, here["over_y"])

    if phase == 0:
        over_core().start()
        load().start()
    elif phase == 1:
        load().wait()
        over_core().wait()

        def one(at, _):
            for side in range(WIDE):
                fromc[piece, at, side] = own[slot, at, side] + fromc[piece, at, side]
            return 0

        lax.fori_loop(0, DEPTH, one, 0)
        over_x().start()
    elif phase == 2:
        over_x().wait()

        def one(at, _):
            fromc[piece, at, x] = fromc[piece, at, x] + fromx[piece, at]
            return 0

        lax.fori_loop(0, DEPTH, one, 0)
        for one in range(DEPTH - 1):
            line_out(one).start()
    elif phase == 3:
        mine = fromc[piece, z, x].astype(F32)
        for one in range(DEPTH - 1):
            line_in(one).wait_recv()
            mine = mine + fromz[piece, here["behind"][one]].astype(F32)
        fromc[piece, z, x] = mine.astype(BF16)
        final().start()
    else:
        for one in range(DEPTH - 1):
            line_out(one).wait_send()
        final().wait()
        out_ref[piece] = fromc[piece, z, x].astype(F32) + last[piece].astype(F32)


def run_slot(slot, table, act):
    for phase in reversed(range(max(map(len, table.values())))):
        due, found = False, 0
        for piece, slots in table.items():
            if slots[phase] is not None:
                now = slot == slots[phase]
                due, found = due | now, jnp.where(now, piece, found)
        if due is not False:

            @pl.when(due)
            def _(phase=phase, found=found):
                act(phase, found)


def run_rest(first, tables, travel):
    end = 1 + max(slot for table in tables for slots in table.values() for slot in slots if slot is not None)

    def one(slot, _):
        travel(slot)
        return 0

    if end > first:
        lax.fori_loop(first, end, one, 0)


def gather_sems(pieces):
    return [pltpu.SemaphoreType.DMA((6, pieces)), pltpu.SemaphoreType.DMA((6, pieces)), pltpu.SemaphoreType.DMA((pieces,))]


def scatter_scratch(pieces, rows, columns, places=2):
    return [
        pltpu.VMEM((places, DEPTH, WIDE, rows, columns), BF16),
        pltpu.VMEM((pieces, DEPTH, WIDE, rows, columns), BF16),
        pltpu.VMEM((pieces, DEPTH, rows, columns), BF16),
        pltpu.VMEM((pieces, DEPTH, rows, columns), BF16),
        pltpu.VMEM((pieces, rows, columns), BF16),
        pltpu.SemaphoreType.DMA((6, pieces)),
        pltpu.SemaphoreType.DMA((6, pieces)),
        pltpu.SemaphoreType.DMA((places,)),
    ]


ATTEND_PIECES, FEED_PIECES = 8, 4
ATTEND_DIRECT = {2: (0, 6, None, 12, 14), 3: (3, 9, None, 15, 17), 5: (9, 14, None, 20, 22), 7: (14, 19, None, 25, 26)}
ATTEND_SHARED = {1: (None, None, 0, 5, 7), 4: (7, 12, 16, 21, 23), 6: (12, 17, 21, 24, 25)}
FEED_DIRECT = {1: (1, 7, None, 12, 15), 3: (6, 12, None, 18, 20)}
FEED_SHARED = {0: (0, 4, 7, 11, 14), 2: (5, 8, 15, 19, 21)}
FEED_SUMS = 5
FEED_SCATTER = {0: (8, 13, 18, 24, 26), 1: (11, 15, 21, 26, 28), 2: (16, 18, 24, 31, 32), 3: (19, 21, 27, 32, 35), 4: (24, 26, 31, 37, 40)}
BACK_BEFORE, BACK_SUMS = 4, 6
BACK_SCATTER = {
    0: (0, 2, 7, 12, 15), 1: (3, 5, 10, 15, 18), 2: (6, 8, 13, 18, 21), 3: (9, 11, 16, 21, 24),
    4: (12, 14, 19, 24, 27), 5: (16, 18, 23, 27, 29),
}
TAIL_SUMS = 4
TAIL_SCATTER = {0: (None, 24, 26, 28, 30), 1: (None, 25, 27, 29, 31), 2: (None, 26, 28, 30, 32), 3: (24, 27, 29, 31, 33)}


def arrange_kernel(wq_ref, wk_ref, wv_ref, wo_ref, win_ref, wout_ref, shares_ref, line_ref):
    for group in range(GROUPS):
        mine = slice(group * GROUP_ROWS, (group + 1) * GROUP_ROWS)
        for which, one in enumerate((wq_ref, wk_ref, wv_ref)):
            shares_ref[group, :, which * GROUP_ROWS : (which + 1) * GROUP_ROWS] = one[:, mine]
    shares_ref[GROUPS] = wo_ref[...]
    for part in range(PARTS):
        for owner in range(OWNERS):
            at = (owner * PARTS + part) * SHARE
            line_ref[:, owner * SHARE : (owner + 1) * SHARE] = win_ref[:, at : at + SHARE].astype(F32)
        shares_ref[GROUPS + 1 + 2 * part] = line_ref[...].astype(BF16)
        shares_ref[GROUPS + 2 + 2 * part] = wout_ref[part * SHARE : (part + 1) * SHARE, :]


def arrange(*weights):
    width = weights[0].shape[1]
    return pl.pallas_call(
        arrange_kernel,
        name="arrange",
        out_shape=jax.ShapeDtypeStruct((GROUPS + 1 + 2 * PARTS, SHARE, width), BF16),
        scratch_shapes=[pltpu.VMEM((SHARE, width), F32)],
    )(*weights)


def attend_kernel(
    x_hbm, og_hbm, pg_ref, flags_ref, instr_ref, shares_hbm, small_hbm,
    qkv_ref, p_ref, inv_ref, mix_ref, mid_ref, n2_ref, bg_hbm, gains_ref, weights_hbm,
    x_ref, bg_ref, mixed_ref, band_ref, aux_ref, normed_ref, wg_ref, wo_ref, small_ref, table_ref, cur_ref, nxt_ref, sa_ref, sb_ref,
    sems, *comm, fast,
):
    group, seq = pl.program_id(0), pl.program_id(1)
    seqs = pl.num_programs(1)
    step = group * seqs + seq
    width = x_ref.shape[1]
    if fast:
        main_sems, first_sems, small_sent, small_got = comm[0:3], comm[3:6], comm[6], comm[7]
        here = place()

        def main(phase, piece, shared=False):
            gather_phase(phase, piece, here, shares_hbm.at[piece], weights_hbm.at[piece], *main_sems, shared=shared)

        def small(start):
            for one, device, source in others(here):
                copy = lambda where: pltpu.make_async_remote_copy(
                    src_ref=small_hbm, dst_ref=small_ref.at[where], send_sem=small_sent.at[one], recv_sem=small_got.at[one],
                    device_id=device, device_id_type=MESH_ID,
                )
                if start:
                    copy(here["at"]).start()
                else:
                    copy(source).wait_recv()
                    copy(here["at"]).wait_send()

        def first(phase, which):
            lanes = pl.ds(which * GROUP_ROWS, GROUP_ROWS)
            every = slice(None)
            gather_phase(
                phase, which, here, shares_hbm.at[0, :, lanes], weights_hbm.at[0, every, every, every, every, lanes], *first_sems
            )

        def travel(slot):
            run_slot(slot, ATTEND_DIRECT, main)
            run_slot(slot, ATTEND_SHARED, partial(main, shared=True))

        point = lambda at: travel(2 * step + at)
    else:
        point = lambda at: None
    small_own = small_ref.at[here["at"]] if fast else small_ref
    load_small = lambda: pltpu.make_async_copy(small_hbm, small_own, sems.at[0])
    load_hidden = lambda: pltpu.make_async_copy(x_hbm, x_ref, sems.at[3])
    load_grad = lambda: pltpu.make_async_copy(og_hbm, bg_ref, sems.at[4])
    keep_grad = lambda: pltpu.make_async_copy(bg_ref, bg_hbm, sems.at[4])
    load_group = lambda at: pltpu.make_async_copy(weights_hbm.at[at], wg_ref, sems.at[1])
    load_output = lambda: pltpu.make_async_copy(weights_hbm.at[GROUPS], wo_ref, sems.at[2])
    square = lambda ref: ref[...].reshape(width, width)

    def prepare(at):
        flags = flags_ref[at]
        chosen, counts = pool_terms(flags, instr_ref[at])
        rows = pl.ds(pl.multiple_of(at * LENGTH, LENGTH), LENGTH)
        bg_ref[rows, :] = (bg_ref[rows, :].astype(F32) + pool_gradient(chosen, counts, pg_ref[at])).astype(BF16)
        row = iota((16, LENGTH), 0)
        aux_ref[0, at] = jnp.where(row == 0, 1 - flags, jnp.where(row == 1, flags, 0)).astype(F32).astype(BF16)
        other = jnp.where(row == 0, flags, jnp.where(row == 1, 1 - flags, 0)).astype(F32) * NEG
        aux_ref[1, at] = other.astype(BF16)

    def normalize(at):
        rows = pl.ds(pl.multiple_of(at * LENGTH, LENGTH), LENGTH)
        hidden = x_ref[rows, :].astype(F32)
        scale = lax.rsqrt(jnp.mean(hidden * hidden, axis=1, keepdims=True) + EPS)
        normed_ref[at] = (hidden * scale * gains_ref[0:1, :]).astype(BF16)

    def every_seq(act):
        def one_seq(at, _):
            act(at)
            return 0

        lax.fori_loop(0, seqs, one_seq, 0)

    def project(at, target):
        target[...] = dot_tt(square(wg_ref), normed_ref[at]).astype(BF16)

    def part(source, which, head):
        first = which * GROUP_ROWS + head * HEAD_DIM
        return source[first : first + HEAD_DIM, :]

    def score(source, at_group, at, head, target):
        queries = jnp.concatenate([part(source, 0, head), aux_ref[0, at]], axis=0)
        keys = jnp.concatenate([part(source, 1, head), aux_ref[1, at]], axis=0)
        scores = dot_tn(keys, queries)
        for row in range(BLOCKS):
            for column in range(BLOCKS):
                bias = band_ref[at_group * GROUP + head, span(row - column + BLOCKS - 1, row - column + BLOCKS), :]
                target[span(row, row + 1), span(column, column + 1)] = scores[span(row, row + 1), span(column, column + 1)] + bias

    def soften(head, source):
        scores = source[...]
        exponent = jnp.exp(scores - jnp.max(scores, axis=0, keepdims=True)).astype(BF16)
        p_ref[0, 0, head] = exponent
        values = jnp.concatenate([part(cur_ref, 2, head), jnp.ones((16, LENGTH), BF16)], axis=0)
        mixed = dot(values, exponent)
        inverse = 1.0 / mixed[HEAD_DIM : HEAD_DIM + 1, :]
        inv_ref[0, 0, head] = inverse
        mixed = (mixed[0:HEAD_DIM, :] * inverse).astype(BF16)
        mix_ref[0, 0, head * HEAD_DIM : (head + 1) * HEAD_DIM, :] = mixed
        mixed_ref[seq, pl.ds(pl.multiple_of(group * GROUP_ROWS + head * HEAD_DIM, HEAD_DIM), HEAD_DIM), :] = mixed

    def read_small():
        owner, inside = owners_of()
        spread = (iota((BLOCK, width), 0) == inside).astype(F32).astype(BF16)
        shares = small_ref[...].astype(F32)

        def line(which):
            placed = dot(shares[:, which, :].astype(BF16), spread)
            return jnp.sum(jnp.where(iota((OWNERS, width), 0) == owner, placed, 0.0), axis=0, keepdims=True)

        row = iota((8, width), 0)
        gains_ref[...] = jnp.where(row == 0, line(0), line(1))
        table_row = line(2)
        heads, buckets = table_places()
        entries = jnp.where((iota((16, width), 0) == heads) & (buckets >= 0), table_row, 0.0).astype(BF16)
        onehot = (bucket_of(iota((OFFSETS, 1), 0) - BLOCKS * BLOCK) == buckets).astype(F32).astype(BF16)
        table_ref[...] = dot_nt(entries, onehot)

    def make_bands(at_group):
        def one_head(head, _):
            table = table_ref[...]
            line = jnp.sum(jnp.where(iota(table.shape, 0) == head, table, 0.0), axis=0, keepdims=True)
            turned = pltpu.roll(jnp.broadcast_to(line, (BLOCK, OFFSETS)), 0, 1, stride=1, stride_axis=0)
            band_ref[head] = turned[:, BLOCK:].T
            return 0

        lax.fori_loop(at_group * GROUP, (at_group + 1) * GROUP, one_head, 0)

    @pl.when(step == 0)
    def _():
        load_grad().start()
        load_hidden().start()
        load_small().start()
        if fast:
            greet_all(here)
            small(True)
            for which in range(3):
                first(0, which)
        load_grad().wait()
        every_seq(prepare)
        keep_grad().start()
        load_hidden().wait()
        load_small().wait()
        if fast:
            small(False)
            first(1, 0)
            main(0, 1, shared=True)
            read_small()
            first(1, 1)
            normalize(0)
            normalize(1)
            first(1, 2)
            normalize(2)
            normalize(3)
            first(3, 0)
            make_bands(0)
            first(3, 1)
            main(1, 1, shared=True)
            make_bands(1)
            first(3, 2)
            make_bands(2)
            for which in range(3):
                first(4, which)
        else:
            read_small()
            every_seq(normalize)
            for one in range(GROUPS):
                make_bands(one)
        load_group(0).start()
        load_group(0).wait()
        project(0, nxt_ref)
        score(nxt_ref, 0, 0, 0, sa_ref)

    last_seq = seq == seqs - 1
    more = step + 1 < GROUPS * seqs
    cur_ref[...] = nxt_ref[...]

    next_seq = jnp.where(last_seq, 0, seq + 1)
    next_group = jnp.where(last_seq, jnp.minimum(group + 1, GROUPS - 1), group)
    point(0)
    qkv_ref[0, 0] = cur_ref[...]
    score(cur_ref, group, seq, 1, sb_ref)
    soften(0, sa_ref)
    score(cur_ref, group, seq, 2, sa_ref)
    soften(1, sb_ref)
    point(1)
    score(cur_ref, group, seq, 3, sb_ref)
    soften(2, sa_ref)

    @pl.when(last_seq & more)
    def _():
        load_group(group + 1).start()
        load_group(group + 1).wait()

    project(next_seq, nxt_ref)
    score(nxt_ref, next_group, next_seq, 0, sa_ref)
    soften(3, sb_ref)

    @pl.when((seq == 0) & (group == GROUPS - 1))
    def _():
        load_output().start()
        load_output().wait()

    @pl.when(group == GROUPS - 1)
    def _():
        rows = pl.ds(pl.multiple_of(seq * LENGTH, LENGTH), LENGTH)
        middle = x_ref[rows, :].astype(F32) + dot_tn(mixed_ref[seq], square(wo_ref))
        mid_ref[...] = middle
        scale = lax.rsqrt(jnp.mean(middle * middle, axis=1, keepdims=True) + EPS)
        n2_ref[...] = (middle * scale * gains_ref[1:2, :]).astype(BF16)

    @pl.when(step == GROUPS * seqs - 1)
    def _():
        keep_grad().wait()
        if fast:
            run_rest(2 * GROUPS * (x_ref.shape[0] // LENGTH), [ATTEND_DIRECT, ATTEND_SHARED], travel)


def attend(x, og, pg, flags, instr, shares, small, fast):
    tokens, width = x.shape
    seqs = tokens // LENGTH
    last_rows = pl.BlockSpec((LENGTH, width), lambda g, s: (jnp.where(g == GROUPS - 1, s, 0), 0))
    low = jax.ShapeDtypeStruct((tokens, width), BF16)
    out_specs = [
        pl.BlockSpec((1, 1, width, LENGTH), lambda g, s: (g, s, 0, 0)),
        pl.BlockSpec((1, 1, GROUP, LENGTH, LENGTH), lambda g, s: (g, s, 0, 0, 0)),
        pl.BlockSpec((1, 1, GROUP, 1, LENGTH), lambda g, s: (g, s, 0, 0, 0)),
        pl.BlockSpec((1, 1, GROUP_ROWS, LENGTH), lambda g, s: (g, s, 0, 0)), last_rows, last_rows, ANY, whole((8, width)),
    ]
    out_shape = [
        jax.ShapeDtypeStruct((GROUPS, seqs, width, LENGTH), BF16),
        jax.ShapeDtypeStruct((GROUPS, seqs, GROUP, LENGTH, LENGTH), BF16),
        jax.ShapeDtypeStruct((GROUPS, seqs, GROUP, 1, LENGTH), F32),
        jax.ShapeDtypeStruct((GROUPS, seqs, GROUP_ROWS, LENGTH), BF16),
        jax.ShapeDtypeStruct((tokens, width), F32), low, low, jax.ShapeDtypeStruct((8, width), F32),
    ]
    scratch = [
        pltpu.VMEM((tokens, width), BF16), pltpu.VMEM((tokens, width), BF16), pltpu.VMEM((seqs, width, LENGTH), BF16),
        pltpu.VMEM((HEADS, BAND, BLOCK), F32), pltpu.VMEM((2, seqs, 16, LENGTH), BF16),
        pltpu.VMEM((seqs, LENGTH, width), BF16), pltpu.VMEM((DEPTH, WIDE, CORES, SHARE, width), BF16),
        pltpu.VMEM((DEPTH, WIDE, CORES, SHARE, width), BF16), pltpu.VMEM((OWNERS, 16, BLOCK), BF16), pltpu.VMEM((16, OFFSETS), F32),
        pltpu.VMEM((width, LENGTH), BF16), pltpu.VMEM((width, LENGTH), BF16),
        pltpu.VMEM((LENGTH, LENGTH), F32), pltpu.VMEM((LENGTH, LENGTH), F32), pltpu.SemaphoreType.DMA((5,)),
    ]
    in_specs = [
        ANY, ANY, whole((seqs, 2, width)), whole((seqs, 1, LENGTH)), whole((seqs, 1, LENGTH)), ANY, ANY,
    ]
    if fast:
        kernel = partial(attend_kernel, fast=True)
        out_specs += [ANY]
        out_shape += [jax.ShapeDtypeStruct((ATTEND_PIECES, DEPTH, WIDE, CORES, SHARE, width), BF16)]
        scratch += gather_sems(ATTEND_PIECES) + gather_sems(3) + [pltpu.SemaphoreType.DMA((OWNERS,)), pltpu.SemaphoreType.DMA((OWNERS,))]
    else:

        def kernel(*refs):
            inputs, outputs, rest = refs[:7], refs[7:15], refs[15:]
            attend_kernel(*inputs, *outputs, inputs[5], *rest, fast=False)

    return pl.pallas_call(
        kernel,
        name="attend",
        grid=(GROUPS, seqs),
        in_specs=in_specs,
        out_specs=out_specs,
        out_shape=out_shape,
        scratch_shapes=scratch,
        compiler_params=pltpu.CompilerParams(
            vmem_limit_bytes=VMEM_LIMIT, collective_id=1 if fast else None, has_side_effects=fast
        ),
    )(x, og, pg, flags, instr, shares, small)


def feed_kernel(
    n2_hbm, bg_hbm, mid_hbm, flags_ref, instr_ref, gains_ref, mid_ref, mix_ref, early_hbm, late_hbm,
    out_ref, pooled_ref, gm_ref, dmix_ref, parts_hbm, *rest, fast,
):
    if fast:
        sums_ref, gathered_hbm = rest[0:2]
        rest = rest[2:]
    n2_ref, bg_ref, res_ref, dn2_ref, act_ref, dinner_ref, win_ref, wout_ref, wo_ref, dwo_ref, staged_ref, sems, block_sems = rest[:13]
    part, block = pl.program_id(0), pl.program_id(1)
    blocks = pl.num_programs(1)
    step = part * blocks + block
    width = res_ref.shape[1]
    rows = pl.ds(pl.multiple_of(block * LENGTH, LENGTH), LENGTH)
    if fast:
        sems_of, scratch = rest[13:16], rest[16:]
        here = place()

        def travel(slot):
            def bring(phase, piece, shared=False):
                share = late_hbm.at[ATTEND_PIECES + piece]
                gather_phase(phase, piece, here, share, gathered_hbm.at[piece], *sems_of, shared=shared)

            def add(phase, piece):
                scatter_phase(phase, piece, here, parts_hbm.at[piece], sums_ref, *scratch)

            run_slot(slot, FEED_DIRECT, bring)
            run_slot(slot, FEED_SHARED, partial(bring, shared=True))
            run_slot(slot, FEED_SCATTER, add)

        point = lambda at: travel(2 * step + at)
    else:
        point = lambda at: None
    square = lambda ref: ref[...].reshape(width, width)

    def weights(at, start):
        def both(source, first):
            for which, target in enumerate((win_ref, wout_ref)):
                slot = lax.rem(at, 2)
                copy = pltpu.make_async_copy(source.at[first + which], target.at[slot], sems.at[slot, which])
                copy.start() if start else copy.wait()

        if start:
            pl.when(at < PARTS // 2)(lambda: both(early_hbm, 4 + 2 * at))
            pl.when(at >= PARTS // 2)(lambda: both(gathered_hbm if fast else late_hbm, 2 * at + (-PARTS if fast else 4)))
        else:
            both(early_hbm, 4)


    def load_block(at, start):
        mine = pl.ds(pl.multiple_of(at * LENGTH, LENGTH), LENGTH)
        for which, (source, target) in enumerate(((n2_hbm, n2_ref), (bg_hbm, bg_ref), (mid_hbm, res_ref))):
            copy = pltpu.make_async_copy(source.at[mine], target.at[mine], block_sems.at[which, at])
            copy.start() if start else copy.wait()

    load_output = lambda: pltpu.make_async_copy(early_hbm.at[GROUPS], wo_ref, sems.at[1, 2])
    keep = lambda at, which: pltpu.make_async_copy(staged_ref.at[which], parts_hbm.at[2 * at + which], sems.at[which, 3])

    @pl.when(step == 0)
    def _():
        weights(0, True)
        for at in range(res_ref.shape[0] // LENGTH):
            load_block(at, True)
        load_output().start()
        if fast:
            greet(here)
        dwo_ref[...] = jnp.zeros_like(dwo_ref)

    @pl.when((part == PARTS) & (block == 0))
    def _():
        load_output().wait()

    @pl.when(part == 0)
    def _():
        dn2_ref[rows, :] = jnp.zeros((LENGTH, width), F32)
        load_block(block, False)

    @pl.when((part < PARTS) & (block == 0))
    def _():
        weights(part, False)

    @pl.when((part > 0) & (block == 0))
    def _():
        keep(part - 1, 0).wait()
        keep(part - 1, 1).wait()

    point(0)

    @pl.when(part < PARTS)
    def _():
        slot = lax.rem(part, 2)
        inner = dot(n2_ref[rows, :], square(win_ref.at[slot]))
        grad_active = dot_nt(bg_ref[rows, :], square(wout_ref.at[slot]))
        squared = inner * inner
        half = 0.5 * jnp.tanh(inner * (ROOT + (ROOT * CUBE) * squared)) + 0.5
        active = inner * half
        slope = half + active * (1.0 - half) * (2.0 * ROOT + (6.0 * ROOT * CUBE) * squared)
        active = active.astype(BF16)
        act_ref[rows, :] = active
        dinner = (grad_active * slope).astype(BF16)
        dinner_ref[rows, :] = dinner
        res_ref[rows, :] += dot(active, square(wout_ref.at[slot]))
        dn2_ref[rows, :] += dot_nt(dinner, square(win_ref.at[slot]))

    point(1)

    @pl.when((part < PARTS - 1) & (block == blocks - 1))
    def _():
        weights(part + 1, True)

    def stage(which, first, value):
        for owner in range(OWNERS):
            z, x, core = owner // 4, owner // 2 % 2, owner % 2
            staged_ref[which, z, x, core, :, first : first + 256] = value[SHARE * owner : SHARE * (owner + 1), :]

    @pl.when((part < PARTS) & (block == blocks - 1))
    def _():
        for first in range(0, width, 256):
            stage(0, first, dot_tn(n2_ref[...], dinner_ref[:, first : first + 256]).astype(BF16))
        keep(part, 0).start()
        for first in range(0, width, 256):
            stage(1, first, dot_tn(act_ref[...], bg_ref[:, first : first + 256]).astype(BF16))
        keep(part, 1).start()

    @pl.when(part == PARTS)
    def _():
        result = res_ref[rows, :]
        out_ref[...] = result.astype(BF16)
        chosen, counts = pool_terms(flags_ref[block], instr_ref[block])
        line = iota((8, LENGTH), 0)
        picks = jnp.where(line == 0, chosen[0], jnp.where(line == 1, chosen[1], 0.0)).astype(BF16)
        high = result.astype(BF16)
        low = (result - high.astype(F32)).astype(BF16)
        total = dot(picks, high) + dot(picks, low)
        total = total / jnp.where(iota((8, 1), 0) == 0, counts[0], counts[1])
        pooled_ref[block] = total[0:2, :]
        change, _ = norm_back(mid_ref[...], gains_ref[1:2, :], dn2_ref[rows, :])
        out_low = (bg_ref[rows, :].astype(F32) + change).astype(BF16)
        gm_ref[...] = out_low
        output = square(wo_ref)
        for group in range(GROUPS):
            mine = slice(group * GROUP_ROWS, (group + 1) * GROUP_ROWS)
            dmix_ref[group, 0] = dot_nt(output[mine, :], out_low).astype(BF16)
            dwo_ref[mine, :] += dot(mix_ref[group, 0], out_low)

    @pl.when(step == (PARTS + 1) * blocks - 1)
    def _():
        for first in range(0, width, 256):
            stage(0, first, dwo_ref[:, first : first + 256].astype(BF16))
        keep(PARTS, 0).start()
        if fast:
            run_rest(2 * (PARTS + 1) * (res_ref.shape[0] // LENGTH), [FEED_DIRECT, FEED_SHARED, FEED_SCATTER], travel)
        keep(PARTS, 0).wait()


def feed(n2, bg, mid, flags, instr, gains, mix, early, late, fast):
    tokens, width = n2.shape
    seqs = tokens // LENGTH
    rows = pl.BlockSpec((LENGTH, width), lambda c, m: (jnp.where(c == PARTS, m, 0), 0))
    heads = pl.BlockSpec((GROUPS, 1, GROUP_ROWS, LENGTH), lambda c, m: (0, jnp.where(c == PARTS, m, 0), 0, 0))
    piece = (DEPTH, WIDE, CORES, SHARE, width)
    sums = FEED_SUMS
    out_specs = [rows, whole((seqs, 2, width)), rows, heads, ANY]
    out_shape = [
        jax.ShapeDtypeStruct((tokens, width), BF16), jax.ShapeDtypeStruct((seqs, 2, width), F32),
        jax.ShapeDtypeStruct((tokens, width), BF16), jax.ShapeDtypeStruct((GROUPS, seqs, GROUP_ROWS, LENGTH), BF16),
        jax.ShapeDtypeStruct((2 * PARTS + 1, *piece), BF16),
    ]
    scratch = [
        pltpu.VMEM((tokens, width), BF16), pltpu.VMEM((tokens, width), BF16),
        pltpu.VMEM((tokens, width), F32), pltpu.VMEM((tokens, width), F32), pltpu.VMEM((tokens, width), BF16),
        pltpu.VMEM((tokens, width), BF16), pltpu.VMEM((2, *piece), BF16), pltpu.VMEM((2, *piece), BF16),
        pltpu.VMEM(piece, BF16), pltpu.VMEM((width, width), F32), pltpu.VMEM((2, *piece), BF16), pltpu.SemaphoreType.DMA((2, 4)),
        pltpu.SemaphoreType.DMA((3, seqs)),
    ]
    if fast:
        out_specs += [whole((sums, SHARE, width)), ANY]
        out_shape += [
            jax.ShapeDtypeStruct((sums, SHARE, width), F32), jax.ShapeDtypeStruct((FEED_PIECES, *piece), BF16)
        ]
        scratch += gather_sems(FEED_PIECES) + scatter_scratch(sums, SHARE, width)
    return pl.pallas_call(
        partial(feed_kernel, fast=fast),
        name="feed",
        grid=(PARTS + 1, seqs),
        in_specs=[
            ANY, ANY, ANY, whole((seqs, 1, LENGTH)), whole((seqs, 1, LENGTH)), whole((8, width)), rows, heads, ANY, ANY,
        ],
        out_specs=out_specs,
        out_shape=out_shape,
        scratch_shapes=scratch,
        compiler_params=pltpu.CompilerParams(
            vmem_limit_bytes=VMEM_LIMIT, collective_id=2 if fast else None, has_side_effects=fast
        ),
    )(n2, bg, mid, flags, instr, gains, mid, mix, early, late)


def back_kernel(
    x_ref, gm_ref, gains_ref, weights_hbm, qkv_ref, p_ref, inv_ref, mix_ref, dmix_ref, early_hbm,
    ig_ref, parts_hbm, small_ref, *rest, fast,
):
    if fast:
        sums_ref, tail_ref = rest[0:2]
        rest = rest[2:]
    band_ref, flipped_ref, grads_ref, wg_ref, diag_ref, staged_ref, ds_ref, sem, weight_sem = rest[:9]
    group, seq = pl.program_id(0), pl.program_id(1)
    seqs = pl.num_programs(1)
    step = group * seqs + seq
    width = x_ref.shape[1]
    if fast:
        extra = len(scatter_scratch(1, SHARE, width))
        scratch, tail_scratch = rest[9 : 9 + extra], rest[9 + extra :]
        here = place()

        def main(phase, piece):
            if phase > 0:
                scatter_phase(phase, piece, here, early_hbm.at[0], sums_ref, *scratch)
                return

            @pl.when(piece < BACK_BEFORE)
            def _():
                scatter_phase(phase, piece, here, early_hbm.at[FEED_SUMS + piece], sums_ref, *scratch)

            @pl.when(piece >= BACK_BEFORE)
            def _():
                scatter_phase(phase, piece, here, parts_hbm.at[piece - BACK_BEFORE], sums_ref, *scratch)

        def tail(phase, piece):
            if phase > 0:
                scatter_phase(phase, piece, here, small_ref, tail_ref, *tail_scratch)
                return
            scatter_phase(phase, GROUPS, here, small_ref, tail_ref, *tail_scratch)

        def tail_start(which):
            mine = slice(which * SMALL, (which + 1) * SMALL)
            scatter_phase(0, which, here, staged_ref.at[:, :, :, :, mine], tail_ref, *tail_scratch)

        def travel(slot):
            run_slot(slot, BACK_SCATTER, main)
            run_slot(slot, TAIL_SCATTER, tail)

        def point(at):
            travel(2 * step + at)
    else:
        point = lambda at: None
    keep = lambda: pltpu.make_async_copy(staged_ref, parts_hbm.at[group], sem)
    lanes = pl.ds(pl.multiple_of(seq * LENGTH, LENGTH), LENGTH)

    def hidden_terms():
        hidden = x_ref[...].astype(F32)
        scale = lax.rsqrt(jnp.mean(hidden * hidden, axis=1, keepdims=True) + EPS)
        return hidden, scale

    load_weights = lambda: pltpu.make_async_copy(weights_hbm.at[0:GROUPS], wg_ref, weight_sem)

    @pl.when(step == 0)
    def _():
        load_weights().start()

    if fast:

        @pl.when(step == 0)
        def _():
            greet(here)

    @pl.when(group == 0)
    def _():
        hidden, scale = hidden_terms()
        flipped_ref[:, lanes] = (hidden * scale * gains_ref[0:1, :]).astype(BF16).T

    @pl.when((seq == 0) & (group < GROUPS))
    def _():
        band_ref[...] = jnp.zeros_like(band_ref)

    def one_head(head):
        at = head * HEAD_DIM
        rows = lambda which: qkv_ref[0, 0, which * GROUP_ROWS + at : which * GROUP_ROWS + at + HEAD_DIM, :]
        grads = dmix_ref[0, 0, at : at + HEAD_DIM, :].astype(F32) * inv_ref[0, 0, head]
        grads = grads.astype(BF16)
        delta = jnp.sum(grads.astype(F32) * mix_ref[0, 0, at : at + HEAD_DIM, :].astype(F32), axis=0, keepdims=True)
        grad_prob = dot_tn(rows(2), grads)
        for column in range(BLOCKS):
            mine = span(column, column + 1)
            for row in range(BLOCKS):
                seen = span(row, row + 1)
                value = p_ref[0, 0, head, seen, mine].astype(F32) * (grad_prob[seen, mine] - delta[:, mine])
                band_ref[head, span(row - column + BLOCKS - 1, row - column + BLOCKS), :] += value
                ds_ref[head % 2, seen, mine] = value.astype(BF16)
        scores = ds_ref[head % 2]
        grads_ref[group, at : at + HEAD_DIM, lanes] = dot(rows(1), scores).astype(BF16)
        grads_ref[group, GROUP_ROWS + at : GROUP_ROWS + at + HEAD_DIM, lanes] = dot_nt(rows(0), scores).astype(BF16)
        grads_ref[group, 2 * GROUP_ROWS + at : 2 * GROUP_ROWS + at + HEAD_DIM, lanes] = dot_nt(grads, p_ref[0, 0, head]).astype(BF16)

    point(0)

    @pl.when(group < GROUPS)
    def _():
        one_head(0)
        one_head(1)

    @pl.when(group < GROUPS)
    def _():
        point(1)

    @pl.when(group < GROUPS)
    def _():
        one_head(2)
        one_head(3)

    @pl.when((seq == seqs - 1) & (group < GROUPS))
    def _():
        for first in range(0, width, 256):
            value = dot_nt(flipped_ref[...], grads_ref[group, first : first + 256, :]).astype(BF16)
            for owner in range(OWNERS):
                z, x, core = owner // 4, owner // 2 % 2, owner % 2
                staged_ref[z, x, core, :, first : first + 256] = value[SHARE * owner : SHARE * (owner + 1), :]
        last_fast = fast & (group == GROUPS - 1)

        @pl.when(jnp.logical_not(last_fast))
        def _():
            keep().start()

        if fast:

            @pl.when(last_fast)
            def _():
                for which in range(3):
                    tail_start(which)

        for head in range(GROUP):
            turned = band_ref[head].T
            total = jnp.zeros((8, OFFSETS), F32)
            for some in range(BLOCK // 8):
                wide = jnp.concatenate([turned[8 * some : 8 * some + 8, :], jnp.zeros((8, BLOCK), F32)], axis=1)
                total = total + pltpu.roll(wide, BLOCK - 8 * some, 1)
            line = iota((8, OFFSETS), 0)
            moved = total
            for row in range(1, 8):
                moved = jnp.where(line == row, pltpu.roll(total, OFFSETS - row, 1), moved)
            diag_ref[pl.ds(group * GROUP + head, 1)] = jnp.sum(moved, axis=0, keepdims=True)[None]
        @pl.when(jnp.logical_not(last_fast))
        def _():
            keep().wait()

    @pl.when((seq == seqs - 1) & (group == GROUPS - 1))
    def _():
        heads, buckets = table_places()
        onehot = (bucket_of(iota((OFFSETS, 1), 0) - BLOCKS * BLOCK) == buckets).astype(F32).astype(BF16)
        row = iota((16, width), 0)
        sums = jnp.concatenate([diag_ref[head] for head in range(HEADS)] + [jnp.zeros((16 - HEADS, OFFSETS), F32)], axis=0)
        high = sums.astype(BF16)
        low = (sums - high.astype(F32)).astype(BF16)
        entries = dot(high, onehot) + dot(low, onehot)
        entries = jnp.sum(jnp.where((row == heads) & (buckets >= 0), entries, 0.0), axis=0, keepdims=True)
        column = jnp.broadcast_to(entries, (BLOCK, width)).T.astype(BF16)
        for owner in range(OWNERS):
            z, x, core = owner // 4, owner // 2 % 2, owner % 2
            mine = column[SHARE * owner : SHARE * (owner + 1), :]
            small_ref[z, x, core, :, 0:BLOCK] = mine
            small_ref[z, x, core, :, BLOCK:SMALL] = mine

    @pl.when((group == GROUPS) & (seq == 0))
    def _():
        load_weights().wait()

    @pl.when(group == GROUPS)
    def _():
        hidden, scale = hidden_terms()
        flat = wg_ref[...].reshape(GROUPS, width, width)
        cotangent = sum(dot(flat[one], grads_ref[one, :, lanes]) for one in range(GROUPS)).T
        scaled = cotangent * gains_ref[0:1, :]
        unit = hidden * scale
        inner = jnp.mean(scaled * unit, axis=1, keepdims=True)
        ig_ref[...] = (gm_ref[...].astype(F32) + scale * (scaled - unit * inner)).astype(BF16)

    @pl.when(group == GROUPS)
    def _():
        point(1)

    if fast:

        @pl.when(step == (GROUPS + 1) * seqs - 1)
        def _():
            run_rest((2 * GROUPS + 2) * (flipped_ref.shape[1] // LENGTH), [BACK_SCATTER, TAIL_SCATTER], travel)


def back(x, gm, gains, weights, qkv, p, inv, mix, dmix, early, fast):
    tokens, width = x.shape
    seqs = tokens // LENGTH
    piece = (DEPTH, WIDE, CORES, SHARE, width)
    last = GROUPS - 1
    group_at = lambda g: jnp.minimum(g, last)
    seq_at = lambda g, s: jnp.where(g <= last, s, seqs - 1)
    four = lambda rows: pl.BlockSpec((1, 1, rows, LENGTH), lambda g, s: (group_at(g), seq_at(g, s), 0, 0))
    x_rows = pl.BlockSpec((LENGTH, width), lambda g, s: (jnp.where((g == 0) | (g == GROUPS), s, 0), 0))
    end_rows = pl.BlockSpec((LENGTH, width), lambda g, s: (jnp.where(g == GROUPS, s, 0), 0))
    out_specs = [end_rows, ANY, whole((DEPTH, WIDE, CORES, SHARE, SMALL))]
    out_shape = [
        jax.ShapeDtypeStruct((tokens, width), BF16), jax.ShapeDtypeStruct((GROUPS, *piece), BF16),
        jax.ShapeDtypeStruct((DEPTH, WIDE, CORES, SHARE, SMALL), BF16),
    ]
    scratch = [
        pltpu.VMEM((GROUP, BAND, BLOCK), F32), pltpu.VMEM((width, tokens), BF16), pltpu.VMEM((GROUPS, width, tokens), BF16),
        pltpu.VMEM((GROUPS, *piece), BF16), pltpu.VMEM((HEADS, 1, OFFSETS), F32), pltpu.VMEM(piece, BF16),
        pltpu.VMEM((2, LENGTH, LENGTH), BF16), pltpu.SemaphoreType.DMA,
        pltpu.SemaphoreType.DMA,
    ]
    kernel = partial(back_kernel, fast=fast)
    if fast:
        sums = BACK_SUMS
        out_specs += [whole((sums, SHARE, width)), whole((TAIL_SUMS, SHARE, SMALL))]
        out_shape += [jax.ShapeDtypeStruct((sums, SHARE, width), F32), jax.ShapeDtypeStruct((TAIL_SUMS, SHARE, SMALL), F32)]
        scratch += scatter_scratch(sums, SHARE, width) + scatter_scratch(TAIL_SUMS, SHARE, SMALL, TAIL_SUMS)
    return pl.pallas_call(
        kernel,
        name="back",
        grid=(GROUPS + 1, seqs),
        in_specs=[
            x_rows, end_rows, whole((8, width)),
            ANY, four(width),
            pl.BlockSpec((1, 1, GROUP, LENGTH, LENGTH), lambda g, s: (group_at(g), seq_at(g, s), 0, 0, 0)),
            pl.BlockSpec((1, 1, GROUP, 1, LENGTH), lambda g, s: (group_at(g), seq_at(g, s), 0, 0, 0)),
            four(GROUP_ROWS), four(GROUP_ROWS), ANY,
        ],
        out_specs=out_specs,
        out_shape=out_shape,
        scratch_shapes=scratch,
        compiler_params=pltpu.CompilerParams(
            vmem_limit_bytes=VMEM_LIMIT, collective_id=3 if fast else None, has_side_effects=fast
        ),
    )(x, gm, gains, weights, qkv, p, inv, mix, dmix, early)


def finish_kernel(
    out_ref, ig_ref, mean_ref, early_ref, late_ref, tail_ref, wq_ref, wk_ref, wv_ref, win_ref, gains_ref,
    output_ref, input_grad_ref, pooled_ref, gq_ref, gk_ref, gv_ref, go_ref, gin_ref, gout_ref, first_ref, second_ref, table_ref,
):
    output_ref[...] = out_ref[...]
    input_grad_ref[...] = ig_ref[...]
    pooled_ref[...] = mean_ref[...]
    step = pl.program_id(0)

    @pl.when(step == 0)
    def _():
        for which, target in enumerate((gq_ref, gk_ref, gv_ref)):
            mine = slice(which * GROUP_ROWS, (which + 1) * GROUP_ROWS)
            for group in range(GROUPS):
                value = tail_ref[which] if group == GROUPS - 1 else late_ref[BACK_BEFORE + group, :, mine]
                target[:, group * GROUP_ROWS : (group + 1) * GROUP_ROWS] = value
        go_ref[...] = late_ref[2 * PARTS - FEED_SUMS]

    @pl.when(step == 1)
    def _():
        for part in range(PARTS):
            piece = 2 * part + 1
            gout_ref[part * SHARE : (part + 1) * SHARE, :] = (
                early_ref[piece] if piece < FEED_SUMS else late_ref[piece - FEED_SUMS]
            )

    @pl.when(step == 2)
    def _():
        for part in range(PARTS):
            piece = 2 * part
            value = early_ref[piece] if piece < FEED_SUMS else late_ref[piece - FEED_SUMS]
            for owner in range(OWNERS):
                at = (owner * PARTS + part) * SHARE
                gin_ref[:, at : at + SHARE] = value[:, owner * SHARE : (owner + 1) * SHARE]

    @pl.when(step == pl.num_programs(0) - 1)
    def _():
        def weigh(weight_ref, grad_ref):
            return jnp.sum(weight_ref[...].astype(F32) * grad_ref[...], axis=1, keepdims=True)

        first = weigh(wq_ref, gq_ref) + weigh(wk_ref, gk_ref) + weigh(wv_ref, gv_ref)
        second = weigh(win_ref, gin_ref)
        column = iota((SHARE, BLOCK), 1)
        lines = jnp.where(column == 0, first, jnp.where(column == 1, second, tail_ref[GROUPS, :, 0:BLOCK])).T
        gains = lines[0:2, 0:SHARE] / gains_ref[0:2, 0:SHARE].astype(F32)
        first_ref[...] = gains[0:1, :]
        second_ref[...] = gains[1:2, :]
        table_ref[...] = lines[2:3, 0:TABLE_SHARE]


def finish(out, ig, mean, early, late, tail, wq, wk, wv, win, gains):
    tokens, width = out.shape
    ff = win.shape[1]
    rows = pl.BlockSpec((LENGTH, width), lambda s: (s, 0))
    means = pl.BlockSpec((1, 2, width), lambda s: (s, 0, 0))
    low = jax.ShapeDtypeStruct((tokens, width), BF16)
    square = whole((SHARE, width))
    table = lambda *shape: jax.ShapeDtypeStruct(shape, F32)
    return pl.pallas_call(
        finish_kernel,
        name="finish",
        grid=(tokens // LENGTH,),
        in_specs=[
            rows, rows, means, whole(early.shape), whole(late.shape), whole(tail.shape), square, square, square, whole((SHARE, ff)),
            whole(gains.shape),
        ],
        out_specs=[
            rows, rows, means, square, square, square, square, whole((SHARE, ff)), whole((ff // OWNERS, width)),
            whole((1, SHARE)), whole((1, SHARE)),
            whole((1, TABLE_SHARE)),
        ],
        out_shape=[
            low, low, table(*mean.shape), table(SHARE, width), table(SHARE, width), table(SHARE, width), table(SHARE, width), table(SHARE, ff),
            table(ff // OWNERS, width), table(1, SHARE), table(1, SHARE), table(1, TABLE_SHARE),
        ],
        compiler_params=pltpu.CompilerParams(vmem_limit_bytes=VMEM_LIMIT),
    )(out, ig, mean, early, late, tail, wq, wk, wv, win, gains)


def ordered(rows, w_query, w_key, w_value, w_output, w_in, w_out):
    width = w_query.shape[1]
    groups = [
        jnp.concatenate([one[:, at * GROUP_ROWS : (at + 1) * GROUP_ROWS] for one in (w_query, w_key, w_value)], axis=1)
        for at in range(GROUPS)
    ]
    inner = w_in.reshape(rows, OWNERS, PARTS, SHARE).transpose(2, 0, 1, 3).reshape(PARTS, rows, width)
    outer = w_out.reshape(-1, PARTS, SHARE, width).transpose(1, 0, 2, 3).reshape(PARTS, rows, width)
    parts = [one for at in range(PARTS) for one in (inner[at], outer[at])]
    return jnp.stack(groups + [w_output] + parts)


def small_of(gain_attn, gain_ffn, rel_table):
    lines = [one.reshape(-1, 1, share) for one, share in ((gain_attn, SHARE), (gain_ffn, SHARE), (rel_table, TABLE_SHARE))]
    padded = [jnp.pad(one, ((0, 0), (0, 0), (0, BLOCK - one.shape[2]))) for one in lines]
    return jnp.pad(jnp.concatenate(padded, axis=1), ((0, 0), (0, 13), (0, 0)))


def shards(
    hidden_in, out_grad, pooled_gradient, gain_attn, w_query, w_key, w_value, w_output, rel_table, gain_ffn, w_in, w_out,
    pair_flags, instruction_mask, *, fast,
):
    width = hidden_in.shape[1]
    own = (w_query, w_key, w_value, w_output, w_in, w_out)
    if fast:
        shares = arrange(*own)
        small = small_of(gain_attn, gain_ffn, rel_table)[0]
    else:
        gather = lambda one: lax.all_gather(one, "fsdp", axis=0, tiled=True)
        shares = ordered(width, *map(gather, own)).reshape(-1, DEPTH, WIDE, CORES, SHARE, width)
        small = small_of(*map(gather, (gain_attn, gain_ffn, rel_table)))
    flags = pair_flags.reshape(-1, 1, LENGTH)
    instr = instruction_mask.reshape(-1, 1, LENGTH)
    qkv, p, inv, mix, mid, n2, bg, gains, *rest = attend(
        hidden_in, out_grad, pooled_gradient, flags, instr, shares, small, fast
    )
    early = rest[0] if fast else shares
    output, pooled, gm, dmix, parts, *rest = feed(
        n2, bg, mid, flags, instr, gains, mix, early, shares, fast
    )
    early_sums = rest
    input_grad, group_parts, small_parts, *rest = back(hidden_in, gm, gains, early, qkv, p, inv, mix, dmix, parts, fast)
    if fast:
        *results, grad_in, grad_out, first, second, table = finish(
            output, input_grad, pooled, early_sums[0], *rest, w_query, w_key, w_value, w_in, small
        )
        output, pooled, input_grad = results[0], results[2], results[1]
        return (output, pooled, input_grad, first[0], *results[3:], table[0], second[0], grad_in, grad_out)
    sums = jnp.concatenate([parts, group_parts]).reshape(-1, width, width)
    table = small_parts.reshape(OWNERS, SHARE, SMALL)[:, :TABLE_SHARE, 0].reshape(-1)
    rows = width
    groups = [sums[2 * PARTS + 1 + at] for at in range(GROUPS)]
    grad_query, grad_key, grad_value = (
        jnp.concatenate([one[:, at * GROUP_ROWS : (at + 1) * GROUP_ROWS] for one in groups], axis=1) for at in range(3)
    )
    grad_output = sums[2 * PARTS]
    grad_in = sums[0 : 2 * PARTS : 2].reshape(PARTS, rows, OWNERS, SHARE).transpose(1, 2, 0, 3).reshape(rows, -1)
    grad_out = sums[1 : 2 * PARTS : 2].reshape(PARTS, -1, SHARE, width).transpose(1, 0, 2, 3).reshape(-1, width)
    scatter = lambda one: lax.psum(lax.psum_scatter(one, "fsdp", scatter_dimension=0, tiled=True), "grp").astype(F32)
    grad_query, grad_key, grad_value, grad_output, grad_in, grad_out, table = map(
        scatter, (grad_query, grad_key, grad_value, grad_output, grad_in, grad_out, table)
    )
    weigh = lambda weight, grad: jnp.sum(weight.astype(F32) * grad, axis=1)
    grad_gain = weigh(w_query, grad_query) + weigh(w_key, grad_key) + weigh(w_value, grad_value)
    return (
        output, pooled, input_grad, grad_gain / gain_attn.astype(F32),
        grad_query, grad_key, grad_value, grad_output, table.astype(F32),
        weigh(w_in, grad_in) / gain_ffn.astype(F32), grad_in, grad_out,
    )


def solution(mesh):
    tokens, square, line = P(("grp", "fsdp"), None), P("fsdp", None), P("fsdp")
    cube, flat = P(("grp", "fsdp"), None, None), P(("grp", "fsdp"))
    fast = mesh.shape["fsdp"] == OWNERS and mesh.shape["grp"] == 2
    return jax.shard_map(
        partial(shards, fast=fast),
        mesh=mesh,
        in_specs=(tokens, tokens, cube, line, square, square, square, square, line, line, square, square, flat, flat),
        out_specs=(tokens, cube, tokens, line, square, square, square, square, line, line, square, square),
        check_vma=False,
    )
```

```python
from functools import partial

import jax
import jax.numpy as jnp
from jax import lax
from jax.experimental import pallas as pl
from jax.experimental.pallas import tpu as pltpu
from jax.sharding import PartitionSpec as P

HEADS = 12
HEAD_DIM = 64
BUCKETS = 32
LENGTH = 512
BLOCK = 128
BLOCKS = LENGTH // BLOCK
BAND_BLOCKS = 2 * BLOCKS - 1
BAND = BAND_BLOCKS * BLOCK
OFFSETS = BAND + BLOCK
GROUPS = 3
GROUP = HEADS // GROUPS
GROUP_ROWS = GROUP * HEAD_DIM
OWNERS, PARTS, SHARE = 16, 4, 48
TABLE_SHARE = HEADS * BUCKETS // OWNERS
SMALL = 256
EPS = 1e-06
NEG = -1e30
LIMITS = (12, 16, 23, 32, 46, 64, 91)
ROOT = 0.7978845608028654
CUBE = 0.044715
F32 = jnp.float32
BF16 = jnp.bfloat16
ANY = pl.BlockSpec(memory_space=pl.ANY)
VMEM_LIMIT = 63 * 1024 * 1024


def bucket_of(offset):
    distance = jnp.abs(offset)
    far_bucket = jnp.full(offset.shape, 8, jnp.int32)
    for threshold in LIMITS:
        far_bucket = far_bucket + (distance >= threshold).astype(jnp.int32)
    near_bucket = jnp.where(distance < 8, distance, far_bucket)
    return near_bucket + BUCKETS // 2 * (offset > 0).astype(jnp.int32)


def dot(a, b):
    return lax.dot_general(a, b, (((1,), (0,)), ((), ())), preferred_element_type=F32)


def dot_nt(a, b):
    return lax.dot_general(a, b, (((1,), (1,)), ((), ())), preferred_element_type=F32)


def dot_tn(a, b):
    return lax.dot_general(a, b, (((0,), (0,)), ((), ())), preferred_element_type=F32)


def dot_tt(a, b):
    return lax.dot_general(a, b, (((0,), (1,)), ((), ())), preferred_element_type=F32)


def iota(shape, axis):
    return lax.broadcasted_iota(jnp.int32, shape, axis)


def whole(shape):
    zeros = (0,) * len(shape)
    return pl.BlockSpec(shape, lambda *_: zeros, pipeline_mode=pl.Buffered(1))


def span(first, last):
    return slice(first * BLOCK, last * BLOCK)


def pool_terms(flags, instruction):
    kept = (instruction == 0).astype(F32)
    chosen = [kept * (flags == part).astype(F32) for part in range(2)]
    counts = [jnp.sum(one, axis=1, keepdims=True) for one in chosen]
    return chosen, counts


def pool_gradient(chosen, counts, pooled_grad):
    row = iota((16, LENGTH), 0)
    picks = jnp.where(row % 2 == 0, chosen[0], chosen[1])
    picks = jnp.where(row < 6, picks, 0.0).astype(BF16)
    scaled = [pooled_grad[part : part + 1, :] / counts[part] for part in range(2)]
    line = iota((16, pooled_grad.shape[1]), 0)
    both = jnp.where(line % 2 == 0, scaled[0], scaled[1])
    high = both.astype(BF16).astype(F32)
    rest = both - high
    middle = rest.astype(BF16).astype(F32)
    low = rest - middle
    parts = jnp.where(line < 2, high, jnp.where(line < 4, middle, jnp.where(line < 6, low, 0.0)))
    return dot_tn(picks, parts.astype(BF16))


def norm_back(value, gain, cotangent):
    scale = lax.rsqrt(jnp.mean(value * value, axis=1, keepdims=True) + EPS)
    scaled = cotangent * gain
    unit = value * scale
    inner = jnp.mean(scaled * unit, axis=1, keepdims=True)
    return scale * (scaled - unit * inner), jnp.sum(cotangent * unit, axis=0, keepdims=True)


def owners_of():
    at = iota((1, OWNERS * SHARE), 1)
    owner = sum((at >= SHARE * one).astype(jnp.int32) for one in range(1, OWNERS))
    return owner, at - SHARE * owner


def table_places():
    owner, inside = owners_of()
    entry = owner * TABLE_SHARE + inside
    bucket = sum((entry >= HEADS * one).astype(jnp.int32) for one in range(1, BUCKETS))
    return entry - HEADS * bucket, jnp.where(inside < TABLE_SHARE, bucket, -1)


DEPTH, WIDE, CORES = 4, 2, 2
MESH_ID = pl.DeviceIdType.MESH


def place():
    grp, at = lax.axis_index("grp"), lax.axis_index("fsdp")
    z, x, core = lax.div(at, WIDE * CORES), lax.rem(lax.div(at, CORES), WIDE), lax.rem(at, CORES)

    def device(grp, z, x, core):
        return (grp, z * (WIDE * CORES) + x * CORES + core)

    return dict(
        at=at, y=grp, z=z, x=x, core=core,
        over_y=device(1 - grp, z, x, core),
        over_x=device(grp, z, 1 - x, core),
        over_core=device(grp, z, x, 1 - core),
        over_z=[device(grp, lax.rem(z + one, DEPTH), x, core) for one in range(1, DEPTH)],
        ahead=[lax.rem(z + one, DEPTH) for one in range(1, DEPTH)],
        behind=[lax.rem(z + DEPTH - one, DEPTH) for one in range(1, DEPTH)],
    )


def greet(here):
    barrier = pltpu.get_barrier_semaphore()
    for device in (here["over_y"], here["over_x"], here["over_core"], *here["over_z"]):
        pl.semaphore_signal(barrier, inc=1, device_id=device, device_id_type=MESH_ID)


def await_greetings():
    pl.semaphore_wait(pltpu.get_barrier_semaphore(), DEPTH + 2)


def others(here):
    at = here["at"]
    for one in range(1, OWNERS):
        yield one, (here["y"], lax.rem(at + one, OWNERS)), lax.rem(at + OWNERS - one, OWNERS)


def greet_all(here):
    barrier = pltpu.get_barrier_semaphore()
    pl.semaphore_signal(barrier, inc=1, device_id=here["over_y"], device_id_type=MESH_ID)
    for _, device, _ in others(here):
        pl.semaphore_signal(barrier, inc=1, device_id=device, device_id_type=MESH_ID)
    pl.semaphore_wait(barrier, OWNERS)


def gather_phase(phase, sem, here, share_ref, whole_ref, sent, got, own_sem, shared=False):
    z, x, core = here["z"], here["x"], here["core"]
    every = slice(None)
    half = share_ref.shape[-1] // 2
    lanes = pl.ds(pl.multiple_of(here["y"] * half, half), half) if shared else every
    other = pl.ds(pl.multiple_of((1 - here["y"]) * half, half), half) if shared else every
    mine = share_ref.at[:, lanes] if shared else share_ref

    def copy(source, where, channel, device):
        return pltpu.make_async_remote_copy(
            src_ref=source, dst_ref=whole_ref.at[where], send_sem=sent.at[channel, sem], recv_sem=got.at[channel, sem],
            device_id=device, device_id_type=MESH_ID,
        )

    def same(where, channel, device):
        return copy(whole_ref.at[where], where, channel, device)

    own = lambda: pltpu.make_async_copy(mine, whole_ref.at[z, x, core, every, lanes], own_sem.at[sem])
    line_out = lambda one: copy(mine, (z, x, core, every, lanes), one, here["over_z"][one])
    line_in = lambda one: copy(mine, (here["behind"][one], x, core, every, lanes), one, here["over_z"][one])
    side_out = lambda: same((every, x, core, every, lanes), 3, here["over_x"])
    side_in = lambda: same((every, 1 - x, core, every, lanes), 3, here["over_x"])
    group_out = lambda: same((every, every, core, every, lanes), 5, here["over_y"])
    group_in = lambda: same((every, every, core, every, other), 5, here["over_y"])
    core_out = lambda: same((every, every, core), 4, here["over_core"])
    core_in = lambda: same((every, every, 1 - core), 4, here["over_core"])
    if phase == 0:
        own().start()
        for one in range(DEPTH - 1):
            line_out(one).start()
    elif phase == 1:
        own().wait()
        for one in range(DEPTH - 1):
            line_in(one).wait_recv()
        side_out().start()
    elif phase == 2:
        side_in().wait_recv()
        group_out().start()
    elif phase == 3:
        if shared:
            group_in().wait_recv()
        else:
            side_in().wait_recv()
        core_out().start()
    else:
        for one in range(DEPTH - 1):
            line_out(one).wait_send()
        side_out().wait_send()
        if shared:
            group_out().wait_send()
        core_out().wait_send()
        core_in().wait_recv()


def scatter_phase(phase, piece, here, part_ref, out_ref, own, fromc, fromx, fromz, last, sent, got, own_sem):
    z, x, core = here["z"], here["x"], here["core"]
    slot = lax.rem(piece, own.shape[0])

    def remote(source, target, channel, device):
        return pltpu.make_async_remote_copy(
            src_ref=source, dst_ref=target, send_sem=sent.at[channel, piece], recv_sem=got.at[channel, piece],
            device_id=device, device_id_type=MESH_ID,
        )

    total = fromc.at[piece]
    over_core = lambda: remote(part_ref.at[:, :, 1 - core], total, 0, here["over_core"])
    load = lambda: pltpu.make_async_copy(part_ref.at[:, :, core], own.at[slot], own_sem.at[slot])
    over_x = lambda: remote(fromc.at[piece, :, 1 - x], fromx.at[piece], 1, here["over_x"])
    line_out = lambda one: remote(fromc.at[piece, here["ahead"][one], x], fromz.at[piece, z], 2 + one, here["over_z"][one])
    line_in = lambda one: remote(
        fromc.at[piece, z, x], fromz.at[piece, here["behind"][one]], 2 + one, here["over_z"][one]
    )
    final = lambda: remote(fromc.at[piece, z, x], last.at[piece], 5, here["over_y"])

    if phase == 0:
        over_core().start()
        load().start()
    elif phase == 1:
        load().wait()
        over_core().wait()

        def one(at, _):
            for side in range(WIDE):
                fromc[piece, at, side] = own[slot, at, side] + fromc[piece, at, side]
            return 0

        lax.fori_loop(0, DEPTH, one, 0)
        over_x().start()
    elif phase == 2:
        over_x().wait()

        def one(at, _):
            fromc[piece, at, x] = fromc[piece, at, x] + fromx[piece, at]
            return 0

        lax.fori_loop(0, DEPTH, one, 0)
        for one in range(DEPTH - 1):
            line_out(one).start()
    elif phase == 3:
        mine = fromc[piece, z, x].astype(F32)
        for one in range(DEPTH - 1):
            line_in(one).wait_recv()
            mine = mine + fromz[piece, here["behind"][one]].astype(F32)
        fromc[piece, z, x] = mine.astype(BF16)
        final().start()
    else:
        for one in range(DEPTH - 1):
            line_out(one).wait_send()
        final().wait()
        out_ref[piece] = fromc[piece, z, x].astype(F32) + last[piece].astype(F32)


def run_slot(slot, table, act):
    for phase in reversed(range(max(map(len, table.values())))):
        due, found = False, 0
        for piece, slots in table.items():
            if slots[phase] is not None:
                now = slot == slots[phase]
                due, found = due | now, jnp.where(now, piece, found)
        if due is not False:

            @pl.when(due)
            def _(phase=phase, found=found):
                act(phase, found)


def run_rest(first, tables, travel):
    end = 1 + max(slot for table in tables for slots in table.values() for slot in slots if slot is not None)

    def one(slot, _):
        travel(slot)
        return 0

    if end > first:
        lax.fori_loop(first, end, one, 0)


def gather_sems(pieces):
    return [pltpu.SemaphoreType.DMA((6, pieces)), pltpu.SemaphoreType.DMA((6, pieces)), pltpu.SemaphoreType.DMA((pieces,))]


def scatter_scratch(pieces, rows, columns, places=2):
    return [
        pltpu.VMEM((places, DEPTH, WIDE, rows, columns), BF16),
        pltpu.VMEM((pieces, DEPTH, WIDE, rows, columns), BF16),
        pltpu.VMEM((pieces, DEPTH, rows, columns), BF16),
        pltpu.VMEM((pieces, DEPTH, rows, columns), BF16),
        pltpu.VMEM((pieces, rows, columns), BF16),
        pltpu.SemaphoreType.DMA((6, pieces)),
        pltpu.SemaphoreType.DMA((6, pieces)),
        pltpu.SemaphoreType.DMA((places,)),
    ]


ATTEND_PIECES, FEED_PIECES = 8, 4
ATTEND_DIRECT = {2: (0, 6, None, 12, 14), 3: (3, 9, None, 15, 17), 5: (9, 14, None, 20, 22), 7: (14, 19, None, 25, 26)}
ATTEND_SHARED = {1: (None, None, 0, 5, 7), 4: (7, 12, 16, 21, 23), 6: (12, 17, 21, 24, 25)}
FEED_DIRECT = {1: (1, 7, None, 12, 15), 3: (6, 12, None, 18, 20)}
FEED_SHARED = {0: (0, 4, 7, 11, 14), 2: (5, 8, 15, 19, 21)}
FEED_SUMS = 5
FEED_SCATTER = {0: (8, 13, 18, 24, 26), 1: (11, 15, 21, 26, 28), 2: (16, 18, 24, 31, 32), 3: (19, 21, 27, 32, 35), 4: (24, 26, 31, 37, 40)}
BACK_BEFORE, BACK_SUMS = 4, 6
BACK_SCATTER = {
    0: (2, 4, 8, 13, 15), 1: (4, 6, 11, 16, 18), 2: (6, 9, 14, 19, 21), 3: (9, 12, 17, 22, 24),
    4: (12, 14, 19, 24, 27), 5: (16, 18, 23, 27, 29),
}
TAIL_SUMS = 4
TAIL_SCATTER = {0: (None, 24, 26, 28, 30), 1: (None, 25, 27, 29, 31), 2: (None, 26, 28, 30, 32), 3: (24, 27, 29, 31, 33)}


def arrange_kernel(wq_ref, wk_ref, wv_ref, wo_ref, win_ref, wout_ref, shares_ref, line_ref):
    for group in range(GROUPS):
        mine = slice(group * GROUP_ROWS, (group + 1) * GROUP_ROWS)
        for which, one in enumerate((wq_ref, wk_ref, wv_ref)):
            shares_ref[group, :, which * GROUP_ROWS : (which + 1) * GROUP_ROWS] = one[:, mine]
    shares_ref[GROUPS] = wo_ref[...]
    for part in range(PARTS):
        for owner in range(OWNERS):
            at = (owner * PARTS + part) * SHARE
            line_ref[:, owner * SHARE : (owner + 1) * SHARE] = win_ref[:, at : at + SHARE].astype(F32)
        shares_ref[GROUPS + 1 + 2 * part] = line_ref[...].astype(BF16)
        shares_ref[GROUPS + 2 + 2 * part] = wout_ref[part * SHARE : (part + 1) * SHARE, :]


def arrange(*weights):
    width = weights[0].shape[1]
    return pl.pallas_call(
        arrange_kernel,
        name="arrange",
        out_shape=jax.ShapeDtypeStruct((GROUPS + 1 + 2 * PARTS, SHARE, width), BF16),
        scratch_shapes=[pltpu.VMEM((SHARE, width), F32)],
    )(*weights)


def attend_kernel(
    x_hbm, og_hbm, pg_ref, flags_ref, instr_ref, shares_hbm, small_hbm,
    qkv_ref, p_ref, inv_ref, mix_ref, mid_ref, n2_ref, bg_hbm, gains_ref, weights_hbm,
    x_ref, bg_ref, mixed_ref, band_ref, aux_ref, normed_ref, wg_ref, wo_ref, small_ref, table_ref, cur_ref, nxt_ref, sa_ref, sb_ref,
    sems, *comm, fast,
):
    group, seq = pl.program_id(0), pl.program_id(1)
    seqs = pl.num_programs(1)
    step = group * seqs + seq
    width = x_ref.shape[1]
    if fast:
        main_sems, first_sems, small_sent, small_got = comm[0:3], comm[3:6], comm[6], comm[7]
        here = place()

        def main(phase, piece, shared=False):
            gather_phase(phase, piece, here, shares_hbm.at[piece], weights_hbm.at[piece], *main_sems, shared=shared)

        def small(start):
            for one, device, source in others(here):
                copy = lambda where: pltpu.make_async_remote_copy(
                    src_ref=small_hbm, dst_ref=small_ref.at[where], send_sem=small_sent.at[one], recv_sem=small_got.at[one],
                    device_id=device, device_id_type=MESH_ID,
                )
                if start:
                    copy(here["at"]).start()
                else:
                    copy(source).wait_recv()
                    copy(here["at"]).wait_send()

        def first(phase, which):
            lanes = pl.ds(which * GROUP_ROWS, GROUP_ROWS)
            every = slice(None)
            gather_phase(
                phase, which, here, shares_hbm.at[0, :, lanes], weights_hbm.at[0, every, every, every, every, lanes], *first_sems
            )

        def travel(slot):
            run_slot(slot, ATTEND_DIRECT, main)
            run_slot(slot, ATTEND_SHARED, partial(main, shared=True))

        point = lambda at: travel(2 * step + at)
    else:
        point = lambda at: None
    small_own = small_ref.at[here["at"]] if fast else small_ref
    load_small = lambda: pltpu.make_async_copy(small_hbm, small_own, sems.at[0])
    load_hidden = lambda: pltpu.make_async_copy(x_hbm, x_ref, sems.at[3])
    load_grad = lambda: pltpu.make_async_copy(og_hbm, bg_ref, sems.at[4])
    keep_grad = lambda: pltpu.make_async_copy(bg_ref, bg_hbm, sems.at[4])
    load_group = lambda at: pltpu.make_async_copy(weights_hbm.at[at], wg_ref, sems.at[1])
    load_output = lambda: pltpu.make_async_copy(weights_hbm.at[GROUPS], wo_ref, sems.at[2])
    square = lambda ref: ref[...].reshape(width, width)

    def prepare(at):
        flags = flags_ref[at]
        chosen, counts = pool_terms(flags, instr_ref[at])
        rows = pl.ds(pl.multiple_of(at * LENGTH, LENGTH), LENGTH)
        bg_ref[rows, :] = (bg_ref[rows, :].astype(F32) + pool_gradient(chosen, counts, pg_ref[at])).astype(BF16)
        row = iota((16, LENGTH), 0)
        aux_ref[0, at] = jnp.where(row == 0, 1 - flags, jnp.where(row == 1, flags, 0)).astype(F32).astype(BF16)
        other = jnp.where(row == 0, flags, jnp.where(row == 1, 1 - flags, 0)).astype(F32) * NEG
        aux_ref[1, at] = other.astype(BF16)

    def normalize(at):
        rows = pl.ds(pl.multiple_of(at * LENGTH, LENGTH), LENGTH)
        hidden = x_ref[rows, :].astype(F32)
        scale = lax.rsqrt(jnp.mean(hidden * hidden, axis=1, keepdims=True) + EPS)
        normed_ref[at] = (hidden * scale * gains_ref[0:1, :]).astype(BF16)

    def every_seq(act):
        def one_seq(at, _):
            act(at)
            return 0

        lax.fori_loop(0, seqs, one_seq, 0)

    def project(at, target):
        target[...] = dot_tt(square(wg_ref), normed_ref[at]).astype(BF16)

    def part(source, which, head):
        first = which * GROUP_ROWS + head * HEAD_DIM
        return source[first : first + HEAD_DIM, :]

    def score(source, at_group, at, head, target):
        queries = jnp.concatenate([part(source, 0, head), aux_ref[0, at]], axis=0)
        keys = jnp.concatenate([part(source, 1, head), aux_ref[1, at]], axis=0)
        scores = dot_tn(keys, queries)
        for row in range(BLOCKS):
            for column in range(BLOCKS):
                bias = band_ref[at_group * GROUP + head, span(row - column + BLOCKS - 1, row - column + BLOCKS), :]
                target[span(row, row + 1), span(column, column + 1)] = scores[span(row, row + 1), span(column, column + 1)] + bias

    def soften(head, source):
        scores = source[...]
        exponent = jnp.exp(scores - jnp.max(scores, axis=0, keepdims=True)).astype(BF16)
        p_ref[0, 0, head] = exponent
        values = jnp.concatenate([part(cur_ref, 2, head), jnp.ones((16, LENGTH), BF16)], axis=0)
        mixed = dot(values, exponent)
        inverse = 1.0 / mixed[HEAD_DIM : HEAD_DIM + 1, :]
        inv_ref[0, 0, head] = inverse
        mixed = (mixed[0:HEAD_DIM, :] * inverse).astype(BF16)
        mix_ref[0, 0, head * HEAD_DIM : (head + 1) * HEAD_DIM, :] = mixed
        mixed_ref[seq, pl.ds(pl.multiple_of(group * GROUP_ROWS + head * HEAD_DIM, HEAD_DIM), HEAD_DIM), :] = mixed

    def read_small():
        owner, inside = owners_of()
        spread = (iota((BLOCK, width), 0) == inside).astype(F32).astype(BF16)
        shares = small_ref[...].astype(F32)

        def line(which):
            placed = dot(shares[:, which, :].astype(BF16), spread)
            return jnp.sum(jnp.where(iota((OWNERS, width), 0) == owner, placed, 0.0), axis=0, keepdims=True)

        row = iota((8, width), 0)
        gains_ref[...] = jnp.where(row == 0, line(0), line(1))
        table_row = line(2)
        heads, buckets = table_places()
        entries = jnp.where((iota((16, width), 0) == heads) & (buckets >= 0), table_row, 0.0).astype(BF16)
        onehot = (bucket_of(iota((OFFSETS, 1), 0) - BLOCKS * BLOCK) == buckets).astype(F32).astype(BF16)
        table_ref[...] = dot_nt(entries, onehot)

    def make_bands(at_group):
        def one_head(head, _):
            table = table_ref[...]
            line = jnp.sum(jnp.where(iota(table.shape, 0) == head, table, 0.0), axis=0, keepdims=True)
            turned = pltpu.roll(jnp.broadcast_to(line, (BLOCK, OFFSETS)), 0, 1, stride=1, stride_axis=0)
            band_ref[head] = turned[:, BLOCK:].T
            return 0

        lax.fori_loop(at_group * GROUP, (at_group + 1) * GROUP, one_head, 0)

    @pl.when(step == 0)
    def _():
        load_grad().start()
        load_hidden().start()
        load_small().start()
        if fast:
            greet_all(here)
            small(True)
            for which in range(3):
                first(0, which)
        load_grad().wait()
        every_seq(prepare)
        keep_grad().start()
        load_hidden().wait()
        load_small().wait()
        if fast:
            small(False)
            first(1, 0)
            main(0, 1, shared=True)
            read_small()
            first(1, 1)
            normalize(0)
            normalize(1)
            first(1, 2)
            normalize(2)
            normalize(3)
            first(3, 0)
            make_bands(0)
            first(3, 1)
            main(1, 1, shared=True)
            make_bands(1)
            first(3, 2)
            make_bands(2)
            for which in range(3):
                first(4, which)
        else:
            read_small()
            every_seq(normalize)
            for one in range(GROUPS):
                make_bands(one)
        load_group(0).start()
        load_group(0).wait()
        project(0, nxt_ref)
        score(nxt_ref, 0, 0, 0, sa_ref)

    last_seq = seq == seqs - 1
    more = step + 1 < GROUPS * seqs
    cur_ref[...] = nxt_ref[...]

    next_seq = jnp.where(last_seq, 0, seq + 1)
    next_group = jnp.where(last_seq, jnp.minimum(group + 1, GROUPS - 1), group)
    point(0)
    qkv_ref[0, 0] = cur_ref[...]
    score(cur_ref, group, seq, 1, sb_ref)
    soften(0, sa_ref)
    score(cur_ref, group, seq, 2, sa_ref)
    soften(1, sb_ref)
    point(1)
    score(cur_ref, group, seq, 3, sb_ref)
    soften(2, sa_ref)

    @pl.when(last_seq & more)
    def _():
        load_group(group + 1).start()
        load_group(group + 1).wait()

    project(next_seq, nxt_ref)
    score(nxt_ref, next_group, next_seq, 0, sa_ref)
    soften(3, sb_ref)

    @pl.when((seq == 0) & (group == GROUPS - 1))
    def _():
        load_output().start()
        load_output().wait()

    @pl.when(group == GROUPS - 1)
    def _():
        rows = pl.ds(pl.multiple_of(seq * LENGTH, LENGTH), LENGTH)
        middle = x_ref[rows, :].astype(F32) + dot_tn(mixed_ref[seq], square(wo_ref))
        mid_ref[...] = middle
        scale = lax.rsqrt(jnp.mean(middle * middle, axis=1, keepdims=True) + EPS)
        n2_ref[...] = (middle * scale * gains_ref[1:2, :]).astype(BF16)

    @pl.when(step == GROUPS * seqs - 1)
    def _():
        keep_grad().wait()
        if fast:
            run_rest(2 * GROUPS * (x_ref.shape[0] // LENGTH), [ATTEND_DIRECT, ATTEND_SHARED], travel)


def attend(x, og, pg, flags, instr, shares, small, fast):
    tokens, width = x.shape
    seqs = tokens // LENGTH
    last_rows = pl.BlockSpec((LENGTH, width), lambda g, s: (jnp.where(g == GROUPS - 1, s, 0), 0))
    low = jax.ShapeDtypeStruct((tokens, width), BF16)
    out_specs = [
        pl.BlockSpec((1, 1, width, LENGTH), lambda g, s: (g, s, 0, 0)),
        pl.BlockSpec((1, 1, GROUP, LENGTH, LENGTH), lambda g, s: (g, s, 0, 0, 0)),
        pl.BlockSpec((1, 1, GROUP, 1, LENGTH), lambda g, s: (g, s, 0, 0, 0)),
        pl.BlockSpec((1, 1, GROUP_ROWS, LENGTH), lambda g, s: (g, s, 0, 0)), last_rows, last_rows, ANY, whole((8, width)),
    ]
    out_shape = [
        jax.ShapeDtypeStruct((GROUPS, seqs, width, LENGTH), BF16),
        jax.ShapeDtypeStruct((GROUPS, seqs, GROUP, LENGTH, LENGTH), BF16),
        jax.ShapeDtypeStruct((GROUPS, seqs, GROUP, 1, LENGTH), F32),
        jax.ShapeDtypeStruct((GROUPS, seqs, GROUP_ROWS, LENGTH), BF16),
        jax.ShapeDtypeStruct((tokens, width), F32), low, low, jax.ShapeDtypeStruct((8, width), F32),
    ]
    scratch = [
        pltpu.VMEM((tokens, width), BF16), pltpu.VMEM((tokens, width), BF16), pltpu.VMEM((seqs, width, LENGTH), BF16),
        pltpu.VMEM((HEADS, BAND, BLOCK), F32), pltpu.VMEM((2, seqs, 16, LENGTH), BF16),
        pltpu.VMEM((seqs, LENGTH, width), BF16), pltpu.VMEM((DEPTH, WIDE, CORES, SHARE, width), BF16),
        pltpu.VMEM((DEPTH, WIDE, CORES, SHARE, width), BF16), pltpu.VMEM((OWNERS, 16, BLOCK), BF16), pltpu.VMEM((16, OFFSETS), F32),
        pltpu.VMEM((width, LENGTH), BF16), pltpu.VMEM((width, LENGTH), BF16),
        pltpu.VMEM((LENGTH, LENGTH), F32), pltpu.VMEM((LENGTH, LENGTH), F32), pltpu.SemaphoreType.DMA((5,)),
    ]
    in_specs = [
        ANY, ANY, whole((seqs, 2, width)), whole((seqs, 1, LENGTH)), whole((seqs, 1, LENGTH)), ANY, ANY,
    ]
    if fast:
        kernel = partial(attend_kernel, fast=True)
        out_specs += [ANY]
        out_shape += [jax.ShapeDtypeStruct((ATTEND_PIECES, DEPTH, WIDE, CORES, SHARE, width), BF16)]
        scratch += gather_sems(ATTEND_PIECES) + gather_sems(3) + [pltpu.SemaphoreType.DMA((OWNERS,)), pltpu.SemaphoreType.DMA((OWNERS,))]
    else:

        def kernel(*refs):
            inputs, outputs, rest = refs[:7], refs[7:15], refs[15:]
            attend_kernel(*inputs, *outputs, inputs[5], *rest, fast=False)

    return pl.pallas_call(
        kernel,
        name="attend",
        grid=(GROUPS, seqs),
        in_specs=in_specs,
        out_specs=out_specs,
        out_shape=out_shape,
        scratch_shapes=scratch,
        compiler_params=pltpu.CompilerParams(
            vmem_limit_bytes=VMEM_LIMIT, collective_id=1 if fast else None, has_side_effects=fast
        ),
    )(x, og, pg, flags, instr, shares, small)


def feed_kernel(
    n2_hbm, bg_hbm, mid_hbm, flags_ref, instr_ref, gains_ref, mid_ref, mix_ref, early_hbm, late_hbm,
    out_ref, pooled_ref, gm_ref, dmix_ref, parts_hbm, *rest, fast,
):
    if fast:
        sums_ref, gathered_hbm = rest[0:2]
        rest = rest[2:]
    n2_ref, bg_ref, res_ref, dn2_ref, act_ref, dinner_ref, win_ref, wout_ref, wo_ref, dwo_ref, staged_ref, sems, block_sems = rest[:13]
    part, block = pl.program_id(0), pl.program_id(1)
    blocks = pl.num_programs(1)
    step = part * blocks + block
    width = res_ref.shape[1]
    rows = pl.ds(pl.multiple_of(block * LENGTH, LENGTH), LENGTH)
    if fast:
        sems_of, scratch = rest[13:16], rest[16:]
        here = place()

        def travel(slot):
            def bring(phase, piece, shared=False):
                share = late_hbm.at[ATTEND_PIECES + piece]
                gather_phase(phase, piece, here, share, gathered_hbm.at[piece], *sems_of, shared=shared)

            def add(phase, piece):
                scatter_phase(phase, piece, here, parts_hbm.at[piece], sums_ref, *scratch)

            run_slot(slot, FEED_DIRECT, bring)
            run_slot(slot, FEED_SHARED, partial(bring, shared=True))
            run_slot(slot, FEED_SCATTER, add)

        point = lambda at: travel(2 * step + at)
    else:
        point = lambda at: None
    square = lambda ref: ref[...].reshape(width, width)

    def weights(at, start):
        def both(source, first):
            for which, target in enumerate((win_ref, wout_ref)):
                slot = lax.rem(at, 2)
                copy = pltpu.make_async_copy(source.at[first + which], target.at[slot], sems.at[slot, which])
                copy.start() if start else copy.wait()

        if start:
            pl.when(at < PARTS // 2)(lambda: both(early_hbm, 4 + 2 * at))
            pl.when(at >= PARTS // 2)(lambda: both(gathered_hbm if fast else late_hbm, 2 * at + (-PARTS if fast else 4)))
        else:
            both(early_hbm, 4)


    def load_block(at, start):
        mine = pl.ds(pl.multiple_of(at * LENGTH, LENGTH), LENGTH)
        for which, (source, target) in enumerate(((n2_hbm, n2_ref), (bg_hbm, bg_ref), (mid_hbm, res_ref))):
            copy = pltpu.make_async_copy(source.at[mine], target.at[mine], block_sems.at[which, at])
            copy.start() if start else copy.wait()

    load_output = lambda: pltpu.make_async_copy(early_hbm.at[GROUPS], wo_ref, sems.at[1, 2])
    keep = lambda at, which: pltpu.make_async_copy(staged_ref.at[which], parts_hbm.at[2 * at + which], sems.at[which, 3])

    @pl.when(step == 0)
    def _():
        weights(0, True)
        for at in range(res_ref.shape[0] // LENGTH):
            load_block(at, True)
        load_output().start()
        if fast:
            greet(here)
            await_greetings()
        dwo_ref[...] = jnp.zeros_like(dwo_ref)

    @pl.when((part == PARTS) & (block == 0))
    def _():
        load_output().wait()

    @pl.when(part == 0)
    def _():
        dn2_ref[rows, :] = jnp.zeros((LENGTH, width), F32)
        load_block(block, False)

    @pl.when((part < PARTS) & (block == 0))
    def _():
        weights(part, False)

    @pl.when((part > 0) & (block == 0))
    def _():
        keep(part - 1, 0).wait()
        keep(part - 1, 1).wait()

    point(0)

    @pl.when(part < PARTS)
    def _():
        slot = lax.rem(part, 2)
        inner = dot(n2_ref[rows, :], square(win_ref.at[slot]))
        grad_active = dot_nt(bg_ref[rows, :], square(wout_ref.at[slot]))
        squared = inner * inner
        half = 0.5 * jnp.tanh(inner * (ROOT + (ROOT * CUBE) * squared)) + 0.5
        active = inner * half
        slope = half + active * (1.0 - half) * (2.0 * ROOT + (6.0 * ROOT * CUBE) * squared)
        active = active.astype(BF16)
        act_ref[rows, :] = active
        dinner = (grad_active * slope).astype(BF16)
        dinner_ref[rows, :] = dinner
        res_ref[rows, :] += dot(active, square(wout_ref.at[slot]))
        dn2_ref[rows, :] += dot_nt(dinner, square(win_ref.at[slot]))

    point(1)

    @pl.when((part < PARTS - 1) & (block == blocks - 1))
    def _():
        weights(part + 1, True)

    def stage(which, first, value):
        for owner in range(OWNERS):
            z, x, core = owner // 4, owner // 2 % 2, owner % 2
            staged_ref[which, z, x, core, :, first : first + 256] = value[SHARE * owner : SHARE * (owner + 1), :]

    @pl.when((part < PARTS) & (block == blocks - 1))
    def _():
        for first in range(0, width, 256):
            stage(0, first, dot_tn(n2_ref[...], dinner_ref[:, first : first + 256]).astype(BF16))
        keep(part, 0).start()
        for first in range(0, width, 256):
            stage(1, first, dot_tn(act_ref[...], bg_ref[:, first : first + 256]).astype(BF16))
        keep(part, 1).start()

    @pl.when(part == PARTS)
    def _():
        result = res_ref[rows, :]
        out_ref[...] = result.astype(BF16)
        chosen, counts = pool_terms(flags_ref[block], instr_ref[block])
        line = iota((8, LENGTH), 0)
        picks = jnp.where(line == 0, chosen[0], jnp.where(line == 1, chosen[1], 0.0)).astype(BF16)
        high = result.astype(BF16)
        low = (result - high.astype(F32)).astype(BF16)
        total = dot(picks, high) + dot(picks, low)
        total = total / jnp.where(iota((8, 1), 0) == 0, counts[0], counts[1])
        pooled_ref[block] = total[0:2, :]
        change, _ = norm_back(mid_ref[...], gains_ref[1:2, :], dn2_ref[rows, :])
        out_low = (bg_ref[rows, :].astype(F32) + change).astype(BF16)
        gm_ref[...] = out_low
        output = square(wo_ref)
        for group in range(GROUPS):
            mine = slice(group * GROUP_ROWS, (group + 1) * GROUP_ROWS)
            dmix_ref[group, 0] = dot_nt(output[mine, :], out_low).astype(BF16)
            dwo_ref[mine, :] += dot(mix_ref[group, 0], out_low)

    @pl.when(step == (PARTS + 1) * blocks - 1)
    def _():
        for first in range(0, width, 256):
            stage(0, first, dwo_ref[:, first : first + 256].astype(BF16))
        keep(PARTS, 0).start()
        if fast:
            run_rest(2 * (PARTS + 1) * (res_ref.shape[0] // LENGTH), [FEED_DIRECT, FEED_SHARED, FEED_SCATTER], travel)
        keep(PARTS, 0).wait()


def feed(n2, bg, mid, flags, instr, gains, mix, early, late, fast):
    tokens, width = n2.shape
    seqs = tokens // LENGTH
    rows = pl.BlockSpec((LENGTH, width), lambda c, m: (jnp.where(c == PARTS, m, 0), 0))
    heads = pl.BlockSpec((GROUPS, 1, GROUP_ROWS, LENGTH), lambda c, m: (0, jnp.where(c == PARTS, m, 0), 0, 0))
    piece = (DEPTH, WIDE, CORES, SHARE, width)
    sums = FEED_SUMS
    out_specs = [rows, whole((seqs, 2, width)), rows, heads, ANY]
    out_shape = [
        jax.ShapeDtypeStruct((tokens, width), BF16), jax.ShapeDtypeStruct((seqs, 2, width), F32),
        jax.ShapeDtypeStruct((tokens, width), BF16), jax.ShapeDtypeStruct((GROUPS, seqs, GROUP_ROWS, LENGTH), BF16),
        jax.ShapeDtypeStruct((2 * PARTS + 1, *piece), BF16),
    ]
    scratch = [
        pltpu.VMEM((tokens, width), BF16), pltpu.VMEM((tokens, width), BF16),
        pltpu.VMEM((tokens, width), F32), pltpu.VMEM((tokens, width), F32), pltpu.VMEM((tokens, width), BF16),
        pltpu.VMEM((tokens, width), BF16), pltpu.VMEM((2, *piece), BF16), pltpu.VMEM((2, *piece), BF16),
        pltpu.VMEM(piece, BF16), pltpu.VMEM((width, width), F32), pltpu.VMEM((2, *piece), BF16), pltpu.SemaphoreType.DMA((2, 4)),
        pltpu.SemaphoreType.DMA((3, seqs)),
    ]
    if fast:
        out_specs += [whole((sums, SHARE, width)), ANY]
        out_shape += [
            jax.ShapeDtypeStruct((sums, SHARE, width), F32), jax.ShapeDtypeStruct((FEED_PIECES, *piece), BF16)
        ]
        scratch += gather_sems(FEED_PIECES) + scatter_scratch(sums, SHARE, width)
    return pl.pallas_call(
        partial(feed_kernel, fast=fast),
        name="feed",
        grid=(PARTS + 1, seqs),
        in_specs=[
            ANY, ANY, ANY, whole((seqs, 1, LENGTH)), whole((seqs, 1, LENGTH)), whole((8, width)), rows, heads, ANY, ANY,
        ],
        out_specs=out_specs,
        out_shape=out_shape,
        scratch_shapes=scratch,
        compiler_params=pltpu.CompilerParams(
            vmem_limit_bytes=VMEM_LIMIT, collective_id=2 if fast else None, has_side_effects=fast
        ),
    )(n2, bg, mid, flags, instr, gains, mid, mix, early, late)


def back_kernel(
    x_ref, gm_ref, gains_ref, weights_hbm, qkv_ref, p_ref, inv_ref, mix_ref, dmix_ref, early_hbm,
    ig_ref, parts_hbm, small_ref, *rest, fast,
):
    if fast:
        sums_ref, tail_ref = rest[0:2]
        rest = rest[2:]
    band_ref, flipped_ref, grads_ref, wg_ref, diag_ref, staged_ref, ds_ref, sem, weight_sem = rest[:9]
    group, seq = pl.program_id(0), pl.program_id(1)
    seqs = pl.num_programs(1)
    step = group * seqs + seq
    width = x_ref.shape[1]
    if fast:
        extra = len(scatter_scratch(1, SHARE, width))
        scratch, tail_scratch = rest[9 : 9 + extra], rest[9 + extra :]
        here = place()

        def main(phase, piece):
            if phase > 0:
                scatter_phase(phase, piece, here, early_hbm.at[0], sums_ref, *scratch)
                return

            @pl.when(piece < BACK_BEFORE)
            def _():
                scatter_phase(phase, piece, here, early_hbm.at[FEED_SUMS + piece], sums_ref, *scratch)

            @pl.when(piece >= BACK_BEFORE)
            def _():
                scatter_phase(phase, piece, here, parts_hbm.at[piece - BACK_BEFORE], sums_ref, *scratch)

        def tail(phase, piece):
            if phase > 0:
                scatter_phase(phase, piece, here, small_ref, tail_ref, *tail_scratch)
                return
            scatter_phase(phase, GROUPS, here, small_ref, tail_ref, *tail_scratch)

        def tail_start(which):
            mine = slice(which * SMALL, (which + 1) * SMALL)
            scatter_phase(0, which, here, staged_ref.at[:, :, :, :, mine], tail_ref, *tail_scratch)

        def travel(slot):
            run_slot(slot, BACK_SCATTER, main)
            run_slot(slot, TAIL_SCATTER, tail)

        def point(at):
            travel(2 * step + at)
    else:
        point = lambda at: None
    keep = lambda: pltpu.make_async_copy(staged_ref, parts_hbm.at[group], sem)
    lanes = pl.ds(pl.multiple_of(seq * LENGTH, LENGTH), LENGTH)

    def hidden_terms():
        hidden = x_ref[...].astype(F32)
        scale = lax.rsqrt(jnp.mean(hidden * hidden, axis=1, keepdims=True) + EPS)
        return hidden, scale

    load_weights = lambda: pltpu.make_async_copy(weights_hbm.at[0:GROUPS], wg_ref, weight_sem)

    @pl.when(step == 0)
    def _():
        load_weights().start()

    if fast:

        @pl.when(step == 0)
        def _():
            greet(here)

        @pl.when(step == 1)
        def _():
            await_greetings()

    @pl.when(group == 0)
    def _():
        hidden, scale = hidden_terms()
        flipped_ref[:, lanes] = (hidden * scale * gains_ref[0:1, :]).astype(BF16).T

    @pl.when((seq == 0) & (group < GROUPS))
    def _():
        band_ref[...] = jnp.zeros_like(band_ref)

    def one_head(head):
        at = head * HEAD_DIM
        rows = lambda which: qkv_ref[0, 0, which * GROUP_ROWS + at : which * GROUP_ROWS + at + HEAD_DIM, :]
        grads = dmix_ref[0, 0, at : at + HEAD_DIM, :].astype(F32) * inv_ref[0, 0, head]
        grads = grads.astype(BF16)
        delta = jnp.sum(grads.astype(F32) * mix_ref[0, 0, at : at + HEAD_DIM, :].astype(F32), axis=0, keepdims=True)
        grad_prob = dot_tn(rows(2), grads)
        for column in range(BLOCKS):
            mine = span(column, column + 1)
            for row in range(BLOCKS):
                seen = span(row, row + 1)
                value = p_ref[0, 0, head, seen, mine].astype(F32) * (grad_prob[seen, mine] - delta[:, mine])
                band_ref[head, span(row - column + BLOCKS - 1, row - column + BLOCKS), :] += value
                ds_ref[head % 2, seen, mine] = value.astype(BF16)
        scores = ds_ref[head % 2]
        grads_ref[group, at : at + HEAD_DIM, lanes] = dot(rows(1), scores).astype(BF16)
        grads_ref[group, GROUP_ROWS + at : GROUP_ROWS + at + HEAD_DIM, lanes] = dot_nt(rows(0), scores).astype(BF16)
        grads_ref[group, 2 * GROUP_ROWS + at : 2 * GROUP_ROWS + at + HEAD_DIM, lanes] = dot_nt(grads, p_ref[0, 0, head]).astype(BF16)

    point(0)

    @pl.when(group < GROUPS)
    def _():
        one_head(0)
        one_head(1)

    @pl.when(group < GROUPS)
    def _():
        point(1)

    @pl.when(group < GROUPS)
    def _():
        one_head(2)
        one_head(3)

    @pl.when((seq == seqs - 1) & (group < GROUPS))
    def _():
        for first in range(0, width, 256):
            value = dot_nt(flipped_ref[...], grads_ref[group, first : first + 256, :]).astype(BF16)
            for owner in range(OWNERS):
                z, x, core = owner // 4, owner // 2 % 2, owner % 2
                staged_ref[z, x, core, :, first : first + 256] = value[SHARE * owner : SHARE * (owner + 1), :]
        last_fast = fast & (group == GROUPS - 1)

        @pl.when(jnp.logical_not(last_fast))
        def _():
            keep().start()

        if fast:

            @pl.when(last_fast)
            def _():
                for which in range(3):
                    tail_start(which)

        for head in range(GROUP):
            turned = band_ref[head].T
            total = jnp.zeros((8, OFFSETS), F32)
            for some in range(BLOCK // 8):
                wide = jnp.concatenate([turned[8 * some : 8 * some + 8, :], jnp.zeros((8, BLOCK), F32)], axis=1)
                total = total + pltpu.roll(wide, BLOCK - 8 * some, 1)
            line = iota((8, OFFSETS), 0)
            moved = total
            for row in range(1, 8):
                moved = jnp.where(line == row, pltpu.roll(total, OFFSETS - row, 1), moved)
            diag_ref[pl.ds(group * GROUP + head, 1)] = jnp.sum(moved, axis=0, keepdims=True)[None]
        @pl.when(jnp.logical_not(last_fast))
        def _():
            keep().wait()

    @pl.when((seq == seqs - 1) & (group == GROUPS - 1))
    def _():
        heads, buckets = table_places()
        onehot = (bucket_of(iota((OFFSETS, 1), 0) - BLOCKS * BLOCK) == buckets).astype(F32).astype(BF16)
        row = iota((16, width), 0)
        sums = jnp.concatenate([diag_ref[head] for head in range(HEADS)] + [jnp.zeros((16 - HEADS, OFFSETS), F32)], axis=0)
        high = sums.astype(BF16)
        low = (sums - high.astype(F32)).astype(BF16)
        entries = dot(high, onehot) + dot(low, onehot)
        entries = jnp.sum(jnp.where((row == heads) & (buckets >= 0), entries, 0.0), axis=0, keepdims=True)
        column = jnp.broadcast_to(entries, (BLOCK, width)).T.astype(BF16)
        for owner in range(OWNERS):
            z, x, core = owner // 4, owner // 2 % 2, owner % 2
            mine = column[SHARE * owner : SHARE * (owner + 1), :]
            small_ref[z, x, core, :, 0:BLOCK] = mine
            small_ref[z, x, core, :, BLOCK:SMALL] = mine

    @pl.when((group == GROUPS) & (seq == 0))
    def _():
        load_weights().wait()

    @pl.when(group == GROUPS)
    def _():
        hidden, scale = hidden_terms()
        flat = wg_ref[...].reshape(GROUPS, width, width)
        cotangent = sum(dot(flat[one], grads_ref[one, :, lanes]) for one in range(GROUPS)).T
        scaled = cotangent * gains_ref[0:1, :]
        unit = hidden * scale
        inner = jnp.mean(scaled * unit, axis=1, keepdims=True)
        ig_ref[...] = (gm_ref[...].astype(F32) + scale * (scaled - unit * inner)).astype(BF16)

    @pl.when(group == GROUPS)
    def _():
        point(1)

    if fast:

        @pl.when(step == (GROUPS + 1) * seqs - 1)
        def _():
            run_rest((2 * GROUPS + 2) * (flipped_ref.shape[1] // LENGTH), [BACK_SCATTER, TAIL_SCATTER], travel)


def back(x, gm, gains, weights, qkv, p, inv, mix, dmix, early, fast):
    tokens, width = x.shape
    seqs = tokens // LENGTH
    piece = (DEPTH, WIDE, CORES, SHARE, width)
    last = GROUPS - 1
    group_at = lambda g: jnp.minimum(g, last)
    seq_at = lambda g, s: jnp.where(g <= last, s, seqs - 1)
    four = lambda rows: pl.BlockSpec((1, 1, rows, LENGTH), lambda g, s: (group_at(g), seq_at(g, s), 0, 0))
    x_rows = pl.BlockSpec((LENGTH, width), lambda g, s: (jnp.where((g == 0) | (g == GROUPS), s, 0), 0))
    end_rows = pl.BlockSpec((LENGTH, width), lambda g, s: (jnp.where(g == GROUPS, s, 0), 0))
    out_specs = [end_rows, ANY, whole((DEPTH, WIDE, CORES, SHARE, SMALL))]
    out_shape = [
        jax.ShapeDtypeStruct((tokens, width), BF16), jax.ShapeDtypeStruct((GROUPS, *piece), BF16),
        jax.ShapeDtypeStruct((DEPTH, WIDE, CORES, SHARE, SMALL), BF16),
    ]
    scratch = [
        pltpu.VMEM((GROUP, BAND, BLOCK), F32), pltpu.VMEM((width, tokens), BF16), pltpu.VMEM((GROUPS, width, tokens), BF16),
        pltpu.VMEM((GROUPS, *piece), BF16), pltpu.VMEM((HEADS, 1, OFFSETS), F32), pltpu.VMEM(piece, BF16),
        pltpu.VMEM((2, LENGTH, LENGTH), BF16), pltpu.SemaphoreType.DMA,
        pltpu.SemaphoreType.DMA,
    ]
    kernel = partial(back_kernel, fast=fast)
    if fast:
        sums = BACK_SUMS
        out_specs += [whole((sums, SHARE, width)), whole((TAIL_SUMS, SHARE, SMALL))]
        out_shape += [jax.ShapeDtypeStruct((sums, SHARE, width), F32), jax.ShapeDtypeStruct((TAIL_SUMS, SHARE, SMALL), F32)]
        scratch += scatter_scratch(sums, SHARE, width) + scatter_scratch(TAIL_SUMS, SHARE, SMALL, TAIL_SUMS)
    return pl.pallas_call(
        kernel,
        name="back",
        grid=(GROUPS + 1, seqs),
        in_specs=[
            x_rows, end_rows, whole((8, width)),
            ANY, four(width),
            pl.BlockSpec((1, 1, GROUP, LENGTH, LENGTH), lambda g, s: (group_at(g), seq_at(g, s), 0, 0, 0)),
            pl.BlockSpec((1, 1, GROUP, 1, LENGTH), lambda g, s: (group_at(g), seq_at(g, s), 0, 0, 0)),
            four(GROUP_ROWS), four(GROUP_ROWS), ANY,
        ],
        out_specs=out_specs,
        out_shape=out_shape,
        scratch_shapes=scratch,
        compiler_params=pltpu.CompilerParams(
            vmem_limit_bytes=VMEM_LIMIT, collective_id=3 if fast else None, has_side_effects=fast
        ),
    )(x, gm, gains, weights, qkv, p, inv, mix, dmix, early)


def finish_kernel(
    out_ref, ig_ref, mean_ref, early_ref, late_ref, tail_ref, wq_ref, wk_ref, wv_ref, win_ref, gains_ref,
    output_ref, input_grad_ref, pooled_ref, gq_ref, gk_ref, gv_ref, go_ref, gin_ref, gout_ref, first_ref, second_ref, table_ref,
):
    output_ref[...] = out_ref[...]
    input_grad_ref[...] = ig_ref[...]
    pooled_ref[...] = mean_ref[...]
    step = pl.program_id(0)

    @pl.when(step == 0)
    def _():
        for which, target in enumerate((gq_ref, gk_ref, gv_ref)):
            mine = slice(which * GROUP_ROWS, (which + 1) * GROUP_ROWS)
            for group in range(GROUPS):
                value = tail_ref[which] if group == GROUPS - 1 else late_ref[BACK_BEFORE + group, :, mine]
                target[:, group * GROUP_ROWS : (group + 1) * GROUP_ROWS] = value
        go_ref[...] = late_ref[2 * PARTS - FEED_SUMS]

    @pl.when(step == 1)
    def _():
        for part in range(PARTS):
            piece = 2 * part + 1
            gout_ref[part * SHARE : (part + 1) * SHARE, :] = (
                early_ref[piece] if piece < FEED_SUMS else late_ref[piece - FEED_SUMS]
            )

    @pl.when(step == 2)
    def _():
        for part in range(PARTS):
            piece = 2 * part
            value = early_ref[piece] if piece < FEED_SUMS else late_ref[piece - FEED_SUMS]
            for owner in range(OWNERS):
                at = (owner * PARTS + part) * SHARE
                gin_ref[:, at : at + SHARE] = value[:, owner * SHARE : (owner + 1) * SHARE]

    @pl.when(step == pl.num_programs(0) - 1)
    def _():
        def weigh(weight_ref, grad_ref):
            return jnp.sum(weight_ref[...].astype(F32) * grad_ref[...], axis=1, keepdims=True)

        first = weigh(wq_ref, gq_ref) + weigh(wk_ref, gk_ref) + weigh(wv_ref, gv_ref)
        second = weigh(win_ref, gin_ref)
        column = iota((SHARE, BLOCK), 1)
        lines = jnp.where(column == 0, first, jnp.where(column == 1, second, tail_ref[GROUPS, :, 0:BLOCK])).T
        gains = lines[0:2, 0:SHARE] / gains_ref[0:2, 0:SHARE].astype(F32)
        first_ref[...] = gains[0:1, :]
        second_ref[...] = gains[1:2, :]
        table_ref[...] = lines[2:3, 0:TABLE_SHARE]


def finish(out, ig, mean, early, late, tail, wq, wk, wv, win, gains):
    tokens, width = out.shape
    ff = win.shape[1]
    rows = pl.BlockSpec((LENGTH, width), lambda s: (s, 0))
    means = pl.BlockSpec((1, 2, width), lambda s: (s, 0, 0))
    low = jax.ShapeDtypeStruct((tokens, width), BF16)
    square = whole((SHARE, width))
    table = lambda *shape: jax.ShapeDtypeStruct(shape, F32)
    return pl.pallas_call(
        finish_kernel,
        name="finish",
        grid=(tokens // LENGTH,),
        in_specs=[
            rows, rows, means, whole(early.shape), whole(late.shape), whole(tail.shape), square, square, square, whole((SHARE, ff)),
            whole(gains.shape),
        ],
        out_specs=[
            rows, rows, means, square, square, square, square, whole((SHARE, ff)), whole((ff // OWNERS, width)),
            whole((1, SHARE)), whole((1, SHARE)),
            whole((1, TABLE_SHARE)),
        ],
        out_shape=[
            low, low, table(*mean.shape), table(SHARE, width), table(SHARE, width), table(SHARE, width), table(SHARE, width), table(SHARE, ff),
            table(ff // OWNERS, width), table(1, SHARE), table(1, SHARE), table(1, TABLE_SHARE),
        ],
        compiler_params=pltpu.CompilerParams(vmem_limit_bytes=VMEM_LIMIT),
    )(out, ig, mean, early, late, tail, wq, wk, wv, win, gains)


def ordered(rows, w_query, w_key, w_value, w_output, w_in, w_out):
    width = w_query.shape[1]
    groups = [
        jnp.concatenate([one[:, at * GROUP_ROWS : (at + 1) * GROUP_ROWS] for one in (w_query, w_key, w_value)], axis=1)
        for at in range(GROUPS)
    ]
    inner = w_in.reshape(rows, OWNERS, PARTS, SHARE).transpose(2, 0, 1, 3).reshape(PARTS, rows, width)
    outer = w_out.reshape(-1, PARTS, SHARE, width).transpose(1, 0, 2, 3).reshape(PARTS, rows, width)
    parts = [one for at in range(PARTS) for one in (inner[at], outer[at])]
    return jnp.stack(groups + [w_output] + parts)


def small_of(gain_attn, gain_ffn, rel_table):
    lines = [one.reshape(-1, 1, share) for one, share in ((gain_attn, SHARE), (gain_ffn, SHARE), (rel_table, TABLE_SHARE))]
    padded = [jnp.pad(one, ((0, 0), (0, 0), (0, BLOCK - one.shape[2]))) for one in lines]
    return jnp.pad(jnp.concatenate(padded, axis=1), ((0, 0), (0, 13), (0, 0)))


def shards(
    hidden_in, out_grad, pooled_gradient, gain_attn, w_query, w_key, w_value, w_output, rel_table, gain_ffn, w_in, w_out,
    pair_flags, instruction_mask, *, fast,
):
    width = hidden_in.shape[1]
    own = (w_query, w_key, w_value, w_output, w_in, w_out)
    if fast:
        shares = arrange(*own)
        small = small_of(gain_attn, gain_ffn, rel_table)[0]
    else:
        gather = lambda one: lax.all_gather(one, "fsdp", axis=0, tiled=True)
        shares = ordered(width, *map(gather, own)).reshape(-1, DEPTH, WIDE, CORES, SHARE, width)
        small = small_of(*map(gather, (gain_attn, gain_ffn, rel_table)))
    flags = pair_flags.reshape(-1, 1, LENGTH)
    instr = instruction_mask.reshape(-1, 1, LENGTH)
    qkv, p, inv, mix, mid, n2, bg, gains, *rest = attend(
        hidden_in, out_grad, pooled_gradient, flags, instr, shares, small, fast
    )
    early = rest[0] if fast else shares
    output, pooled, gm, dmix, parts, *rest = feed(
        n2, bg, mid, flags, instr, gains, mix, early, shares, fast
    )
    early_sums = rest
    input_grad, group_parts, small_parts, *rest = back(hidden_in, gm, gains, early, qkv, p, inv, mix, dmix, parts, fast)
    if fast:
        *results, grad_in, grad_out, first, second, table = finish(
            output, input_grad, pooled, early_sums[0], *rest, w_query, w_key, w_value, w_in, small
        )
        output, pooled, input_grad = results[0], results[2], results[1]
        return (output, pooled, input_grad, first[0], *results[3:], table[0], second[0], grad_in, grad_out)
    sums = jnp.concatenate([parts, group_parts]).reshape(-1, width, width)
    table = small_parts.reshape(OWNERS, SHARE, SMALL)[:, :TABLE_SHARE, 0].reshape(-1)
    rows = width
    groups = [sums[2 * PARTS + 1 + at] for at in range(GROUPS)]
    grad_query, grad_key, grad_value = (
        jnp.concatenate([one[:, at * GROUP_ROWS : (at + 1) * GROUP_ROWS] for one in groups], axis=1) for at in range(3)
    )
    grad_output = sums[2 * PARTS]
    grad_in = sums[0 : 2 * PARTS : 2].reshape(PARTS, rows, OWNERS, SHARE).transpose(1, 2, 0, 3).reshape(rows, -1)
    grad_out = sums[1 : 2 * PARTS : 2].reshape(PARTS, -1, SHARE, width).transpose(1, 0, 2, 3).reshape(-1, width)
    scatter = lambda one: lax.psum(lax.psum_scatter(one, "fsdp", scatter_dimension=0, tiled=True), "grp").astype(F32)
    grad_query, grad_key, grad_value, grad_output, grad_in, grad_out, table = map(
        scatter, (grad_query, grad_key, grad_value, grad_output, grad_in, grad_out, table)
    )
    weigh = lambda weight, grad: jnp.sum(weight.astype(F32) * grad, axis=1)
    grad_gain = weigh(w_query, grad_query) + weigh(w_key, grad_key) + weigh(w_value, grad_value)
    return (
        output, pooled, input_grad, grad_gain / gain_attn.astype(F32),
        grad_query, grad_key, grad_value, grad_output, table.astype(F32),
        weigh(w_in, grad_in) / gain_ffn.astype(F32), grad_in, grad_out,
    )


def solution(mesh):
    tokens, square, line = P(("grp", "fsdp"), None), P("fsdp", None), P("fsdp")
    cube, flat = P(("grp", "fsdp"), None, None), P(("grp", "fsdp"))
    fast = mesh.shape["fsdp"] == OWNERS and mesh.shape["grp"] == 2
    return jax.shard_map(
        partial(shards, fast=fast),
        mesh=mesh,
        in_specs=(tokens, tokens, cube, line, square, square, square, square, line, line, square, square, flat, flat),
        out_specs=(tokens, cube, tokens, line, square, square, square, square, line, line, square, square),
        check_vma=False,
    )
```

```python
from functools import partial

import jax
import jax.numpy as jnp
from jax import lax
from jax.experimental import pallas as pl
from jax.experimental.pallas import tpu as pltpu
from jax.sharding import PartitionSpec as P

HEADS = 12
HEAD_DIM = 64
BUCKETS = 32
LENGTH = 512
BLOCK = 128
BLOCKS = LENGTH // BLOCK
BAND_BLOCKS = 2 * BLOCKS - 1
BAND = BAND_BLOCKS * BLOCK
OFFSETS = BAND + BLOCK
GROUPS = 3
GROUP = HEADS // GROUPS
GROUP_ROWS = GROUP * HEAD_DIM
OWNERS, PARTS, SHARE = 16, 4, 48
TABLE_SHARE = HEADS * BUCKETS // OWNERS
SMALL = 256
EPS = 1e-06
NEG = -1e30
LIMITS = (12, 16, 23, 32, 46, 64, 91)
ROOT = 0.7978845608028654
CUBE = 0.044715
F32 = jnp.float32
BF16 = jnp.bfloat16
ANY = pl.BlockSpec(memory_space=pl.ANY)
VMEM_LIMIT = 63 * 1024 * 1024


def bucket_of(offset):
    distance = jnp.abs(offset)
    far_bucket = jnp.full(offset.shape, 8, jnp.int32)
    for threshold in LIMITS:
        far_bucket = far_bucket + (distance >= threshold).astype(jnp.int32)
    near_bucket = jnp.where(distance < 8, distance, far_bucket)
    return near_bucket + BUCKETS // 2 * (offset > 0).astype(jnp.int32)


def dot(a, b):
    return lax.dot_general(a, b, (((1,), (0,)), ((), ())), preferred_element_type=F32)


def dot_nt(a, b):
    return lax.dot_general(a, b, (((1,), (1,)), ((), ())), preferred_element_type=F32)


def dot_tn(a, b):
    return lax.dot_general(a, b, (((0,), (0,)), ((), ())), preferred_element_type=F32)


def dot_tt(a, b):
    return lax.dot_general(a, b, (((0,), (1,)), ((), ())), preferred_element_type=F32)


def iota(shape, axis):
    return lax.broadcasted_iota(jnp.int32, shape, axis)


def whole(shape):
    zeros = (0,) * len(shape)
    return pl.BlockSpec(shape, lambda *_: zeros, pipeline_mode=pl.Buffered(1))


def span(first, last):
    return slice(first * BLOCK, last * BLOCK)


def pool_terms(flags, instruction):
    kept = (instruction == 0).astype(F32)
    chosen = [kept * (flags == part).astype(F32) for part in range(2)]
    counts = [jnp.sum(one, axis=1, keepdims=True) for one in chosen]
    return chosen, counts


def pool_gradient(chosen, counts, pooled_grad):
    row = iota((16, LENGTH), 0)
    picks = jnp.where(row % 2 == 0, chosen[0], chosen[1])
    picks = jnp.where(row < 6, picks, 0.0).astype(BF16)
    scaled = [pooled_grad[part : part + 1, :] / counts[part] for part in range(2)]
    line = iota((16, pooled_grad.shape[1]), 0)
    both = jnp.where(line % 2 == 0, scaled[0], scaled[1])
    high = both.astype(BF16).astype(F32)
    rest = both - high
    middle = rest.astype(BF16).astype(F32)
    low = rest - middle
    parts = jnp.where(line < 2, high, jnp.where(line < 4, middle, jnp.where(line < 6, low, 0.0)))
    return dot_tn(picks, parts.astype(BF16))


def norm_back(value, gain, cotangent):
    scale = lax.rsqrt(jnp.mean(value * value, axis=1, keepdims=True) + EPS)
    scaled = cotangent * gain
    unit = value * scale
    inner = jnp.mean(scaled * unit, axis=1, keepdims=True)
    return scale * (scaled - unit * inner), jnp.sum(cotangent * unit, axis=0, keepdims=True)


def owners_of():
    at = iota((1, OWNERS * SHARE), 1)
    owner = sum((at >= SHARE * one).astype(jnp.int32) for one in range(1, OWNERS))
    return owner, at - SHARE * owner


def table_places():
    owner, inside = owners_of()
    entry = owner * TABLE_SHARE + inside
    bucket = sum((entry >= HEADS * one).astype(jnp.int32) for one in range(1, BUCKETS))
    return entry - HEADS * bucket, jnp.where(inside < TABLE_SHARE, bucket, -1)


DEPTH, WIDE, CORES = 4, 2, 2
MESH_ID = pl.DeviceIdType.MESH


def place():
    grp, at = lax.axis_index("grp"), lax.axis_index("fsdp")
    z, x, core = lax.div(at, WIDE * CORES), lax.rem(lax.div(at, CORES), WIDE), lax.rem(at, CORES)

    def device(grp, z, x, core):
        return (grp, z * (WIDE * CORES) + x * CORES + core)

    return dict(
        at=at, y=grp, z=z, x=x, core=core,
        over_y=device(1 - grp, z, x, core),
        over_x=device(grp, z, 1 - x, core),
        over_core=device(grp, z, x, 1 - core),
        over_z=[device(grp, lax.rem(z + one, DEPTH), x, core) for one in range(1, DEPTH)],
        ahead=[lax.rem(z + one, DEPTH) for one in range(1, DEPTH)],
        behind=[lax.rem(z + DEPTH - one, DEPTH) for one in range(1, DEPTH)],
    )


def greet(here):
    barrier = pltpu.get_barrier_semaphore()
    for device in (here["over_y"], here["over_x"], here["over_core"], *here["over_z"]):
        pl.semaphore_signal(barrier, inc=1, device_id=device, device_id_type=MESH_ID)


def await_greetings():
    pl.semaphore_wait(pltpu.get_barrier_semaphore(), DEPTH + 2)


def others(here):
    at = here["at"]
    for one in range(1, OWNERS):
        yield one, (here["y"], lax.rem(at + one, OWNERS)), lax.rem(at + OWNERS - one, OWNERS)


def greet_all(here):
    barrier = pltpu.get_barrier_semaphore()
    pl.semaphore_signal(barrier, inc=1, device_id=here["over_y"], device_id_type=MESH_ID)
    for _, device, _ in others(here):
        pl.semaphore_signal(barrier, inc=1, device_id=device, device_id_type=MESH_ID)
    pl.semaphore_wait(barrier, OWNERS)


def gather_phase(phase, sem, here, share_ref, whole_ref, sent, got, own_sem, shared=False):
    z, x, core = here["z"], here["x"], here["core"]
    every = slice(None)
    half = share_ref.shape[-1] // 2
    lanes = pl.ds(pl.multiple_of(here["y"] * half, half), half) if shared else every
    other = pl.ds(pl.multiple_of((1 - here["y"]) * half, half), half) if shared else every
    mine = share_ref.at[:, lanes] if shared else share_ref

    def copy(source, where, channel, device):
        return pltpu.make_async_remote_copy(
            src_ref=source, dst_ref=whole_ref.at[where], send_sem=sent.at[channel, sem], recv_sem=got.at[channel, sem],
            device_id=device, device_id_type=MESH_ID,
        )

    def same(where, channel, device):
        return copy(whole_ref.at[where], where, channel, device)

    own = lambda: pltpu.make_async_copy(mine, whole_ref.at[z, x, core, every, lanes], own_sem.at[sem])
    line_out = lambda one: copy(mine, (z, x, core, every, lanes), one, here["over_z"][one])
    line_in = lambda one: copy(mine, (here["behind"][one], x, core, every, lanes), one, here["over_z"][one])
    side_out = lambda: same((every, x, core, every, lanes), 3, here["over_x"])
    side_in = lambda: same((every, 1 - x, core, every, lanes), 3, here["over_x"])
    group_out = lambda: same((every, every, core, every, lanes), 5, here["over_y"])
    group_in = lambda: same((every, every, core, every, other), 5, here["over_y"])
    core_out = lambda: same((every, every, core), 4, here["over_core"])
    core_in = lambda: same((every, every, 1 - core), 4, here["over_core"])
    if phase == 0:
        own().start()
        for one in range(DEPTH - 1):
            line_out(one).start()
    elif phase == 1:
        own().wait()
        for one in range(DEPTH - 1):
            line_in(one).wait_recv()
        side_out().start()
    elif phase == 2:
        side_in().wait_recv()
        group_out().start()
    elif phase == 3:
        if shared:
            group_in().wait_recv()
        else:
            side_in().wait_recv()
        core_out().start()
    else:
        for one in range(DEPTH - 1):
            line_out(one).wait_send()
        side_out().wait_send()
        if shared:
            group_out().wait_send()
        core_out().wait_send()
        core_in().wait_recv()


def scatter_phase(phase, piece, here, part_ref, out_ref, own, fromc, fromx, fromz, last, sent, got, own_sem):
    z, x, core = here["z"], here["x"], here["core"]
    slot = lax.rem(piece, own.shape[0])

    def remote(source, target, channel, device):
        return pltpu.make_async_remote_copy(
            src_ref=source, dst_ref=target, send_sem=sent.at[channel, piece], recv_sem=got.at[channel, piece],
            device_id=device, device_id_type=MESH_ID,
        )

    total = fromc.at[piece]
    over_core = lambda: remote(part_ref.at[:, :, 1 - core], total, 0, here["over_core"])
    load = lambda: pltpu.make_async_copy(part_ref.at[:, :, core], own.at[slot], own_sem.at[slot])
    over_x = lambda: remote(fromc.at[piece, :, 1 - x], fromx.at[piece], 1, here["over_x"])
    line_out = lambda one: remote(fromc.at[piece, here["ahead"][one], x], fromz.at[piece, z], 2 + one, here["over_z"][one])
    line_in = lambda one: remote(
        fromc.at[piece, z, x], fromz.at[piece, here["behind"][one]], 2 + one, here["over_z"][one]
    )
    final = lambda: remote(fromc.at[piece, z, x], last.at[piece], 5, here["over_y"])

    if phase == 0:
        over_core().start()
        load().start()
    elif phase == 1:
        load().wait()
        over_core().wait()

        def one(at, _):
            for side in range(WIDE):
                fromc[piece, at, side] = own[slot, at, side] + fromc[piece, at, side]
            return 0

        lax.fori_loop(0, DEPTH, one, 0)
        over_x().start()
    elif phase == 2:
        over_x().wait()

        def one(at, _):
            fromc[piece, at, x] = fromc[piece, at, x] + fromx[piece, at]
            return 0

        lax.fori_loop(0, DEPTH, one, 0)
        for one in range(DEPTH - 1):
            line_out(one).start()
    elif phase == 3:
        mine = fromc[piece, z, x].astype(F32)
        for one in range(DEPTH - 1):
            line_in(one).wait_recv()
            mine = mine + fromz[piece, here["behind"][one]].astype(F32)
        fromc[piece, z, x] = mine.astype(BF16)
        final().start()
    else:
        for one in range(DEPTH - 1):
            line_out(one).wait_send()
        final().wait()
        out_ref[piece] = fromc[piece, z, x].astype(F32) + last[piece].astype(F32)


def run_slot(slot, table, act):
    for phase in reversed(range(max(map(len, table.values())))):
        due, found = False, 0
        for piece, slots in table.items():
            if slots[phase] is not None:
                now = slot == slots[phase]
                due, found = due | now, jnp.where(now, piece, found)
        if due is not False:

            @pl.when(due)
            def _(phase=phase, found=found):
                act(phase, found)


def run_rest(first, tables, travel):
    end = 1 + max(slot for table in tables for slots in table.values() for slot in slots if slot is not None)

    def one(slot, _):
        travel(slot)
        return 0

    if end > first:
        lax.fori_loop(first, end, one, 0)


def gather_sems(pieces):
    return [pltpu.SemaphoreType.DMA((6, pieces)), pltpu.SemaphoreType.DMA((6, pieces)), pltpu.SemaphoreType.DMA((pieces,))]


def scatter_scratch(pieces, rows, columns, places=2):
    return [
        pltpu.VMEM((places, DEPTH, WIDE, rows, columns), BF16),
        pltpu.VMEM((pieces, DEPTH, WIDE, rows, columns), BF16),
        pltpu.VMEM((pieces, DEPTH, rows, columns), BF16),
        pltpu.VMEM((pieces, DEPTH, rows, columns), BF16),
        pltpu.VMEM((pieces, rows, columns), BF16),
        pltpu.SemaphoreType.DMA((6, pieces)),
        pltpu.SemaphoreType.DMA((6, pieces)),
        pltpu.SemaphoreType.DMA((places,)),
    ]


ATTEND_PIECES, FEED_PIECES = 8, 4
ATTEND_DIRECT = {2: (0, 6, None, 12, 14), 3: (3, 9, None, 15, 17), 5: (9, 14, None, 20, 22), 7: (14, 19, None, 25, 26)}
ATTEND_SHARED = {1: (None, None, 0, 5, 7), 4: (7, 12, 16, 21, 23), 6: (12, 17, 21, 24, 25)}
FEED_DIRECT = {1: (1, 7, None, 12, 15), 3: (6, 12, None, 18, 20)}
FEED_SHARED = {0: (0, 4, 7, 11, 14), 2: (5, 8, 15, 19, 21)}
FEED_SUMS = 5
FEED_SCATTER = {0: (8, 13, 18, 24, 26), 1: (11, 15, 21, 26, 28), 2: (16, 18, 24, 31, 32), 3: (19, 21, 27, 32, 35), 4: (24, 26, 31, 37, 40)}
BACK_BEFORE, BACK_SUMS = 4, 6
BACK_SCATTER = {
    0: (2, 4, 8, 13, 15), 1: (4, 6, 11, 16, 18), 2: (6, 9, 14, 19, 21), 3: (9, 12, 17, 22, 24),
    4: (12, 14, 19, 24, 27), 5: (16, 18, 23, 27, 29),
}
TAIL_SUMS = 4
TAIL_SCATTER = {0: (None, 24, 26, 28, 30), 1: (None, 25, 27, 29, 31), 2: (None, 26, 28, 30, 32), 3: (24, 27, 29, 31, 33)}


def arrange_kernel(wq_ref, wk_ref, wv_ref, wo_ref, win_ref, wout_ref, shares_ref, line_ref):
    for group in range(GROUPS):
        mine = slice(group * GROUP_ROWS, (group + 1) * GROUP_ROWS)
        for which, one in enumerate((wq_ref, wk_ref, wv_ref)):
            shares_ref[group, :, which * GROUP_ROWS : (which + 1) * GROUP_ROWS] = one[:, mine]
    shares_ref[GROUPS] = wo_ref[...]
    for part in range(PARTS):
        for owner in range(OWNERS):
            at = (owner * PARTS + part) * SHARE
            line_ref[:, owner * SHARE : (owner + 1) * SHARE] = win_ref[:, at : at + SHARE].astype(F32)
        shares_ref[GROUPS + 1 + 2 * part] = line_ref[...].astype(BF16)
        shares_ref[GROUPS + 2 + 2 * part] = wout_ref[part * SHARE : (part + 1) * SHARE, :]


def arrange(*weights):
    width = weights[0].shape[1]
    return pl.pallas_call(
        arrange_kernel,
        name="arrange",
        out_shape=jax.ShapeDtypeStruct((GROUPS + 1 + 2 * PARTS, SHARE, width), BF16),
        scratch_shapes=[pltpu.VMEM((SHARE, width), F32)],
    )(*weights)


def attend_kernel(
    x_hbm, og_hbm, pg_ref, flags_ref, instr_ref, shares_hbm, small_hbm,
    qkv_ref, p_ref, inv_ref, mix_ref, mid_ref, n2_ref, bg_hbm, gains_ref, weights_hbm,
    x_ref, bg_ref, mixed_ref, band_ref, aux_ref, normed_ref, wg_ref, wo_ref, small_ref, table_ref, cur_ref, nxt_ref, sa_ref, sb_ref,
    sems, *comm, fast,
):
    group, seq = pl.program_id(0), pl.program_id(1)
    seqs = pl.num_programs(1)
    step = group * seqs + seq
    width = x_ref.shape[1]
    if fast:
        main_sems, first_sems, small_sent, small_got = comm[0:3], comm[3:6], comm[6], comm[7]
        here = place()

        def main(phase, piece, shared=False):
            gather_phase(phase, piece, here, shares_hbm.at[piece], weights_hbm.at[piece], *main_sems, shared=shared)

        def small(start):
            for one, device, source in others(here):
                copy = lambda where: pltpu.make_async_remote_copy(
                    src_ref=small_hbm, dst_ref=small_ref.at[where], send_sem=small_sent.at[one], recv_sem=small_got.at[one],
                    device_id=device, device_id_type=MESH_ID,
                )
                if start:
                    copy(here["at"]).start()
                else:
                    copy(source).wait_recv()
                    copy(here["at"]).wait_send()

        def first(phase, which):
            lanes = pl.ds(which * GROUP_ROWS, GROUP_ROWS)
            every = slice(None)
            gather_phase(
                phase, which, here, shares_hbm.at[0, :, lanes], weights_hbm.at[0, every, every, every, every, lanes], *first_sems
            )

        def travel(slot):
            run_slot(slot, ATTEND_DIRECT, main)
            run_slot(slot, ATTEND_SHARED, partial(main, shared=True))

        point = lambda at: travel(2 * step + at)
    else:
        point = lambda at: None
    small_own = small_ref.at[here["at"]] if fast else small_ref
    load_small = lambda: pltpu.make_async_copy(small_hbm, small_own, sems.at[0])
    load_hidden = lambda: pltpu.make_async_copy(x_hbm, x_ref, sems.at[3])
    load_grad = lambda: pltpu.make_async_copy(og_hbm, bg_ref, sems.at[4])
    keep_grad = lambda: pltpu.make_async_copy(bg_ref, bg_hbm, sems.at[4])
    load_group = lambda at: pltpu.make_async_copy(weights_hbm.at[at], wg_ref, sems.at[1])
    load_output = lambda: pltpu.make_async_copy(weights_hbm.at[GROUPS], wo_ref, sems.at[2])
    square = lambda ref: ref[...].reshape(width, width)

    def prepare(at):
        flags = flags_ref[at]
        chosen, counts = pool_terms(flags, instr_ref[at])
        rows = pl.ds(pl.multiple_of(at * LENGTH, LENGTH), LENGTH)
        bg_ref[rows, :] = (bg_ref[rows, :].astype(F32) + pool_gradient(chosen, counts, pg_ref[at])).astype(BF16)
        row = iota((16, LENGTH), 0)
        aux_ref[0, at] = jnp.where(row == 0, 1 - flags, jnp.where(row == 1, flags, 0)).astype(F32).astype(BF16)
        other = jnp.where(row == 0, flags, jnp.where(row == 1, 1 - flags, 0)).astype(F32) * NEG
        aux_ref[1, at] = other.astype(BF16)

    def normalize(at):
        rows = pl.ds(pl.multiple_of(at * LENGTH, LENGTH), LENGTH)
        hidden = x_ref[rows, :].astype(F32)
        scale = lax.rsqrt(jnp.mean(hidden * hidden, axis=1, keepdims=True) + EPS)
        normed_ref[at] = (hidden * scale * gains_ref[0:1, :]).astype(BF16)

    def every_seq(act):
        def one_seq(at, _):
            act(at)
            return 0

        lax.fori_loop(0, seqs, one_seq, 0)

    def project(at, target):
        target[...] = dot_tt(square(wg_ref), normed_ref[at]).astype(BF16)

    def part(source, which, head):
        first = which * GROUP_ROWS + head * HEAD_DIM
        return source[first : first + HEAD_DIM, :]

    def score(source, at_group, at, head, target):
        queries = jnp.concatenate([part(source, 0, head), aux_ref[0, at]], axis=0)
        keys = jnp.concatenate([part(source, 1, head), aux_ref[1, at]], axis=0)
        scores = dot_tn(keys, queries)
        for row in range(BLOCKS):
            for column in range(BLOCKS):
                bias = band_ref[at_group * GROUP + head, span(row - column + BLOCKS - 1, row - column + BLOCKS), :]
                target[span(row, row + 1), span(column, column + 1)] = scores[span(row, row + 1), span(column, column + 1)] + bias

    def soften(head, source):
        scores = source[...]
        exponent = jnp.exp(scores - jnp.max(scores, axis=0, keepdims=True)).astype(BF16)
        p_ref[0, 0, head] = exponent
        values = jnp.concatenate([part(cur_ref, 2, head), jnp.ones((16, LENGTH), BF16)], axis=0)
        mixed = dot(values, exponent)
        inverse = 1.0 / mixed[HEAD_DIM : HEAD_DIM + 1, :]
        inv_ref[0, 0, head] = inverse
        mixed = (mixed[0:HEAD_DIM, :] * inverse).astype(BF16)
        mix_ref[0, 0, head * HEAD_DIM : (head + 1) * HEAD_DIM, :] = mixed
        mixed_ref[seq, pl.ds(pl.multiple_of(group * GROUP_ROWS + head * HEAD_DIM, HEAD_DIM), HEAD_DIM), :] = mixed

    def read_small():
        owner, inside = owners_of()
        spread = (iota((BLOCK, width), 0) == inside).astype(F32).astype(BF16)
        shares = small_ref[...].astype(F32)

        def line(which):
            placed = dot(shares[:, which, :].astype(BF16), spread)
            return jnp.sum(jnp.where(iota((OWNERS, width), 0) == owner, placed, 0.0), axis=0, keepdims=True)

        row = iota((8, width), 0)
        gains_ref[...] = jnp.where(row == 0, line(0), line(1))
        table_row = line(2)
        heads, buckets = table_places()
        entries = jnp.where((iota((16, width), 0) == heads) & (buckets >= 0), table_row, 0.0).astype(BF16)
        onehot = (bucket_of(iota((OFFSETS, 1), 0) - BLOCKS * BLOCK) == buckets).astype(F32).astype(BF16)
        table_ref[...] = dot_nt(entries, onehot)

    def make_bands(at_group):
        def one_head(head, _):
            table = table_ref[...]
            line = jnp.sum(jnp.where(iota(table.shape, 0) == head, table, 0.0), axis=0, keepdims=True)
            turned = pltpu.roll(jnp.broadcast_to(line, (BLOCK, OFFSETS)), 0, 1, stride=1, stride_axis=0)
            band_ref[head] = turned[:, BLOCK:].T
            return 0

        lax.fori_loop(at_group * GROUP, (at_group + 1) * GROUP, one_head, 0)

    @pl.when(step == 0)
    def _():
        load_grad().start()
        load_hidden().start()
        load_small().start()
        if fast:
            greet_all(here)
            small(True)
            for which in range(3):
                first(0, which)
        load_grad().wait()
        every_seq(prepare)
        keep_grad().start()
        load_hidden().wait()
        load_small().wait()
        if fast:
            small(False)
            first(1, 0)
            main(0, 1, shared=True)
            read_small()
            first(1, 1)
            normalize(0)
            normalize(1)
            first(1, 2)
            normalize(2)
            normalize(3)
            first(3, 0)
            make_bands(0)
            first(3, 1)
            main(1, 1, shared=True)
            make_bands(1)
            first(3, 2)
            make_bands(2)
            for which in range(3):
                first(4, which)
        else:
            read_small()
            every_seq(normalize)
            for one in range(GROUPS):
                make_bands(one)
        load_group(0).start()
        load_group(0).wait()
        project(0, nxt_ref)
        score(nxt_ref, 0, 0, 0, sa_ref)

    last_seq = seq == seqs - 1
    more = step + 1 < GROUPS * seqs
    cur_ref[...] = nxt_ref[...]

    next_seq = jnp.where(last_seq, 0, seq + 1)
    next_group = jnp.where(last_seq, jnp.minimum(group + 1, GROUPS - 1), group)
    point(0)
    qkv_ref[0, 0] = cur_ref[...]
    score(cur_ref, group, seq, 1, sb_ref)
    soften(0, sa_ref)
    score(cur_ref, group, seq, 2, sa_ref)
    soften(1, sb_ref)
    point(1)
    score(cur_ref, group, seq, 3, sb_ref)
    soften(2, sa_ref)

    @pl.when(last_seq & more)
    def _():
        load_group(group + 1).start()
        load_group(group + 1).wait()

    project(next_seq, nxt_ref)
    score(nxt_ref, next_group, next_seq, 0, sa_ref)
    soften(3, sb_ref)

    @pl.when((seq == 0) & (group == GROUPS - 1))
    def _():
        load_output().start()
        load_output().wait()

    @pl.when(group == GROUPS - 1)
    def _():
        rows = pl.ds(pl.multiple_of(seq * LENGTH, LENGTH), LENGTH)
        middle = x_ref[rows, :].astype(F32) + dot_tn(mixed_ref[seq], square(wo_ref))
        mid_ref[...] = middle
        scale = lax.rsqrt(jnp.mean(middle * middle, axis=1, keepdims=True) + EPS)
        n2_ref[...] = (middle * scale * gains_ref[1:2, :]).astype(BF16)

    @pl.when(step == GROUPS * seqs - 1)
    def _():
        keep_grad().wait()
        if fast:
            run_rest(2 * GROUPS * (x_ref.shape[0] // LENGTH), [ATTEND_DIRECT, ATTEND_SHARED], travel)


def attend(x, og, pg, flags, instr, shares, small, fast):
    tokens, width = x.shape
    seqs = tokens // LENGTH
    last_rows = pl.BlockSpec((LENGTH, width), lambda g, s: (jnp.where(g == GROUPS - 1, s, 0), 0))
    low = jax.ShapeDtypeStruct((tokens, width), BF16)
    out_specs = [
        pl.BlockSpec((1, 1, width, LENGTH), lambda g, s: (g, s, 0, 0)),
        pl.BlockSpec((1, 1, GROUP, LENGTH, LENGTH), lambda g, s: (g, s, 0, 0, 0)),
        pl.BlockSpec((1, 1, GROUP, 1, LENGTH), lambda g, s: (g, s, 0, 0, 0)),
        pl.BlockSpec((1, 1, GROUP_ROWS, LENGTH), lambda g, s: (g, s, 0, 0)), last_rows, last_rows, ANY, whole((8, width)),
    ]
    out_shape = [
        jax.ShapeDtypeStruct((GROUPS, seqs, width, LENGTH), BF16),
        jax.ShapeDtypeStruct((GROUPS, seqs, GROUP, LENGTH, LENGTH), BF16),
        jax.ShapeDtypeStruct((GROUPS, seqs, GROUP, 1, LENGTH), F32),
        jax.ShapeDtypeStruct((GROUPS, seqs, GROUP_ROWS, LENGTH), BF16),
        jax.ShapeDtypeStruct((tokens, width), F32), low, low, jax.ShapeDtypeStruct((8, width), F32),
    ]
    scratch = [
        pltpu.VMEM((tokens, width), BF16), pltpu.VMEM((tokens, width), BF16), pltpu.VMEM((seqs, width, LENGTH), BF16),
        pltpu.VMEM((HEADS, BAND, BLOCK), F32), pltpu.VMEM((2, seqs, 16, LENGTH), BF16),
        pltpu.VMEM((seqs, LENGTH, width), BF16), pltpu.VMEM((DEPTH, WIDE, CORES, SHARE, width), BF16),
        pltpu.VMEM((DEPTH, WIDE, CORES, SHARE, width), BF16), pltpu.VMEM((OWNERS, 16, BLOCK), BF16), pltpu.VMEM((16, OFFSETS), F32),
        pltpu.VMEM((width, LENGTH), BF16), pltpu.VMEM((width, LENGTH), BF16),
        pltpu.VMEM((LENGTH, LENGTH), F32), pltpu.VMEM((LENGTH, LENGTH), F32), pltpu.SemaphoreType.DMA((5,)),
    ]
    in_specs = [
        ANY, ANY, whole((seqs, 2, width)), whole((seqs, 1, LENGTH)), whole((seqs, 1, LENGTH)), ANY, ANY,
    ]
    if fast:
        kernel = partial(attend_kernel, fast=True)
        out_specs += [ANY]
        out_shape += [jax.ShapeDtypeStruct((ATTEND_PIECES, DEPTH, WIDE, CORES, SHARE, width), BF16)]
        scratch += gather_sems(ATTEND_PIECES) + gather_sems(3) + [pltpu.SemaphoreType.DMA((OWNERS,)), pltpu.SemaphoreType.DMA((OWNERS,))]
    else:

        def kernel(*refs):
            inputs, outputs, rest = refs[:7], refs[7:15], refs[15:]
            attend_kernel(*inputs, *outputs, inputs[5], *rest, fast=False)

    return pl.pallas_call(
        kernel,
        name="attend",
        grid=(GROUPS, seqs),
        in_specs=in_specs,
        out_specs=out_specs,
        out_shape=out_shape,
        scratch_shapes=scratch,
        compiler_params=pltpu.CompilerParams(
            vmem_limit_bytes=VMEM_LIMIT, collective_id=1 if fast else None, has_side_effects=fast
        ),
    )(x, og, pg, flags, instr, shares, small)


def feed_kernel(
    n2_hbm, bg_hbm, mid_hbm, flags_ref, instr_ref, gains_ref, mid_ref, mix_ref, early_hbm, late_hbm,
    out_ref, pooled_ref, gm_ref, dmix_ref, parts_hbm, *rest, fast,
):
    if fast:
        sums_ref, gathered_hbm = rest[0:2]
        rest = rest[2:]
    n2_ref, bg_ref, res_ref, dn2_ref, act_ref, dinner_ref, win_ref, wout_ref, wo_ref, dwo_ref, staged_ref, sems, block_sems = rest[:13]
    part, block = pl.program_id(0), pl.program_id(1)
    blocks = pl.num_programs(1)
    step = part * blocks + block
    width = res_ref.shape[1]
    rows = pl.ds(pl.multiple_of(block * LENGTH, LENGTH), LENGTH)
    if fast:
        sems_of, scratch = rest[13:16], rest[16:]
        here = place()

        def travel(slot):
            def bring(phase, piece, shared=False):
                share = late_hbm.at[ATTEND_PIECES + piece]
                gather_phase(phase, piece, here, share, gathered_hbm.at[piece], *sems_of, shared=shared)

            def add(phase, piece):
                scatter_phase(phase, piece, here, parts_hbm.at[piece], sums_ref, *scratch)

            run_slot(slot, FEED_DIRECT, bring)
            run_slot(slot, FEED_SHARED, partial(bring, shared=True))
            run_slot(slot, FEED_SCATTER, add)

        point = lambda at: travel(2 * step + at)
    else:
        point = lambda at: None
    square = lambda ref: ref[...].reshape(width, width)

    def weights(at, start):
        def both(source, first):
            for which, target in enumerate((win_ref, wout_ref)):
                slot = lax.rem(at, 2)
                copy = pltpu.make_async_copy(source.at[first + which], target.at[slot], sems.at[slot, which])
                copy.start() if start else copy.wait()

        if start:
            pl.when(at < PARTS // 2)(lambda: both(early_hbm, 4 + 2 * at))
            pl.when(at >= PARTS // 2)(lambda: both(gathered_hbm if fast else late_hbm, 2 * at + (-PARTS if fast else 4)))
        else:
            both(early_hbm, 4)


    def load_block(at, start):
        mine = pl.ds(pl.multiple_of(at * LENGTH, LENGTH), LENGTH)
        for which, (source, target) in enumerate(((n2_hbm, n2_ref), (bg_hbm, bg_ref), (mid_hbm, res_ref))):
            copy = pltpu.make_async_copy(source.at[mine], target.at[mine], block_sems.at[which, at])
            copy.start() if start else copy.wait()

    load_output = lambda: pltpu.make_async_copy(early_hbm.at[GROUPS], wo_ref, sems.at[1, 2])
    keep = lambda at, which: pltpu.make_async_copy(staged_ref.at[which], parts_hbm.at[2 * at + which], sems.at[which, 3])

    @pl.when(step == 0)
    def _():
        if fast:
            greet(here)
        weights(0, True)
        for at in range(res_ref.shape[0] // LENGTH):
            load_block(at, True)
        load_output().start()
        dwo_ref[...] = jnp.zeros_like(dwo_ref)

    @pl.when((part == PARTS) & (block == 0))
    def _():
        load_output().wait()

    @pl.when(part == 0)
    def _():
        dn2_ref[rows, :] = jnp.zeros((LENGTH, width), F32)
        load_block(block, False)

    @pl.when((part < PARTS) & (block == 0))
    def _():
        weights(part, False)

    @pl.when((part > 0) & (block == 0))
    def _():
        keep(part - 1, 0).wait()
        keep(part - 1, 1).wait()

    if fast:

        @pl.when(step == 0)
        def _():
            await_greetings()

    point(0)

    @pl.when(part < PARTS)
    def _():
        slot = lax.rem(part, 2)
        inner = dot(n2_ref[rows, :], square(win_ref.at[slot]))
        grad_active = dot_nt(bg_ref[rows, :], square(wout_ref.at[slot]))
        squared = inner * inner
        half = 0.5 * jnp.tanh(inner * (ROOT + (ROOT * CUBE) * squared)) + 0.5
        active = inner * half
        slope = half + active * (1.0 - half) * (2.0 * ROOT + (6.0 * ROOT * CUBE) * squared)
        active = active.astype(BF16)
        act_ref[rows, :] = active
        dinner = (grad_active * slope).astype(BF16)
        dinner_ref[rows, :] = dinner
        res_ref[rows, :] += dot(active, square(wout_ref.at[slot]))
        dn2_ref[rows, :] += dot_nt(dinner, square(win_ref.at[slot]))

    point(1)

    @pl.when((part < PARTS - 1) & (block == blocks - 1))
    def _():
        weights(part + 1, True)

    def stage(which, first, value):
        for owner in range(OWNERS):
            z, x, core = owner // 4, owner // 2 % 2, owner % 2
            staged_ref[which, z, x, core, :, first : first + 256] = value[SHARE * owner : SHARE * (owner + 1), :]

    @pl.when((part < PARTS) & (block == blocks - 1))
    def _():
        for first in range(0, width, 256):
            stage(0, first, dot_tn(n2_ref[...], dinner_ref[:, first : first + 256]).astype(BF16))
        keep(part, 0).start()
        for first in range(0, width, 256):
            stage(1, first, dot_tn(act_ref[...], bg_ref[:, first : first + 256]).astype(BF16))
        keep(part, 1).start()

    @pl.when(part == PARTS)
    def _():
        result = res_ref[rows, :]
        out_ref[...] = result.astype(BF16)
        chosen, counts = pool_terms(flags_ref[block], instr_ref[block])
        line = iota((8, LENGTH), 0)
        picks = jnp.where(line == 0, chosen[0], jnp.where(line == 1, chosen[1], 0.0)).astype(BF16)
        high = result.astype(BF16)
        low = (result - high.astype(F32)).astype(BF16)
        total = dot(picks, high) + dot(picks, low)
        total = total / jnp.where(iota((8, 1), 0) == 0, counts[0], counts[1])
        pooled_ref[block] = total[0:2, :]
        change, _ = norm_back(mid_ref[...], gains_ref[1:2, :], dn2_ref[rows, :])
        out_low = (bg_ref[rows, :].astype(F32) + change).astype(BF16)
        gm_ref[...] = out_low
        output = square(wo_ref)
        for group in range(GROUPS):
            mine = slice(group * GROUP_ROWS, (group + 1) * GROUP_ROWS)
            dmix_ref[group, 0] = dot_nt(output[mine, :], out_low).astype(BF16)
            dwo_ref[mine, :] += dot(mix_ref[group, 0], out_low)

    @pl.when(step == (PARTS + 1) * blocks - 1)
    def _():
        for first in range(0, width, 256):
            stage(0, first, dwo_ref[:, first : first + 256].astype(BF16))
        keep(PARTS, 0).start()
        if fast:
            run_rest(2 * (PARTS + 1) * (res_ref.shape[0] // LENGTH), [FEED_DIRECT, FEED_SHARED, FEED_SCATTER], travel)
        keep(PARTS, 0).wait()


def feed(n2, bg, mid, flags, instr, gains, mix, early, late, fast):
    tokens, width = n2.shape
    seqs = tokens // LENGTH
    rows = pl.BlockSpec((LENGTH, width), lambda c, m: (jnp.where(c == PARTS, m, 0), 0))
    heads = pl.BlockSpec((GROUPS, 1, GROUP_ROWS, LENGTH), lambda c, m: (0, jnp.where(c == PARTS, m, 0), 0, 0))
    piece = (DEPTH, WIDE, CORES, SHARE, width)
    sums = FEED_SUMS
    out_specs = [rows, whole((seqs, 2, width)), rows, heads, ANY]
    out_shape = [
        jax.ShapeDtypeStruct((tokens, width), BF16), jax.ShapeDtypeStruct((seqs, 2, width), F32),
        jax.ShapeDtypeStruct((tokens, width), BF16), jax.ShapeDtypeStruct((GROUPS, seqs, GROUP_ROWS, LENGTH), BF16),
        jax.ShapeDtypeStruct((2 * PARTS + 1, *piece), BF16),
    ]
    scratch = [
        pltpu.VMEM((tokens, width), BF16), pltpu.VMEM((tokens, width), BF16),
        pltpu.VMEM((tokens, width), F32), pltpu.VMEM((tokens, width), F32), pltpu.VMEM((tokens, width), BF16),
        pltpu.VMEM((tokens, width), BF16), pltpu.VMEM((2, *piece), BF16), pltpu.VMEM((2, *piece), BF16),
        pltpu.VMEM(piece, BF16), pltpu.VMEM((width, width), F32), pltpu.VMEM((2, *piece), BF16), pltpu.SemaphoreType.DMA((2, 4)),
        pltpu.SemaphoreType.DMA((3, seqs)),
    ]
    if fast:
        out_specs += [whole((sums, SHARE, width)), ANY]
        out_shape += [
            jax.ShapeDtypeStruct((sums, SHARE, width), F32), jax.ShapeDtypeStruct((FEED_PIECES, *piece), BF16)
        ]
        scratch += gather_sems(FEED_PIECES) + scatter_scratch(sums, SHARE, width)
    return pl.pallas_call(
        partial(feed_kernel, fast=fast),
        name="feed",
        grid=(PARTS + 1, seqs),
        in_specs=[
            ANY, ANY, ANY, whole((seqs, 1, LENGTH)), whole((seqs, 1, LENGTH)), whole((8, width)), rows, heads, ANY, ANY,
        ],
        out_specs=out_specs,
        out_shape=out_shape,
        scratch_shapes=scratch,
        compiler_params=pltpu.CompilerParams(
            vmem_limit_bytes=VMEM_LIMIT, collective_id=2 if fast else None, has_side_effects=fast
        ),
    )(n2, bg, mid, flags, instr, gains, mid, mix, early, late)


def back_kernel(
    x_ref, gm_ref, gains_ref, weights_hbm, qkv_ref, p_ref, inv_ref, mix_ref, dmix_ref, early_hbm,
    ig_ref, parts_hbm, small_ref, *rest, fast,
):
    if fast:
        sums_ref, tail_ref = rest[0:2]
        rest = rest[2:]
    band_ref, flipped_ref, grads_ref, wg_ref, diag_ref, staged_ref, ds_ref, sem, weight_sem = rest[:9]
    group, seq = pl.program_id(0), pl.program_id(1)
    seqs = pl.num_programs(1)
    step = group * seqs + seq
    width = x_ref.shape[1]
    if fast:
        extra = len(scatter_scratch(1, SHARE, width))
        scratch, tail_scratch = rest[9 : 9 + extra], rest[9 + extra :]
        here = place()

        def main(phase, piece):
            if phase > 0:
                scatter_phase(phase, piece, here, early_hbm.at[0], sums_ref, *scratch)
                return

            @pl.when(piece < BACK_BEFORE)
            def _():
                scatter_phase(phase, piece, here, early_hbm.at[FEED_SUMS + piece], sums_ref, *scratch)

            @pl.when(piece >= BACK_BEFORE)
            def _():
                scatter_phase(phase, piece, here, parts_hbm.at[piece - BACK_BEFORE], sums_ref, *scratch)

        def tail(phase, piece):
            if phase > 0:
                scatter_phase(phase, piece, here, small_ref, tail_ref, *tail_scratch)
                return
            scatter_phase(phase, GROUPS, here, small_ref, tail_ref, *tail_scratch)

        def tail_start(which):
            mine = slice(which * SMALL, (which + 1) * SMALL)
            scatter_phase(0, which, here, staged_ref.at[:, :, :, :, mine], tail_ref, *tail_scratch)

        def travel(slot):
            run_slot(slot, BACK_SCATTER, main)
            run_slot(slot, TAIL_SCATTER, tail)

        def point(at):
            travel(2 * step + at)
    else:
        point = lambda at: None
    keep = lambda: pltpu.make_async_copy(staged_ref, parts_hbm.at[group], sem)
    lanes = pl.ds(pl.multiple_of(seq * LENGTH, LENGTH), LENGTH)

    def hidden_terms():
        hidden = x_ref[...].astype(F32)
        scale = lax.rsqrt(jnp.mean(hidden * hidden, axis=1, keepdims=True) + EPS)
        return hidden, scale

    load_weights = lambda: pltpu.make_async_copy(weights_hbm.at[0:GROUPS], wg_ref, weight_sem)

    @pl.when(step == 0)
    def _():
        load_weights().start()

    if fast:

        @pl.when(step == 0)
        def _():
            greet(here)

        @pl.when(step == 1)
        def _():
            await_greetings()

    @pl.when(group == 0)
    def _():
        hidden, scale = hidden_terms()
        flipped_ref[:, lanes] = (hidden * scale * gains_ref[0:1, :]).astype(BF16).T

    @pl.when((seq == 0) & (group < GROUPS))
    def _():
        band_ref[...] = jnp.zeros_like(band_ref)

    def one_head(head):
        at = head * HEAD_DIM
        rows = lambda which: qkv_ref[0, 0, which * GROUP_ROWS + at : which * GROUP_ROWS + at + HEAD_DIM, :]
        grads = dmix_ref[0, 0, at : at + HEAD_DIM, :].astype(F32) * inv_ref[0, 0, head]
        grads = grads.astype(BF16)
        delta = jnp.sum(grads.astype(F32) * mix_ref[0, 0, at : at + HEAD_DIM, :].astype(F32), axis=0, keepdims=True)
        grad_prob = dot_tn(rows(2), grads)
        for column in range(BLOCKS):
            mine = span(column, column + 1)
            for row in range(BLOCKS):
                seen = span(row, row + 1)
                value = p_ref[0, 0, head, seen, mine].astype(F32) * (grad_prob[seen, mine] - delta[:, mine])
                band_ref[head, span(row - column + BLOCKS - 1, row - column + BLOCKS), :] += value
                ds_ref[head % 2, seen, mine] = value.astype(BF16)
        scores = ds_ref[head % 2]
        grads_ref[group, at : at + HEAD_DIM, lanes] = dot(rows(1), scores).astype(BF16)
        grads_ref[group, GROUP_ROWS + at : GROUP_ROWS + at + HEAD_DIM, lanes] = dot_nt(rows(0), scores).astype(BF16)
        grads_ref[group, 2 * GROUP_ROWS + at : 2 * GROUP_ROWS + at + HEAD_DIM, lanes] = dot_nt(grads, p_ref[0, 0, head]).astype(BF16)

    point(0)

    @pl.when(group < GROUPS)
    def _():
        one_head(0)
        one_head(1)

    @pl.when(group < GROUPS)
    def _():
        point(1)

    @pl.when(group < GROUPS)
    def _():
        one_head(2)
        one_head(3)

    @pl.when((seq == seqs - 1) & (group < GROUPS))
    def _():
        for first in range(0, width, 256):
            value = dot_nt(flipped_ref[...], grads_ref[group, first : first + 256, :]).astype(BF16)
            for owner in range(OWNERS):
                z, x, core = owner // 4, owner // 2 % 2, owner % 2
                staged_ref[z, x, core, :, first : first + 256] = value[SHARE * owner : SHARE * (owner + 1), :]
        last_fast = fast & (group == GROUPS - 1)

        @pl.when(jnp.logical_not(last_fast))
        def _():
            keep().start()

        if fast:

            @pl.when(last_fast)
            def _():
                for which in range(3):
                    tail_start(which)

        for head in range(GROUP):
            turned = band_ref[head].T
            total = jnp.zeros((8, OFFSETS), F32)
            for some in range(BLOCK // 8):
                wide = jnp.concatenate([turned[8 * some : 8 * some + 8, :], jnp.zeros((8, BLOCK), F32)], axis=1)
                total = total + pltpu.roll(wide, BLOCK - 8 * some, 1)
            line = iota((8, OFFSETS), 0)
            moved = total
            for row in range(1, 8):
                moved = jnp.where(line == row, pltpu.roll(total, OFFSETS - row, 1), moved)
            diag_ref[pl.ds(group * GROUP + head, 1)] = jnp.sum(moved, axis=0, keepdims=True)[None]
        @pl.when(jnp.logical_not(last_fast))
        def _():
            keep().wait()

    @pl.when((seq == seqs - 1) & (group == GROUPS - 1))
    def _():
        heads, buckets = table_places()
        onehot = (bucket_of(iota((OFFSETS, 1), 0) - BLOCKS * BLOCK) == buckets).astype(F32).astype(BF16)
        row = iota((16, width), 0)
        sums = jnp.concatenate([diag_ref[head] for head in range(HEADS)] + [jnp.zeros((16 - HEADS, OFFSETS), F32)], axis=0)
        high = sums.astype(BF16)
        low = (sums - high.astype(F32)).astype(BF16)
        entries = dot(high, onehot) + dot(low, onehot)
        entries = jnp.sum(jnp.where((row == heads) & (buckets >= 0), entries, 0.0), axis=0, keepdims=True)
        column = jnp.broadcast_to(entries, (BLOCK, width)).T.astype(BF16)
        for owner in range(OWNERS):
            z, x, core = owner // 4, owner // 2 % 2, owner % 2
            mine = column[SHARE * owner : SHARE * (owner + 1), :]
            small_ref[z, x, core, :, 0:BLOCK] = mine
            small_ref[z, x, core, :, BLOCK:SMALL] = mine

    @pl.when((group == GROUPS) & (seq == 0))
    def _():
        load_weights().wait()

    @pl.when(group == GROUPS)
    def _():
        hidden, scale = hidden_terms()
        flat = wg_ref[...].reshape(GROUPS, width, width)
        cotangent = sum(dot(flat[one], grads_ref[one, :, lanes]) for one in range(GROUPS)).T
        scaled = cotangent * gains_ref[0:1, :]
        unit = hidden * scale
        inner = jnp.mean(scaled * unit, axis=1, keepdims=True)
        ig_ref[...] = (gm_ref[...].astype(F32) + scale * (scaled - unit * inner)).astype(BF16)

    @pl.when(group == GROUPS)
    def _():
        point(1)

    if fast:

        @pl.when(step == (GROUPS + 1) * seqs - 1)
        def _():
            run_rest((2 * GROUPS + 2) * (flipped_ref.shape[1] // LENGTH), [BACK_SCATTER, TAIL_SCATTER], travel)


def back(x, gm, gains, weights, qkv, p, inv, mix, dmix, early, fast):
    tokens, width = x.shape
    seqs = tokens // LENGTH
    piece = (DEPTH, WIDE, CORES, SHARE, width)
    last = GROUPS - 1
    group_at = lambda g: jnp.minimum(g, last)
    seq_at = lambda g, s: jnp.where(g <= last, s, seqs - 1)
    four = lambda rows: pl.BlockSpec((1, 1, rows, LENGTH), lambda g, s: (group_at(g), seq_at(g, s), 0, 0))
    x_rows = pl.BlockSpec((LENGTH, width), lambda g, s: (jnp.where((g == 0) | (g == GROUPS), s, 0), 0))
    end_rows = pl.BlockSpec((LENGTH, width), lambda g, s: (jnp.where(g == GROUPS, s, 0), 0))
    out_specs = [end_rows, ANY, whole((DEPTH, WIDE, CORES, SHARE, SMALL))]
    out_shape = [
        jax.ShapeDtypeStruct((tokens, width), BF16), jax.ShapeDtypeStruct((GROUPS, *piece), BF16),
        jax.ShapeDtypeStruct((DEPTH, WIDE, CORES, SHARE, SMALL), BF16),
    ]
    scratch = [
        pltpu.VMEM((GROUP, BAND, BLOCK), F32), pltpu.VMEM((width, tokens), BF16), pltpu.VMEM((GROUPS, width, tokens), BF16),
        pltpu.VMEM((GROUPS, *piece), BF16), pltpu.VMEM((HEADS, 1, OFFSETS), F32), pltpu.VMEM(piece, BF16),
        pltpu.VMEM((2, LENGTH, LENGTH), BF16), pltpu.SemaphoreType.DMA,
        pltpu.SemaphoreType.DMA,
    ]
    kernel = partial(back_kernel, fast=fast)
    if fast:
        sums = BACK_SUMS
        out_specs += [whole((sums, SHARE, width)), whole((TAIL_SUMS, SHARE, SMALL))]
        out_shape += [jax.ShapeDtypeStruct((sums, SHARE, width), F32), jax.ShapeDtypeStruct((TAIL_SUMS, SHARE, SMALL), F32)]
        scratch += scatter_scratch(sums, SHARE, width) + scatter_scratch(TAIL_SUMS, SHARE, SMALL, TAIL_SUMS)
    return pl.pallas_call(
        kernel,
        name="back",
        grid=(GROUPS + 1, seqs),
        in_specs=[
            x_rows, end_rows, whole((8, width)),
            ANY, four(width),
            pl.BlockSpec((1, 1, GROUP, LENGTH, LENGTH), lambda g, s: (group_at(g), seq_at(g, s), 0, 0, 0)),
            pl.BlockSpec((1, 1, GROUP, 1, LENGTH), lambda g, s: (group_at(g), seq_at(g, s), 0, 0, 0)),
            four(GROUP_ROWS), four(GROUP_ROWS), ANY,
        ],
        out_specs=out_specs,
        out_shape=out_shape,
        scratch_shapes=scratch,
        compiler_params=pltpu.CompilerParams(
            vmem_limit_bytes=VMEM_LIMIT, collective_id=3 if fast else None, has_side_effects=fast
        ),
    )(x, gm, gains, weights, qkv, p, inv, mix, dmix, early)


def finish_kernel(
    out_ref, ig_ref, mean_ref, early_ref, late_ref, tail_ref, wq_ref, wk_ref, wv_ref, win_ref, gains_ref,
    output_ref, input_grad_ref, pooled_ref, gq_ref, gk_ref, gv_ref, go_ref, gin_ref, gout_ref, first_ref, second_ref, table_ref,
):
    output_ref[...] = out_ref[...]
    input_grad_ref[...] = ig_ref[...]
    pooled_ref[...] = mean_ref[...]
    step = pl.program_id(0)

    @pl.when(step == 0)
    def _():
        for which, target in enumerate((gq_ref, gk_ref, gv_ref)):
            mine = slice(which * GROUP_ROWS, (which + 1) * GROUP_ROWS)
            for group in range(GROUPS):
                value = tail_ref[which] if group == GROUPS - 1 else late_ref[BACK_BEFORE + group, :, mine]
                target[:, group * GROUP_ROWS : (group + 1) * GROUP_ROWS] = value
        go_ref[...] = late_ref[2 * PARTS - FEED_SUMS]

    @pl.when(step == 1)
    def _():
        for part in range(PARTS):
            piece = 2 * part + 1
            gout_ref[part * SHARE : (part + 1) * SHARE, :] = (
                early_ref[piece] if piece < FEED_SUMS else late_ref[piece - FEED_SUMS]
            )

    @pl.when(step == 2)
    def _():
        for part in range(PARTS):
            piece = 2 * part
            value = early_ref[piece] if piece < FEED_SUMS else late_ref[piece - FEED_SUMS]
            for owner in range(OWNERS):
                at = (owner * PARTS + part) * SHARE
                gin_ref[:, at : at + SHARE] = value[:, owner * SHARE : (owner + 1) * SHARE]

    @pl.when(step == pl.num_programs(0) - 1)
    def _():
        def weigh(weight_ref, grad_ref):
            return jnp.sum(weight_ref[...].astype(F32) * grad_ref[...], axis=1, keepdims=True)

        first = weigh(wq_ref, gq_ref) + weigh(wk_ref, gk_ref) + weigh(wv_ref, gv_ref)
        second = weigh(win_ref, gin_ref)
        column = iota((SHARE, BLOCK), 1)
        lines = jnp.where(column == 0, first, jnp.where(column == 1, second, tail_ref[GROUPS, :, 0:BLOCK])).T
        gains = lines[0:2, 0:SHARE] / gains_ref[0:2, 0:SHARE].astype(F32)
        first_ref[...] = gains[0:1, :]
        second_ref[...] = gains[1:2, :]
        table_ref[...] = lines[2:3, 0:TABLE_SHARE]


def finish(out, ig, mean, early, late, tail, wq, wk, wv, win, gains):
    tokens, width = out.shape
    ff = win.shape[1]
    rows = pl.BlockSpec((LENGTH, width), lambda s: (s, 0))
    means = pl.BlockSpec((1, 2, width), lambda s: (s, 0, 0))
    low = jax.ShapeDtypeStruct((tokens, width), BF16)
    square = whole((SHARE, width))
    table = lambda *shape: jax.ShapeDtypeStruct(shape, F32)
    return pl.pallas_call(
        finish_kernel,
        name="finish",
        grid=(tokens // LENGTH,),
        in_specs=[
            rows, rows, means, whole(early.shape), whole(late.shape), whole(tail.shape), square, square, square, whole((SHARE, ff)),
            whole(gains.shape),
        ],
        out_specs=[
            rows, rows, means, square, square, square, square, whole((SHARE, ff)), whole((ff // OWNERS, width)),
            whole((1, SHARE)), whole((1, SHARE)),
            whole((1, TABLE_SHARE)),
        ],
        out_shape=[
            low, low, table(*mean.shape), table(SHARE, width), table(SHARE, width), table(SHARE, width), table(SHARE, width), table(SHARE, ff),
            table(ff // OWNERS, width), table(1, SHARE), table(1, SHARE), table(1, TABLE_SHARE),
        ],
        compiler_params=pltpu.CompilerParams(vmem_limit_bytes=VMEM_LIMIT),
    )(out, ig, mean, early, late, tail, wq, wk, wv, win, gains)


def ordered(rows, w_query, w_key, w_value, w_output, w_in, w_out):
    width = w_query.shape[1]
    groups = [
        jnp.concatenate([one[:, at * GROUP_ROWS : (at + 1) * GROUP_ROWS] for one in (w_query, w_key, w_value)], axis=1)
        for at in range(GROUPS)
    ]
    inner = w_in.reshape(rows, OWNERS, PARTS, SHARE).transpose(2, 0, 1, 3).reshape(PARTS, rows, width)
    outer = w_out.reshape(-1, PARTS, SHARE, width).transpose(1, 0, 2, 3).reshape(PARTS, rows, width)
    parts = [one for at in range(PARTS) for one in (inner[at], outer[at])]
    return jnp.stack(groups + [w_output] + parts)


def small_of(gain_attn, gain_ffn, rel_table):
    lines = [one.reshape(-1, 1, share) for one, share in ((gain_attn, SHARE), (gain_ffn, SHARE), (rel_table, TABLE_SHARE))]
    padded = [jnp.pad(one, ((0, 0), (0, 0), (0, BLOCK - one.shape[2]))) for one in lines]
    return jnp.pad(jnp.concatenate(padded, axis=1), ((0, 0), (0, 13), (0, 0)))


def shards(
    hidden_in, out_grad, pooled_gradient, gain_attn, w_query, w_key, w_value, w_output, rel_table, gain_ffn, w_in, w_out,
    pair_flags, instruction_mask, *, fast,
):
    width = hidden_in.shape[1]
    own = (w_query, w_key, w_value, w_output, w_in, w_out)
    if fast:
        shares = arrange(*own)
        small = small_of(gain_attn, gain_ffn, rel_table)[0]
    else:
        gather = lambda one: lax.all_gather(one, "fsdp", axis=0, tiled=True)
        shares = ordered(width, *map(gather, own)).reshape(-1, DEPTH, WIDE, CORES, SHARE, width)
        small = small_of(*map(gather, (gain_attn, gain_ffn, rel_table)))
    flags = pair_flags.reshape(-1, 1, LENGTH)
    instr = instruction_mask.reshape(-1, 1, LENGTH)
    qkv, p, inv, mix, mid, n2, bg, gains, *rest = attend(
        hidden_in, out_grad, pooled_gradient, flags, instr, shares, small, fast
    )
    early = rest[0] if fast else shares
    output, pooled, gm, dmix, parts, *rest = feed(
        n2, bg, mid, flags, instr, gains, mix, early, shares, fast
    )
    early_sums = rest
    input_grad, group_parts, small_parts, *rest = back(hidden_in, gm, gains, early, qkv, p, inv, mix, dmix, parts, fast)
    if fast:
        *results, grad_in, grad_out, first, second, table = finish(
            output, input_grad, pooled, early_sums[0], *rest, w_query, w_key, w_value, w_in, small
        )
        output, pooled, input_grad = results[0], results[2], results[1]
        return (output, pooled, input_grad, first[0], *results[3:], table[0], second[0], grad_in, grad_out)
    sums = jnp.concatenate([parts, group_parts]).reshape(-1, width, width)
    table = small_parts.reshape(OWNERS, SHARE, SMALL)[:, :TABLE_SHARE, 0].reshape(-1)
    rows = width
    groups = [sums[2 * PARTS + 1 + at] for at in range(GROUPS)]
    grad_query, grad_key, grad_value = (
        jnp.concatenate([one[:, at * GROUP_ROWS : (at + 1) * GROUP_ROWS] for one in groups], axis=1) for at in range(3)
    )
    grad_output = sums[2 * PARTS]
    grad_in = sums[0 : 2 * PARTS : 2].reshape(PARTS, rows, OWNERS, SHARE).transpose(1, 2, 0, 3).reshape(rows, -1)
    grad_out = sums[1 : 2 * PARTS : 2].reshape(PARTS, -1, SHARE, width).transpose(1, 0, 2, 3).reshape(-1, width)
    scatter = lambda one: lax.psum(lax.psum_scatter(one, "fsdp", scatter_dimension=0, tiled=True), "grp").astype(F32)
    grad_query, grad_key, grad_value, grad_output, grad_in, grad_out, table = map(
        scatter, (grad_query, grad_key, grad_value, grad_output, grad_in, grad_out, table)
    )
    weigh = lambda weight, grad: jnp.sum(weight.astype(F32) * grad, axis=1)
    grad_gain = weigh(w_query, grad_query) + weigh(w_key, grad_key) + weigh(w_value, grad_value)
    return (
        output, pooled, input_grad, grad_gain / gain_attn.astype(F32),
        grad_query, grad_key, grad_value, grad_output, table.astype(F32),
        weigh(w_in, grad_in) / gain_ffn.astype(F32), grad_in, grad_out,
    )


def solution(mesh):
    tokens, square, line = P(("grp", "fsdp"), None), P("fsdp", None), P("fsdp")
    cube, flat = P(("grp", "fsdp"), None, None), P(("grp", "fsdp"))
    fast = mesh.shape["fsdp"] == OWNERS and mesh.shape["grp"] == 2
    return jax.shard_map(
        partial(shards, fast=fast),
        mesh=mesh,
        in_specs=(tokens, tokens, cube, line, square, square, square, square, line, line, square, square, flat, flat),
        out_specs=(tokens, cube, tokens, line, square, square, square, square, line, line, square, square),
        check_vma=False,
    )
```
